32 devices in a mesh: replica: 8 (over z, core), group: 4 (over y, x).
Axes of the slice: x: 2, y: 2, z: 4, core: 2. Of those that a mesh axis runs over, the one named last changes fastest.
Arguments:
- tokens: bfloat16 [256, 197, 768], P(('replica', 'group')), may hold values from -6 to 6
- cotangent: bfloat16 [256, 197, 768], P(('replica', 'group')), may hold values from -6 to 6
- w_qkv: float32 [768, 2304], P('group'), may hold values from -0.21875 to 0.21875
- m_qkv: float32 [768, 2304], P('group'), may hold values from -160 to 160
- v_qkv: float32 [768, 2304], P('group'), may hold values from 50.432 to 201.728
- w_out: float32 [768, 768], P('group'), may hold values from -0.875 to 0.875
- m_out: float32 [768, 768], P('group'), may hold values from -160 to 160
- v_out: float32 [768, 768], P('group'), may hold values from 50.432 to 201.728
- w_up: float32 [768, 3072], P('group'), may hold values from -0.21875 to 0.21875
- m_up: float32 [768, 3072], P('group'), may hold values from -160 to 160
- v_up: float32 [768, 3072], P('group'), may hold values from 50.432 to 201.728
- w_down: float32 [3072, 768], P('group'), may hold values from -0.109375 to 0.109375
- m_down: float32 [3072, 768], P('group'), may hold values from -160 to 160
- v_down: float32 [3072, 768], P('group'), may hold values from 50.432 to 201.728
- vectors: float32 [12, 768], P(None, 'group'), may hold values from -1.2 to 1.2, as said below
- m_vectors: float32 [12, 768], P(None, 'group'), may hold values from -160 to 160
- v_vectors: float32 [12, 768], P(None, 'group'), may hold values from 50.432 to 201.728
Outputs:
- output: bfloat16 [256, 197, 768], P(('replica', 'group'))
- input_grad: bfloat16 [256, 197, 768], P(('replica', 'group'))
- grad_qkv: float32 [768, 2304], P('group')
- first_qkv: float32 [768, 2304], P('group')
- second_qkv: float32 [768, 2304], P('group')
- new_qkv: float32 [768, 2304], P('group')
- grad_out: float32 [768, 768], P('group')
- first_out: float32 [768, 768], P('group')
- second_out: float32 [768, 768], P('group')
- new_out: float32 [768, 768], P('group')
- grad_up: float32 [768, 3072], P('group')
- first_up: float32 [768, 3072], P('group')
- second_up: float32 [768, 3072], P('group')
- new_up: float32 [768, 3072], P('group')
- grad_down: float32 [3072, 768], P('group')
- first_down: float32 [3072, 768], P('group')
- second_down: float32 [3072, 768], P('group')
- new_down: float32 [3072, 768], P('group')
- grad_vectors: float32 [12, 768], P(None, 'group')
- first_vectors: float32 [12, 768], P(None, 'group')
- second_vectors: float32 [12, 768], P(None, 'group')
- new_vectors: float32 [12, 768], P(None, 'group')
The draws below stay inside these ranges and needn't reach their ends.
Inputs may be any that keep to these rules, and one draw needn't show every extreme that they name: `vectors`: the two norm gain rows lie in 0.85 to 1.15.
All inputs are finite; a program needn't handle non-finite values.
Results may differ from the reference program's by a relative error of at most 0.025.
Values may be sent and summed in bfloat16 or wider, within the bound.
A program may use at most 384 MiB of HBM per device.

```python
import math
import jax
import jax.numpy as jnp
from jax import lax

D = 768
HEADS = 12
HEAD_DIM = 64
FF = 3072
SEQ = 197
IMG_DEV = 8
STEP = 10
IMAGES = 256


def draw_vectors(key, part):
    key = jax.random.fold_in(key, 7)
    key_base = jax.random.fold_in(key, 1)
    key_gain = jax.random.fold_in(key, 2)
    base = jnp.clip(0.3 * jax.random.normal(key_base, (12, D), jnp.float32), -1.2, 1.2)
    gains = 1.0 + jax.random.uniform(key_gain, (12, D), jnp.float32, -0.15, 0.15)
    row_index = jnp.arange(12)[:, None]
    is_gain = (row_index == 4) | (row_index == 6)
    return jnp.where(is_gain, gains, base)


def shard_levels(own_key, extent, pieces, least, high):
    loudness = 1.0
    for position, parts in pieces:
        steps = jax.random.uniform(jax.random.fold_in(jax.random.fold_in(own_key, 6), position), (parts,), jnp.float32, least / len(pieces), high / len(pieces))
        loudness = loudness * jnp.repeat(jnp.exp(steps), extent[position] // parts).reshape((-1,) + (1,) * (len(extent) - 1 - position))
    return loudness


def bell_draw(rng, shape, spread, limit, shards=(), held_as=jnp.bfloat16):
    values = jax.random.normal(rng, shape, jnp.float32) * spread
    if len(shards) > 0:
        values = shard_levels(rng, shape, shards, -0.22, 0.18) * values
    return jnp.clip(values, min=-limit, max=limit).astype(held_as)


def setup_inputs(seed: int = 0) -> dict:
    arg_keys = jax.random.split(jax.random.key(seed), 18)
    return {
        "tokens": bell_draw(arg_keys[0], (IMAGES, SEQ, D), 1.0, 6.0, ((0, 32),)),
        "cotangent": bell_draw(arg_keys[1], (IMAGES, SEQ, D), 1.0, 6.0, ((0, 32),)),
        "w_qkv": bell_draw(arg_keys[2], (D, 3 * D), D ** -0.5, 0.21875, ((0, 4),), jnp.float32),
        "m_qkv": bell_draw(arg_keys[3], (D, 3 * D), (0.11 * (IMAGES * SEQ) ** 0.5), 160.0, ((0, 4),), jnp.float32),
        "v_qkv": jnp.clip(jnp.exp(math.log(201.728) - 1.3862944 * jax.random.uniform(arg_keys[4], (D, 3 * D), jnp.float32) ** shard_levels(arg_keys[4], (D, 3 * D), ((0, 4),), -0.2, 0.2)), 50.432, 201.728),
        "w_out": bell_draw(arg_keys[5], (D, D), (D // 16) ** -0.5, 0.875, ((0, 4),), jnp.float32),
        "m_out": bell_draw(arg_keys[6], (D, D), (0.11 * (IMAGES * SEQ) ** 0.5), 160.0, ((0, 4),), jnp.float32),
        "v_out": jnp.clip(jnp.exp(math.log(201.728) - 1.3862944 * jax.random.uniform(arg_keys[7], (D, D), jnp.float32) ** shard_levels(arg_keys[7], (D, D), ((0, 4),), -0.2, 0.2)), 50.432, 201.728),
        "w_up": bell_draw(arg_keys[8], (D, FF), D ** -0.5, 0.21875, ((0, 4),), jnp.float32),
        "m_up": bell_draw(arg_keys[9], (D, FF), (0.11 * (IMAGES * SEQ) ** 0.5), 160.0, ((0, 4),), jnp.float32),
        "v_up": jnp.clip(jnp.exp(math.log(201.728) - 1.3862944 * jax.random.uniform(arg_keys[10], (D, FF), jnp.float32) ** shard_levels(arg_keys[10], (D, FF), ((0, 4),), -0.2, 0.2)), 50.432, 201.728),
        "w_down": bell_draw(arg_keys[11], (FF, D), FF ** -0.5, 0.109375, ((0, 4),), jnp.float32),
        "m_down": bell_draw(arg_keys[12], (FF, D), (0.11 * (IMAGES * SEQ) ** 0.5), 160.0, ((0, 4),), jnp.float32),
        "v_down": jnp.clip(jnp.exp(math.log(201.728) - 1.3862944 * jax.random.uniform(arg_keys[13], (FF, D), jnp.float32) ** shard_levels(arg_keys[13], (FF, D), ((0, 4),), -0.2, 0.2)), 50.432, 201.728),
        "vectors": draw_vectors(jax.random.fold_in(arg_keys[17], 71), 0),
        "m_vectors": bell_draw(arg_keys[15], (12, D), (0.11 * (IMAGES * SEQ) ** 0.5), 160.0, ((1, 4),), jnp.float32),
        "v_vectors": jnp.clip(jnp.exp(math.log(201.728) - 1.3862944 * jax.random.uniform(arg_keys[16], (12, D), jnp.float32) ** shard_levels(arg_keys[16], (12, D), ((1, 4),), -0.2, 0.2)), 50.432, 201.728),
    }


highest = lax.Precision.HIGHEST
norm_eps = 1e-06
beta_one = 0.9
beta_two = 0.999
adam_eps = 1e-08

@jax.custom_vjp
def low(v):
    return lax.optimization_barrier(v.astype(jnp.bfloat16)).astype(jnp.float32)

@jax.custom_vjp
def low_back(v):
    return v

def low_keep(v):
    return (low(v), None)

def low_pass(kept, grad):
    return (grad,)

def back_keep(v):
    return (v, None)

def back_low(kept, grad):
    return (low(grad),)
low.defvjp(low_keep, low_pass)
low_back.defvjp(back_keep, back_low)

def layer_norm(hidden, gain_vec, shift_vec):
    row_mean = lax.optimization_barrier(jnp.mean(hidden, -1, keepdims=True))
    centered = hidden - row_mean
    row_var = lax.optimization_barrier(jnp.mean(centered * centered, -1, keepdims=True))
    return centered * lax.rsqrt(row_var + norm_eps) * gain_vec + shift_vec

def forward(params, inputs):
    qkv_low, out_low, up_low, down_low, vec_low = [low(item) for item in params]
    images = inputs.shape[0]
    length = inputs.shape[1]
    width = inputs.shape[2]
    bias_up = vec_low[8:12].reshape(-1)
    normed_one = low(layer_norm(inputs, vec_low[4], vec_low[5]))
    bias_qkv = jnp.concatenate([vec_low[0], jnp.zeros_like(vec_low[0]), vec_low[1]])
    projected = jnp.einsum('isd,de->ise', normed_one, qkv_low, precision=highest) + bias_qkv
    projected = low(low_back(projected)).reshape(images, length, 3, HEADS, HEAD_DIM)
    query_rows = projected[:, :, 0]
    key_rows = projected[:, :, 1]
    value_rows = projected[:, :, 2]
    scores = jnp.einsum('ishd,ithd->ihst', query_rows, key_rows, precision=highest) * HEAD_DIM ** (-0.5)
    scores = low_back(scores)
    attn_probs = low(jax.nn.softmax(scores, axis=-1))
    attended = jnp.einsum('ihst,ithd->ishd', attn_probs, value_rows, precision=highest)
    attended = low(low_back(attended.reshape(images, length, width)))
    branch = low_back(jnp.einsum('isd,de->ise', attended, out_low, precision=highest) + vec_low[2])
    middle = inputs + branch
    normed_two = low(layer_norm(middle, vec_low[6], vec_low[7]))
    up_proj = low_back(jnp.einsum('isd,df->isf', normed_two, up_low, precision=highest) + bias_up)
    activated = low(jax.nn.gelu(up_proj, approximate=False))
    down_proj = low_back(jnp.einsum('isf,fd->isd', activated, down_low, precision=highest) + vec_low[3])
    return middle + down_proj

def adamw_update(weight, first_moment, second, gradient, step_rate, decay_coef):
    first_new = beta_one * first_moment + (1.0 - beta_one) * gradient
    second_new = beta_two * second + (1.0 - beta_two) * gradient * gradient
    fix_one = 1.0 - beta_one ** STEP
    fix_two = 1.0 - beta_two ** STEP
    weight_new = weight - step_rate * (first_new / fix_one / (jnp.sqrt(second_new / fix_two) + adam_eps) + decay_coef * weight)
    return (first_new, second_new, weight_new)

def reference(tokens, cotangent, w_qkv, m_qkv, v_qkv, w_out, m_out, v_out, w_up, m_up, v_up, w_down, m_down, v_down, vectors, m_vectors, v_vectors):
    params = (w_qkv, w_out, w_up, w_down, vectors)
    in_blocks = tokens.astype(jnp.float32).reshape(IMAGES // IMG_DEV, IMG_DEV, SEQ, D)
    cot_blocks = cotangent.astype(jnp.float32).reshape(IMAGES // IMG_DEV, IMG_DEV, SEQ, D)

    def one_block(totals, block_pair):
        in_block, cot_block = block_pair
        result, pullback = jax.vjp(forward, params, in_block)
        gradients, in_grad = pullback(cot_block)
        totals = tuple((left + right for left, right in zip(totals, gradients)))
        return (totals, (result.astype(jnp.bfloat16), in_grad.astype(jnp.bfloat16)))
    zeros_init = tuple((jnp.zeros_like(item) for item in params))
    totals, (results, in_grads) = lax.scan(one_block, zeros_init, (in_blocks, cot_blocks))
    output = results.reshape(IMAGES, SEQ, D)
    input_grad = in_grads.reshape(IMAGES, SEQ, D)
    states = ((w_qkv, m_qkv, v_qkv, 0.1, 0.05), (w_out, m_out, v_out, 0.1, 0.05), (w_up, m_up, v_up, 0.1, 0.05), (w_down, m_down, v_down, 0.1, 0.05), (vectors, m_vectors, v_vectors, 0.8, 0.0))
    outcome = [output, input_grad]
    for index in range(5):
        weight, first_moment, second, step_rate, decay_coef = states[index]
        first_new, second_new, weight_new = adamw_update(weight, first_moment, second, totals[index], step_rate, decay_coef)
        outcome.extend([totals[index], first_new, second_new, weight_new])
    return tuple(outcome)
```

```python
import functools

import jax
import jax.numpy as jnp
from jax import lax
from jax.experimental import pallas as pl
from jax.experimental.pallas import tpu as pltpu
from jax.sharding import PartitionSpec as P

F32 = jnp.float32
BF = jnp.bfloat16
HEADS = 12
HEAD_DIM = 64
STEP = 10
MIB = 2**20
MESH = pl.DeviceIdType.MESH

norm_eps = 1e-06
beta_one = 0.9
beta_two = 0.999
adam_eps = 1e-08


def dot(a, b):
    return jnp.dot(a, b, preferred_element_type=F32)


def dot_t(a, b):
    return lax.dot_general(a, b, (((1,), (1,)), ((), ())), preferred_element_type=F32)


def flip(index, mask):
    out, bit = index, 1
    while bit <= mask:
        if mask & bit:
            out = out + bit * (1 - 2 * lax.rem(lax.div(index, bit), 2))
        bit *= 2
    return out


def rows_at(start, size):
    return pl.ds(pl.multiple_of(start, 16), size)


def normalize(hidden):
    centered = hidden - jnp.mean(hidden, -1, keepdims=True)
    rstd = lax.rsqrt(jnp.mean(centered * centered, -1, keepdims=True) + norm_eps)
    return centered * rstd, rstd


def norm_back(grad, normed, rstd, gain):
    e = grad * gain
    mean_e = jnp.mean(e, -1, keepdims=True)
    mean_en = jnp.mean(e * normed, -1, keepdims=True)
    return (e - mean_e - normed * mean_en) * rstd


def gelu_parts(u):
    x = jnp.abs(u) * 0.7071067811865476
    t = 1.0 / (1.0 + 0.3275911 * x)
    e = jnp.exp(-x * x)
    poly = (
        (((1.061405429 * t - 1.453152027) * t + 1.421413741) * t - 0.284496736) * t + 0.254829592
    ) * t
    q = 0.5 * poly * e
    phi = jnp.where(u > 0, 1.0 - q, q)
    return u * phi, phi + u * (e * 0.3989422804014327)


def pad_images(x_ref, scratch):
    n, length, width = x_ref.shape
    full = scratch.shape[1]
    for i in range(n):
        scratch[i, 0:length, :] = x_ref[i].astype(F32)
        scratch[i, length:full, :] = jnp.zeros((full - length, width), F32)
    return scratch[...].reshape(n * full, width)


def whole_block(shape):
    return pl.BlockSpec(shape, lambda *_: (0,) * len(shape), pipeline_mode=pl.Buffered(1))


def params(mib=58, **kw):
    return pltpu.CompilerParams(vmem_limit_bytes=mib * MIB, **kw)


def gather_attend(
    ng, x_hbm, wq_hbm, wo_hbm, wu_hbm, wd_hbm, vec_hbm,
    wq_out, wo_out, wu_out, wd_out, vec_out, a1_out, qkv_out, o_out,
    x_s, fq, fo, fu, fd, vec_s, bq, bo, bu, bd, vall, xpad, a1_s, qkv_s, o_s,
    in_sem, ag_send, ag_recv, fw_send, fw_recv, v_send, v_recv, out_sem,
):
    r, g = lax.axis_index("replica"), lax.axis_index("group")
    c = lax.rem(r, 2)
    sib = flip(r, 1)
    images, length, width = x_s.shape
    full = a1_s.shape[1]
    stages = [(wq_hbm, fq, bq, wq_out), (wo_hbm, fo, bo, wo_out), (wu_hbm, fu, bu, wu_out), (wd_hbm, fd, bd, wd_out)]
    loads = [pltpu.make_async_copy(src, dst, in_sem.at[i]) for i, (src, dst, _, _) in enumerate(stages)]
    vec_load = pltpu.make_async_copy(vec_hbm, vec_s, in_sem.at[4])
    x_load = pltpu.make_async_copy(x_hbm, x_s, in_sem.at[5])
    vec_load.start()
    loads[0].start()
    x_load.start()
    for load in loads[1:]:
        load.start()

    barrier = pltpu.get_barrier_semaphore()
    for k in range(1, ng):
        pl.semaphore_signal(barrier, inc=1, device_id={"replica": r, "group": flip(g, k)}, device_id_type=MESH)
    pl.semaphore_signal(barrier, inc=1, device_id={"replica": sib, "group": g}, device_id_type=MESH)
    pl.semaphore_wait(barrier, ng)

    vec_load.wait()
    vall[g] = vec_s[...].astype(BF).astype(F32)
    v_copies = [
        pltpu.make_async_remote_copy(
            vall.at[g], vall.at[g], v_send.at[k - 1], v_recv.at[k - 1],
            device_id={"replica": r, "group": flip(g, k)}, device_id_type=MESH)
        for k in range(1, ng)
    ]
    for copy in v_copies:
        copy.start()

    def own(i):
        loads[i].wait()
        shard = stages[i][1].shape[0]
        stages[i][2][rows_at(g * shard, shard), :] = stages[i][1][...].astype(BF)

    def sends(i):
        buf, half = stages[i][2], stages[i][1].shape[0] // 2
        part = buf.at[rows_at(g * 2 * half + c * half, half), :]
        return [
            pltpu.make_async_remote_copy(
                part, part, ag_send.at[i, k - 1], ag_recv.at[i, k - 1],
                device_id={"replica": r, "group": flip(g, k)}, device_id_type=MESH)
            for k in range(1, ng)
        ]

    def forwards(i):
        buf, half = stages[i][2], stages[i][1].shape[0] // 2
        out = []
        for k in range(1, ng):
            part = buf.at[rows_at(flip(g, k) * 2 * half + c * half, half), :]
            out.append(
                pltpu.make_async_remote_copy(
                    part, part, fw_send.at[i, k - 1], fw_recv.at[i, k - 1],
                    device_id={"replica": sib, "group": g}, device_id_type=MESH)
            )
        return out

    def pass_on(i):
        copies, onward = sends(i), forwards(i)
        for k in range(ng - 1):
            copies[k].wait_recv()
            onward[k].start()

    def finish(i):
        for copy in forwards(i):
            copy.wait_recv()
        for copy in forwards(i) + sends(i):
            copy.wait_send()
        pltpu.make_async_copy(stages[i][2], stages[i][3], out_sem.at[i]).start()

    own(0)
    for copy in sends(0):
        copy.start()
    for i in range(1, 4):
        own(i)

    for copy in v_copies:
        copy.wait()
    w = vall.shape[2]
    vecs = jnp.zeros((vall.shape[1], width), F32)
    for j in range(ng):
        row = lax.broadcasted_iota(jnp.int32, (w, width), 0)
        col = lax.broadcasted_iota(jnp.int32, (w, width), 1)
        place = jnp.where(col == row + j * w, 1.0, 0.0).astype(BF)
        vecs = vecs + dot(vall[j].astype(BF), place)
    vec_out[...] = vecs

    x_load.wait()

    def norm_image(i, _):
        xpad[0:length, :] = x_s[i].astype(F32)
        xpad[length:full, :] = jnp.zeros((full - length, width), F32)
        normed, _r = normalize(xpad[...])
        a1_s[i] = (normed * vec_out[4:5, :] + vec_out[5:6, :]).astype(BF)
        return 0

    lax.fori_loop(0, images, norm_image, 0)
    a1_copy = pltpu.make_async_copy(a1_s, a1_out, out_sem.at[4])
    a1_copy.start()

    pass_on(0)
    for i in range(1, 4):
        for copy in sends(i):
            copy.start()
    finish(0)

    zero = jnp.zeros((1, width), F32)
    biases = [vec_out[0:1, :], zero, vec_out[1:2, :]]
    block = images // 2

    def project(i, _):
        a1 = a1_s[pl.ds(i * block, block)].reshape(block * full, width)
        for n in range(3):
            cols = slice(n * width, (n + 1) * width)
            out = (dot(a1, bq[:, cols]) + biases[n]).astype(BF)
            qkv_s[pl.ds(i * block, block), :, cols] = out.reshape(block, full, width)
        return 0

    lax.fori_loop(0, 2, project, 0)
    qkv_copy = pltpu.make_async_copy(qkv_s, qkv_out, out_sem.at[5])
    qkv_copy.start()
    pass_on(1)

    low_half = lax.broadcasted_iota(jnp.int32, (full, 128), 1) < HEAD_DIM
    key_bias = jnp.where(lax.broadcasted_iota(jnp.int32, (1, full), 1) < length, 0.0, -1e30).astype(F32)
    ones = jnp.ones((full, 128), BF)

    def attend(i, _):
        for p in range(HEADS // 2):
            at = p * 128
            q = qkv_s[i, :, at : at + 128] * jnp.asarray(HEAD_DIM**-0.5, BF)
            k = qkv_s[i, :, at + width : at + width + 128]
            v = jnp.concatenate([qkv_s[i, :, at + 2 * width : at + 2 * width + 128], ones], axis=1)
            heads = []
            for h in range(2):
                mine = low_half if h == 0 else ~low_half
                s = dot_t(jnp.where(mine, q, jnp.zeros_like(q)), k) + key_bias
                e = jnp.exp(s - jnp.max(s, -1, keepdims=True)).astype(BF)
                both = dot(e, v)
                heads.append(both[:, :128] / both[:, 128:])
            o_s[i, :, at : at + 128] = jnp.where(low_half, heads[0], heads[1]).astype(BF)
        return 0

    lax.fori_loop(0, images, attend, 0)
    o_copy = pltpu.make_async_copy(o_s, o_out, out_sem.at[6])
    o_copy.start()
    finish(1)
    pass_on(2)
    pass_on(3)
    finish(2)
    finish(3)
    for i in range(4):
        pltpu.make_async_copy(stages[i][2], stages[i][3], out_sem.at[i]).wait()
    a1_copy.wait()
    qkv_copy.wait()
    o_copy.wait()


def run_gather_attend(ng, full, tokens, w_qkv, w_out, w_up, w_down, vectors):
    images, length, width = tokens.shape
    weights = (w_qkv, w_out, w_up, w_down)
    rows_all = [(ng * w.shape[0], w.shape[1]) for w in weights]
    any_spec = pl.BlockSpec(memory_space=pl.ANY)
    dma = pltpu.SemaphoreType.DMA
    return pl.pallas_call(
        functools.partial(gather_attend, ng),
        out_shape=tuple(jax.ShapeDtypeStruct(s, BF) for s in rows_all)
        + (
            jax.ShapeDtypeStruct((vectors.shape[0], width), F32),
            jax.ShapeDtypeStruct((images, full, width), BF),
            jax.ShapeDtypeStruct((images, full, 3 * width), BF),
            jax.ShapeDtypeStruct((images, full, width), BF),
        ),
        in_specs=[any_spec] * 6,
        out_specs=(any_spec,) * 4 + (pl.BlockSpec(memory_space=pltpu.VMEM),) + (any_spec,) * 3,
        scratch_shapes=[pltpu.VMEM(tokens.shape, BF)]
        + [pltpu.VMEM(w.shape, F32) for w in weights]
        + [pltpu.VMEM(vectors.shape, F32)]
        + [pltpu.VMEM(s, BF) for s in rows_all]
        + [
            pltpu.VMEM((ng,) + vectors.shape, F32),
            pltpu.VMEM((full, width), F32),
            pltpu.VMEM((images, full, width), BF),
            pltpu.VMEM((images, full, 3 * width), BF),
            pltpu.VMEM((images, full, width), BF),
            dma((6,)),
            dma((4, ng - 1)),
            dma((4, ng - 1)),
            dma((4, ng - 1)),
            dma((4, ng - 1)),
            dma((ng - 1,)),
            dma((ng - 1,)),
            dma((7,)),
        ],
        compiler_params=params(collective_id=0, has_side_effects=True),
    )(tokens, w_qkv, w_out, w_up, w_down, vectors)


def mid_block(x_ref, o_ref, cot_ref, wo_ref, vec_ref, h_ref, a2_ref, dm_ref, xpad):
    n, full, width = o_ref.shape
    x = pad_images(x_ref, xpad)
    h = x + dot(o_ref[...].reshape(n * full, width), wo_ref[...]) + vec_ref[2:3, :]
    normed, _r = normalize(h)
    h_ref[...] = h.reshape(n, full, width)
    a2_ref[...] = (normed * vec_ref[6:7, :] + vec_ref[7:8, :]).astype(BF).reshape(n, full, width)
    dm_ref[...] = pad_images(cot_ref, xpad).astype(BF).reshape(n, full, width)


def run_mid(tokens, attended, cotangent, wo, vecs):
    images, length, width = tokens.shape
    full = attended.shape[1]
    n = images // 2
    short = pl.BlockSpec((n, length, width), lambda i: (i, 0, 0))
    long = pl.BlockSpec((n, full, width), lambda i: (i, 0, 0))
    shape = (images, full, width)
    return pl.pallas_call(
        mid_block,
        grid=(2,),
        out_shape=(jax.ShapeDtypeStruct(shape, F32), jax.ShapeDtypeStruct(shape, BF), jax.ShapeDtypeStruct(shape, BF)),
        in_specs=[short, long, short, whole_block(wo.shape), whole_block(vecs.shape)],
        out_specs=(long, long, long),
        scratch_shapes=[pltpu.VMEM((n, full, width), F32)],
        compiler_params=params(),
    )(tokens, attended, cotangent, wo, vecs)


def mlp_block(rb, a2_ref, dm_ref, wu_ref, wd_ref, bu_ref, out_ref, da_ref, gwd_ref, gwu_ref, gbu_ref, a2t, act_s, du_s, sums):
    rows, width = a2_ref.shape
    ft = wu_ref.shape[1]

    @pl.when(pl.program_id(0) == 0)
    def _():
        out_ref[...] = jnp.zeros_like(out_ref)
        da_ref[...] = jnp.zeros_like(da_ref)
        a2t[...] = a2_ref[...].T

    sums[...] = jnp.zeros_like(sums)

    def body(i, _):
        sl = rows_at(i * rb, rb)
        u = dot(a2_ref[sl, :], wu_ref[...]) + bu_ref[...]
        da = dot_t(dm_ref[sl, :], wd_ref[...])
        act, slope = gelu_parts(u)
        act = act.astype(BF)
        du = (da * slope).astype(BF)
        act_s[sl, :] = act
        du_s[sl, :] = du
        sums[...] += jnp.sum(du.astype(F32).reshape(rb // 8, 8, ft), 0)
        out_ref[sl, :] += dot(act, wd_ref[...])
        da_ref[sl, :] += dot_t(du, wu_ref[...])
        return 0

    lax.fori_loop(0, rows // rb, body, 0)
    gwd_ref[...] = dot(act_s[...].T, dm_ref[...]).astype(BF)
    gwu_ref[...] = dot(a2t[...], du_s[...]).astype(BF)
    gbu_ref[...] = jnp.sum(sums[...], 0, keepdims=True)


def run_mlp(a2, dm, wu, wd, bu, ft=768):
    rows, width = a2.shape
    ff = wu.shape[1]
    acc = jax.ShapeDtypeStruct((rows, width), F32)
    return pl.pallas_call(
        functools.partial(mlp_block, rows // 2),
        grid=(ff // ft,),
        out_shape=(acc, acc, jax.ShapeDtypeStruct((ff, width), BF), jax.ShapeDtypeStruct((width, ff), BF), jax.ShapeDtypeStruct((1, ff), F32)),
        in_specs=[
            whole_block((rows, width)),
            whole_block((rows, width)),
            pl.BlockSpec((width, ft), lambda f: (0, f)),
            pl.BlockSpec((ft, width), lambda f: (f, 0)),
            pl.BlockSpec((1, ft), lambda f: (0, f)),
        ],
        out_specs=(
            whole_block((rows, width)),
            whole_block((rows, width)),
            pl.BlockSpec((ft, width), lambda f: (f, 0)),
            pl.BlockSpec((width, ft), lambda f: (0, f)),
            pl.BlockSpec((1, ft), lambda f: (0, f)),
        ),
        scratch_shapes=[
            pltpu.VMEM((width, rows), BF),
            pltpu.VMEM((rows, ft), BF),
            pltpu.VMEM((rows, ft), BF),
            pltpu.VMEM((8, ft), F32),
        ],
        compiler_params=params(),
    )(a2, dm, wu, wd, bu)


def post_block(h_ref, acc_ref, da_ref, cot_ref, o_ref, wo_ref, vec_ref, out_ref, dh_ref, do_ref, gwo_ref, sum_ref, cpad, gacc):
    n, full, width = o_ref.shape
    length = cot_ref.shape[1]
    rows = n * full
    step = pl.program_id(0)

    @pl.when(step == 0)
    def _():
        gacc[...] = jnp.zeros_like(gacc)
        sum_ref[...] = jnp.zeros_like(sum_ref)

    h = h_ref[...].reshape(rows, width)
    result = (h + acc_ref[...].reshape(rows, width) + vec_ref[3:4, :]).astype(BF).reshape(n, full, width)
    for i in range(n):
        out_ref[i] = result[i, :length, :]
    cot = pad_images(cot_ref, cpad)
    normed, rstd = normalize(h)
    da = da_ref[...].reshape(rows, width)
    dh = cot + norm_back(da, normed, rstd, vec_ref[6:7, :])
    dh_ref[...] = dh.reshape(n, full, width)
    dz = dh.astype(BF)
    do_ref[...] = dot_t(dz, wo_ref[...]).astype(BF).reshape(n, full, width)
    gacc[...] += dot(o_ref[...].reshape(rows, width).T, dz)
    for j, term in enumerate((dz.astype(F32), cot, da * normed, da)):
        sum_ref[j : j + 1, :] += jnp.sum(term, 0, keepdims=True)

    @pl.when(step == pl.num_programs(0) - 1)
    def _():
        gwo_ref[...] = gacc[...].astype(BF)


def run_post(h, acc, da, cotangent, attended, wo, vecs):
    images, full, width = attended.shape
    length = cotangent.shape[1]
    n = images // 2
    short = pl.BlockSpec((n, length, width), lambda i: (i, 0, 0))
    long = pl.BlockSpec((n, full, width), lambda i: (i, 0, 0))
    shape = (images, full, width)
    return pl.pallas_call(
        post_block,
        grid=(2,),
        out_shape=(
            jax.ShapeDtypeStruct(cotangent.shape, BF),
            jax.ShapeDtypeStruct(shape, F32),
            jax.ShapeDtypeStruct(shape, BF),
            jax.ShapeDtypeStruct((width, width), BF),
            jax.ShapeDtypeStruct((8, width), F32),
        ),
        in_specs=[long, long, long, short, long, whole_block(wo.shape), whole_block(vecs.shape)],
        out_specs=(short, long, long, whole_block((width, width)), whole_block((8, width))),
        scratch_shapes=[pltpu.VMEM((n, full, width), F32), pltpu.VMEM((width, width), F32)],
        compiler_params=params(),
    )(h, acc.reshape(shape), da.reshape(shape), cotangent, attended, wo, vecs)


def attend_back(length, qkv_ref, do_ref, o_ref, dp_ref):
    full, width = do_ref.shape[1], do_ref.shape[2]
    scale = HEAD_DIM**-0.5
    cut = length // 16 * 16
    low_half = lax.broadcasted_iota(jnp.int32, (full, 128), 1) < HEAD_DIM
    pick = lax.broadcasted_iota(jnp.int32, (16, width), 1) // HEAD_DIM == lax.broadcasted_iota(jnp.int32, (16, width), 0)
    pick = jnp.where(pick, 1.0, 0.0).astype(BF)
    live = lax.broadcasted_iota(jnp.int32, (full - cut, full), 0) < length - cut
    prod = do_ref[0].astype(F32) * o_ref[0].astype(F32)
    high = prod.astype(BF)
    inner = dot_t(pick, high) + dot_t(pick, (prod - high.astype(F32)).astype(BF))
    for p in range(HEADS // 2):
        at = p * 128
        q = qkv_ref[0, :, at : at + 128] * jnp.asarray(scale, BF)
        k = qkv_ref[0, :, at + width : at + width + 128]
        v = qkv_ref[0, :, at + 2 * width : at + 2 * width + 128]
        do = do_ref[0, :, at : at + 128]
        kt = k.T
        dq, dk, dv = [], None, None
        for h in range(2):
            mine = low_half if h == 0 else ~low_half
            qm = jnp.where(mine, q, jnp.zeros_like(q))
            dom = jnp.where(mine, do, jnp.zeros_like(do))
            s = dot_t(k, qm)
            s = jnp.concatenate([s[:cut], jnp.where(live, s[cut:], -1e30)], 0)
            e = jnp.exp(s - jnp.max(s, 0, keepdims=True))
            probs = e * (1.0 / jnp.sum(e, 0, keepdims=True))
            ds = (probs * (dot_t(v, dom) - inner[2 * p + h : 2 * p + h + 1, :])).astype(BF)
            dv_h, dk_h = dot(probs.astype(BF), dom), dot(ds, qm)
            dv = dv_h if dv is None else dv + dv_h
            dk = dk_h if dk is None else dk + dk_h
            dq.append(dot(kt[HEAD_DIM * h : HEAD_DIM * (h + 1), :], ds))
        dq = (jnp.concatenate(dq, 0) * scale).astype(BF).T
        dp_ref[0, :, at : at + 128] = dq
        dp_ref[0, :, at + width : at + width + 128] = dk.astype(BF)
        dp_ref[0, :, at + 2 * width : at + 2 * width + 128] = dv.astype(BF)


def run_attend_back(length, qkv, do, attended):
    images, full, width = attended.shape
    wide = pl.BlockSpec((1, full, 3 * width), lambda i: (i, 0, 0))
    long = pl.BlockSpec((1, full, width), lambda i: (i, 0, 0))
    return pl.pallas_call(
        functools.partial(attend_back, length),
        grid=(images,),
        out_shape=jax.ShapeDtypeStruct((images, full, 3 * width), BF),
        in_specs=[wide, long, long],
        out_specs=wide,
        compiler_params=params(),
    )(qkv, do, attended)


def proj_weight(a1_ref, dp_ref, g_ref, sum_ref, a1t):
    rows = a1_ref.shape[0]

    @pl.when(pl.program_id(0) == 0)
    def _():
        a1t[...] = a1_ref[...].T

    g_ref[...] = dot(a1t[...], dp_ref[...]).astype(BF)
    sum_ref[...] = jnp.sum(dp_ref[...].astype(F32).reshape(rows // 8, 8, -1), 0)


def run_proj_weight(a1, dp):
    rows, width = a1.shape
    cols = pl.BlockSpec((rows, width), lambda n: (0, n))
    return pl.pallas_call(
        proj_weight,
        grid=(3,),
        out_shape=(jax.ShapeDtypeStruct((width, 3 * width), BF), jax.ShapeDtypeStruct((8, 3 * width), F32)),
        in_specs=[whole_block((rows, width)), cols],
        out_specs=(pl.BlockSpec((width, width), lambda n: (0, n)), pl.BlockSpec((8, width), lambda n: (0, n))),
        scratch_shapes=[pltpu.VMEM((width, rows), BF)],
        compiler_params=params(),
    )(a1, dp)


def proj_input(dp_ref, w_ref, x_ref, dh_ref, vec_ref, out_ref, sum_ref, xpad):
    n, full, width = dh_ref.shape
    length = x_ref.shape[1]
    rows = n * full

    @pl.when(pl.program_id(0) == 0)
    def _():
        sum_ref[...] = jnp.zeros_like(sum_ref)

    da = dot_t(dp_ref[...].reshape(rows, 3 * width), w_ref[...])
    normed, rstd = normalize(pad_images(x_ref, xpad))
    grad = dh_ref[...].reshape(rows, width) + norm_back(da, normed, rstd, vec_ref[4:5, :])
    grad = grad.astype(BF).reshape(n, full, width)
    for i in range(n):
        out_ref[i] = grad[i, :length, :]
    sum_ref[0:1, :] += jnp.sum(da * normed, 0, keepdims=True)
    sum_ref[1:2, :] += jnp.sum(da, 0, keepdims=True)


def run_proj_input(dp, wq, tokens, dh, vecs):
    images, length, width = tokens.shape
    full = dh.shape[1]
    n = images // 2
    short = pl.BlockSpec((n, length, width), lambda i: (i, 0, 0))
    long = pl.BlockSpec((n, full, width), lambda i: (i, 0, 0))
    return pl.pallas_call(
        proj_input,
        grid=(2,),
        out_shape=(jax.ShapeDtypeStruct(tokens.shape, BF), jax.ShapeDtypeStruct((8, width), F32)),
        in_specs=[
            pl.BlockSpec((n, full, 3 * width), lambda i: (i, 0, 0)),
            whole_block(wq.shape), short, long, whole_block(vecs.shape),
        ],
        out_specs=(short, whole_block((8, width))),
        scratch_shapes=[pltpu.VMEM((n, full, width), F32)],
        compiler_params=params(),
    )(dp, wq, tokens, dh, vecs)


def reduce_grads(ng, nz, *refs):
    n = 4
    grads, vec_hbm = refs[:n], refs[n]
    outs, vec_out = refs[n + 1 : 2 * n + 1], refs[2 * n + 1]
    rest = refs[2 * n + 2 :]
    gs, rc, rx, tz, rz, fin = (rest[i * n : (i + 1) * n] for i in range(6))
    v_s, v_g, v_z, v_c = rest[6 * n : 6 * n + 4]
    (in_sem, c_send, c_recv, x_send, x_recv, z_send, z_recv, a_send, a_recv, f_send, f_recv, o_sem,
     vg_send, vg_recv, vz_send, vz_recv, vc_send, vc_recv) = rest[6 * n + 4 :]
    r, g = lax.axis_index("replica"), lax.axis_index("group")
    c, z = lax.rem(r, 2), lax.div(r, 2)
    sib = flip(r, 1)
    to_sib = {"replica": sib, "group": g}

    def to_group(k):
        return {"replica": r, "group": flip(g, k)}

    def to_chip(j):
        return {"replica": flip(r, 2 * j), "group": g}

    def remote(src, dst, send, recv, target):
        return pltpu.make_async_remote_copy(src, dst, send, recv, device_id=target, device_id_type=MESH)

    loads = [pltpu.make_async_copy(grads[i], gs[i], in_sem.at[i]) for i in range(n)]
    v_load = pltpu.make_async_copy(vec_hbm, v_s, in_sem.at[n])
    for load in loads:
        load.start()
    v_load.start()
    barrier = pltpu.get_barrier_semaphore()
    pl.semaphore_signal(barrier, inc=1, device_id=to_sib, device_id_type=MESH)
    for k in range(1, ng):
        pl.semaphore_signal(barrier, inc=1, device_id=to_group(k), device_id_type=MESH)
    for j in range(1, nz):
        pl.semaphore_signal(barrier, inc=1, device_id=to_chip(j), device_id_type=MESH)
    pl.semaphore_wait(barrier, ng + nz - 1)

    def half(i):
        return rc[i].shape[1]

    def core_copies(i):
        h = half(i)
        return [
            remote(gs[i].at[rows_at(m * 2 * h + (1 - c) * h, h), :], rc[i].at[m], c_send.at[i, m], c_recv.at[i, m], to_sib)
            for m in range(ng)
        ]

    def group_copies(i):
        return [
            remote(rc[i].at[flip(g, k)], rx[i].at[k - 1], x_send.at[i, k - 1], x_recv.at[i, k - 1], to_group(k))
            for k in range(1, ng)
        ]

    def chip_copies(i):
        return [
            remote(tz[i].at[flip(z, j)], rz[i].at[j - 1], z_send.at[i, j - 1], z_recv.at[i, j - 1], to_chip(j))
            for j in range(1, nz)
        ]

    def back_copies(i):
        part = fin[i].at[c, z]
        return [remote(part, part, a_send.at[i, j - 1], a_recv.at[i, j - 1], to_chip(j)) for j in range(1, nz)]

    def last_copies(i):
        copies = []
        for j in range(nz):
            part = fin[i].at[c, flip(z, j)]
            copies.append(remote(part, part, f_send.at[i, j], f_recv.at[i, j], to_sib))
        return copies

    def start(copies):
        for copy in copies:
            copy.start()

    def wait_recv(copies):
        for copy in copies:
            copy.wait_recv()

    def wait_send(copies):
        for copy in copies:
            copy.wait_send()

    def stage_core(i):
        loads[i].wait()
        start(core_copies(i))

    def stage_group(i):
        h = half(i)
        wait_recv(core_copies(i))
        for k in list(range(1, ng)) + [0]:
            m = flip(g, k)
            mine = gs[i][rows_at(m * 2 * h + c * h, h), :]
            rc[i][m] = (mine.astype(F32) + rc[i][m].astype(F32)).astype(BF)
            if k:
                group_copies(i)[k - 1].start()

    def stage_chip(i):
        wait_recv(group_copies(i))
        total = rc[i][g].astype(F32)
        for k in range(ng - 1):
            total = total + rx[i][k].astype(F32)
        p = half(i) // nz
        for j in range(nz):
            tz[i][j] = total[j * p : (j + 1) * p].astype(BF)
        start(chip_copies(i))

    def stage_back(i):
        wait_recv(chip_copies(i))
        total = tz[i][z].astype(F32)
        for j in range(nz - 1):
            total = total + rz[i][j].astype(F32)
        fin[i][c, z] = total.astype(BF)
        start(back_copies(i))

    def stage_last(i):
        copies = last_copies(i)
        copies[0].start()
        back = back_copies(i)
        for j in range(1, nz):
            back[j - 1].wait_recv()
            copies[j].start()

    def stage_out(i):
        wait_recv(last_copies(i))
        pltpu.make_async_copy(fin[i], outs[i], o_sem.at[i]).start()

    for i in range(n):
        stage_core(i)

    v_load.wait()
    vg = [remote(v_s, v_g.at[k - 1], vg_send.at[k - 1], vg_recv.at[k - 1], to_group(k)) for k in range(1, ng)]
    vz = [remote(v_s, v_z.at[j - 1], vz_send.at[j - 1], vz_recv.at[j - 1], to_chip(j)) for j in range(1, nz)]
    vc = [remote(v_s, v_c.at[0], vc_send.at[0], vc_recv.at[0], to_sib)]

    def vec_step(copies, landed, following):
        wait_recv(copies)
        wait_send(copies)
        total = v_s[...]
        for j in range(landed.shape[0]):
            total = total + landed[j]
        v_s[...] = total
        start(following)

    start(vg)
    stages = [stage_group, stage_chip, stage_back, stage_last, stage_out]
    for tick in range(n + len(stages) - 1):
        for depth in reversed(range(len(stages))):
            if 0 <= tick - depth < n:
                stages[depth](tick - depth)
        if tick == 1:
            vec_step(vg, v_g, vz)
        if tick == 2:
            vec_step(vz, v_z, vc)
        if tick == 3:
            vec_step(vc, v_c, [])
            vec_out[...] = v_s[...]
    for i in range(n):
        for copies in (core_copies(i), group_copies(i), chip_copies(i), back_copies(i), last_copies(i)):
            wait_send(copies)
        pltpu.make_async_copy(fin[i], outs[i], o_sem.at[i]).wait()


def run_reduce(ng, nr, grads, vec_sums):
    nz = nr // 2
    any_spec = pl.BlockSpec(memory_space=pl.ANY)
    dma = pltpu.SemaphoreType.DMA
    halves = [g.shape[0] // ng // 2 for g in grads]
    cols = [g.shape[1] for g in grads]
    fin_shapes = [(2, nz, h // nz, w) for h, w in zip(halves, cols)]
    n = len(grads)
    scratch = [pltpu.VMEM(g.shape, BF) for g in grads]
    scratch += [pltpu.VMEM((ng, h, w), BF) for h, w in zip(halves, cols)]
    scratch += [pltpu.VMEM((ng - 1, h, w), BF) for h, w in zip(halves, cols)]
    scratch += [pltpu.VMEM((nz, h // nz, w), BF) for h, w in zip(halves, cols)]
    scratch += [pltpu.VMEM((nz - 1, h // nz, w), BF) for h, w in zip(halves, cols)]
    scratch += [pltpu.VMEM(s, BF) for s in fin_shapes]
    scratch += [pltpu.VMEM(vec_sums.shape, F32)]
    scratch += [pltpu.VMEM((m,) + vec_sums.shape, F32) for m in (ng - 1, nz - 1, 1)]
    scratch += [dma((n + 1,))]
    for m in (ng, ng - 1, nz - 1, nz - 1, nz):
        scratch += [dma((n, m)), dma((n, m))]
    scratch += [dma((n,))]
    for m in (ng - 1, nz - 1, 1):
        scratch += [dma((m,)), dma((m,))]
    out = pl.pallas_call(
        functools.partial(reduce_grads, ng, nz),
        out_shape=tuple(jax.ShapeDtypeStruct(s, BF) for s in fin_shapes) + (jax.ShapeDtypeStruct(vec_sums.shape, F32),),
        in_specs=[any_spec] * (n + 1),
        out_specs=(any_spec,) * n + (pl.BlockSpec(memory_space=pltpu.VMEM),),
        scratch_shapes=scratch,
        compiler_params=params(collective_id=1, has_side_effects=True),
    )(*grads, vec_sums)
    totals = [o.reshape(2 * h, w).astype(F32) for o, h, w in zip(out[:n], halves, cols)]
    return totals, out[n]


def adamw_update(weight, first_moment, second, gradient, step_rate, decay_coef):
    first_new = beta_one * first_moment + (1.0 - beta_one) * gradient
    second_new = beta_two * second + (1.0 - beta_two) * gradient * gradient
    fix_one = 1.0 - beta_one**STEP
    fix_two = 1.0 - beta_two**STEP
    weight_new = weight - step_rate * (
        first_new / fix_one / (jnp.sqrt(second_new / fix_two) + adam_eps) + decay_coef * weight
    )
    return (first_new, second_new, weight_new)


def per_device(
    ng, nr, tokens, cotangent, w_qkv, m_qkv, v_qkv, w_out, m_out, v_out, w_up, m_up, v_up,
    w_down, m_down, v_down, vectors, m_vectors, v_vectors,
):
    images, length, width = tokens.shape
    full = -(-length // 16) * 16
    rows = images * full
    wq, wo, wu, wd, vecs, a1, qkv, attended = run_gather_attend(ng, full, tokens, w_qkv, w_out, w_up, w_down, vectors)
    h, a2, dm = run_mid(tokens, attended, cotangent, wo, vecs)
    acc, da, g_down, g_up, g_bu = run_mlp(
        a2.reshape(rows, width), dm.reshape(rows, width), wu, wd, vecs[8:].reshape(1, -1)
    )
    output, dh, do, g_out, sums_two = run_post(h, acc, da, cotangent, attended, wo, vecs)
    dp = run_attend_back(length, qkv, do, attended)
    g_qkv, proj_sums = run_proj_weight(a1.reshape(rows, width), dp.reshape(rows, 3 * width))
    input_grad, sums_one = run_proj_input(dp, wq, tokens, dh, vecs)
    proj_sum = jnp.sum(proj_sums, 0, keepdims=True)
    vec_sums = jnp.concatenate(
        [
            proj_sum[:, :width], proj_sum[:, 2 * width :], sums_two[0:2], sums_one[0:2], sums_two[2:4],
            g_bu.reshape(-1, width),
        ],
        0,
    )
    totals, vec_total = run_reduce(ng, nr, (g_down, g_up, g_out, g_qkv), vec_sums)
    own = vectors.shape[1]
    vec_total = lax.dynamic_slice_in_dim(vec_total, lax.axis_index("group") * own, own, 1)
    states = (
        (w_qkv, m_qkv, v_qkv, totals[3], 0.1, 0.05),
        (w_out, m_out, v_out, totals[2], 0.1, 0.05),
        (w_up, m_up, v_up, totals[1], 0.1, 0.05),
        (w_down, m_down, v_down, totals[0], 0.1, 0.05),
        (vectors, m_vectors, v_vectors, vec_total, 0.8, 0.0),
    )
    outcome = [output, input_grad]
    for weight, first_moment, second, gradient, rate, decay in states:
        first_new, second_new, weight_new = adamw_update(weight, first_moment, second, gradient, rate, decay)
        outcome.extend([gradient, first_new, second_new, weight_new])
    return tuple(outcome)


def solution(mesh):
    ng, nr = mesh.shape["group"], mesh.shape["replica"]
    tokens_spec = P(("replica", "group"), None, None)
    rows_spec, cols_spec = P("group", None), P(None, "group")
    in_specs = (tokens_spec,) * 2 + (rows_spec,) * 12 + (cols_spec,) * 3
    out_specs = (tokens_spec,) * 2 + (rows_spec,) * 16 + (cols_spec,) * 4
    return jax.shard_map(
        functools.partial(per_device, ng, nr), mesh=mesh, in_specs=in_specs, out_specs=out_specs, check_vma=False
    )
```

```python
import functools

import jax
import jax.numpy as jnp
from jax import lax
from jax.experimental import pallas as pl
from jax.experimental.pallas import tpu as pltpu
from jax.sharding import PartitionSpec as P

F32 = jnp.float32
BF = jnp.bfloat16
HEADS = 12
HEAD_DIM = 64
STEP = 10
MIB = 2**20
MESH = pl.DeviceIdType.MESH

norm_eps = 1e-06
beta_one = 0.9
beta_two = 0.999
adam_eps = 1e-08


def dot(a, b):
    return jnp.dot(a, b, preferred_element_type=F32)


def dot_t(a, b):
    return lax.dot_general(a, b, (((1,), (1,)), ((), ())), preferred_element_type=F32)


def flip(index, mask):
    out, bit = index, 1
    while bit <= mask:
        if mask & bit:
            out = out + bit * (1 - 2 * lax.rem(lax.div(index, bit), 2))
        bit *= 2
    return out


def rows_at(start, size):
    return pl.ds(pl.multiple_of(start, 16), size)


def normalize(hidden):
    centered = hidden - jnp.mean(hidden, -1, keepdims=True)
    rstd = lax.rsqrt(jnp.mean(centered * centered, -1, keepdims=True) + norm_eps)
    return centered * rstd, rstd


def norm_back(grad, normed, rstd, gain):
    e = grad * gain
    mean_e = jnp.mean(e, -1, keepdims=True)
    mean_en = jnp.mean(e * normed, -1, keepdims=True)
    return (e - mean_e - normed * mean_en) * rstd


def gelu_parts(u):
    x = jnp.abs(u) * 0.7071067811865476
    t = 1.0 / (1.0 + 0.3275911 * x)
    e = jnp.exp(-x * x)
    poly = (
        (((1.061405429 * t - 1.453152027) * t + 1.421413741) * t - 0.284496736) * t + 0.254829592
    ) * t
    q = 0.5 * poly * e
    phi = jnp.where(u > 0, 1.0 - q, q)
    return u * phi, phi + u * (e * 0.3989422804014327)


def pad_images(x_ref, scratch):
    n, length, width = x_ref.shape
    full = scratch.shape[1]
    for i in range(n):
        scratch[i, 0:length, :] = x_ref[i].astype(F32)
        scratch[i, length:full, :] = jnp.zeros((full - length, width), F32)
    return scratch[...].reshape(n * full, width)


def whole_block(shape):
    return pl.BlockSpec(shape, lambda *_: (0,) * len(shape), pipeline_mode=pl.Buffered(1))


def params(mib=58, **kw):
    return pltpu.CompilerParams(vmem_limit_bytes=mib * MIB, **kw)


class Places:
    def __init__(self, ng, nz):
        self.ng, self.nz = ng, nz
        self.r, self.g = lax.axis_index("replica"), lax.axis_index("group")
        self.c, self.z = lax.rem(self.r, 2), lax.div(self.r, 2)
        self.sib = {"replica": flip(self.r, 1), "group": self.g}

    def group(self, k):
        return {"replica": self.r, "group": flip(self.g, k)}

    def chip(self, j):
        return {"replica": flip(self.r, 2 * j), "group": self.g}

    def greet(self, group, chips):
        barrier = pltpu.get_barrier_semaphore()
        targets = [self.sib]
        if group:
            targets += [self.group(k) for k in range(1, self.ng)]
        if chips:
            targets += [self.chip(j) for j in range(1, self.nz)]
        for target in targets:
            pl.semaphore_signal(barrier, inc=1, device_id=target, device_id_type=MESH)
        pl.semaphore_wait(barrier, len(targets))


def remote(src, dst, send, recv, target):
    return pltpu.make_async_remote_copy(src, dst, send, recv, device_id=target, device_id_type=MESH)


class Gather:
    def __init__(self, at, buf, sems):
        self.at, self.buf = at, buf
        self.x_send, self.x_recv, self.f_send, self.f_recv = sems
        self.half = buf.shape[0] // at.ng // 2
        self.relay = at.ng == 4

    def rows(self, k, c, lower=None):
        start, size = flip(self.at.g, k) * 2 * self.half + c * self.half, self.half
        if lower is not None:
            size = self.half // 2
            start = start + (0 if lower else size)
        return self.buf.at[rows_at(start, size), :]

    def direct(self, k):
        part = self.rows(0, self.at.c)
        return remote(part, part, self.x_send.at[k - 1], self.x_recv.at[k - 1], self.at.group(k))

    def relayed(self, k):
        part = self.rows(k, self.at.c, k == 1)
        return remote(part, part, self.x_send.at[1 + k], self.x_recv.at[1 + k], self.at.group(3 - k))

    def relayed_in(self, k):
        part = self.rows(3, self.at.c, k == 1)
        return remote(part, part, self.x_send.at[1 + k], self.x_recv.at[1 + k], self.at.group(3 - k))

    def across(self, k):
        part = self.rows(k, self.at.c)
        return remote(part, part, self.f_send.at[k - 1], self.f_recv.at[k - 1], self.at.sib)

    def across_in(self, k):
        part = self.rows(k, 1 - self.at.c)
        return remote(part, part, self.f_send.at[k - 1], self.f_recv.at[k - 1], self.at.sib)

    def near(self):
        return (1, 2) if self.relay else range(1, self.at.ng)

    def start(self):
        for k in self.near():
            self.direct(k).start()

    def pass_on(self):
        for k in self.near():
            self.direct(k).wait_recv()
            if self.relay:
                self.relayed(k).start()
            self.across(k).start()

    def settle(self):
        if self.relay:
            for k in (1, 2):
                self.relayed_in(k).wait_recv()
            self.across(3).start()

    def finish(self):
        for k in range(1, self.at.ng):
            self.across_in(k).wait_recv()

    def close(self):
        for k in self.near():
            self.direct(k).wait_send()
            if self.relay:
                self.relayed(k).wait_send()
        for k in range(1, self.at.ng):
            self.across(k).wait_send()


def gather_sems(ng):
    dma = pltpu.SemaphoreType.DMA
    n = 4 if ng == 4 else ng - 1
    return [dma((n,)), dma((n,)), dma((ng - 1,)), dma((ng - 1,))]


def strips(ng, ff):
    share = ff // ng
    one = -(-share // 256) * 128
    return share, one, share - one


def tile_of(size):
    return 768 if size % 768 == 0 else 512


def mlp_tile(t, ft, blocks, a2, a2t, dm, wu, wd, bias, acc, da_acc, act_s, du_s, sums, gd_slot, gu_slot, gbu, before=(), ready=lambda i: None):
    units = slice(t * ft, (t + 1) * ft)
    sums[...] = jnp.zeros_like(sums)
    rows = acc.shape[0] // blocks

    def body(i, _):
        im = rows_at(i * rows, rows)
        u = dot(a2[im, :], wu[:, units]) + bias[:, units]
        da = dot_t(dm[im, :], wd[units, :])
        act, slope = gelu_parts(u)
        act = act.astype(BF)
        du = (da * slope).astype(BF)
        act_s[im, 0:ft] = act
        du_s[im, 0:ft] = du
        sums[...] += jnp.sum(du.astype(F32).reshape(rows // 8, 8, ft), 0)
        ready(i)
        acc[im, :] += dot(act, wd[units, :])
        da_acc[im, :] += dot_t(du, wu[:, units])
        return 0

    lax.fori_loop(0, blocks, body, 0)
    for step in before:
        step()
    gd_slot[...] = dot(act_s[:, 0:ft].T, dm[...]).astype(BF)
    gu_slot[...] = dot(a2t[...], du_s[:, 0:ft]).astype(BF)
    gbu[:, units] = jnp.sum(sums[...], 0, keepdims=True)


def forward(ng, nz, length, *refs):
    at = Places(ng, nz)
    (x_hbm, cot_hbm, wq_hbm, wo_hbm, wu_hbm, wd_hbm, vec_hbm,
     wq_out, wo_out, u2_out, d2_out, vec_out, a1_out, qkv_out, o_out, a2_out, dm_out, h_out, acc_out, da_out, gd_out, gu_out, gbu_out,
     xs, cs, acc, da, h, bq, bo, bu1, bd1, bu2, bd2, vec_s, vall, a1o, qkv, dm, a2t, sums, xf,
     w_sem, v_sem, in_sem, v_send, v_recv, out_sem, g_sem) = refs[:49]
    gathers = [Gather(at, buf, refs[49 + 4 * i : 53 + 4 * i]) for i, buf in enumerate((bq, bo, bu1, bd1, bu2, bd2))]
    g_q, g_o, g_u1, g_d1, g_u2, g_d2 = gathers
    width = h.shape[1]
    images = xs.shape[0] // length
    full = h.shape[0] // images
    shard = wq_hbm.shape[0]
    ff = wu_hbm.shape[1]
    share, one, two = strips(ng, ff)
    nq, nu = wq_hbm.shape[1] // width, ff // width

    flat, flat_h = acc, h
    loads = []
    for n in range(nq):
        loads.append((wq_hbm.at[:, n * width : (n + 1) * width], flat.at[n * shard : (n + 1) * shard]))
    loads.append((wo_hbm, flat.at[nq * shard : (nq + 1) * shard]))
    for n in range(nu):
        loads.append((wu_hbm.at[:, n * width : (n + 1) * width], flat.at[(nq + 1 + n) * shard : (nq + 2 + n) * shard]))
    loads.append((wd_hbm, flat_h.at[0:share]))
    loads = [pltpu.make_async_copy(src, dst, w_sem.at[i]) for i, (src, dst) in enumerate(loads)]
    vec_load = pltpu.make_async_copy(vec_hbm, vec_s, v_sem)
    x_load = pltpu.make_async_copy(x_hbm, xs, in_sem.at[0])
    cot_load = pltpu.make_async_copy(cot_hbm, cs, in_sem.at[1])
    vec_load.start()
    for n in range(nq):
        loads[n].start()
    x_load.start()
    for load in loads[nq:]:
        load.start()
    cot_load.start()
    at.greet(True, False)

    vec_load.wait()
    vall[at.g] = vec_s[...].astype(BF).astype(F32)
    v_copies = [remote(vall.at[at.g], vall.at[at.g], v_send.at[k - 1], v_recv.at[k - 1], at.group(k)) for k in range(1, ng)]
    for copy in v_copies:
        copy.start()
    for n in range(nq):
        loads[n].wait()
        bq[rows_at(at.g * shard, shard), n * width : (n + 1) * width] = flat[n * shard : (n + 1) * shard, :].astype(BF)
    g_q.start()
    loads[nq].wait()
    bo[rows_at(at.g * shard, shard), :] = flat[nq * shard : (nq + 1) * shard, :].astype(BF)
    for n in range(nu):
        loads[nq + 1 + n].wait()
    for m in range(ng):
        block, col = divmod(m * share, width)
        src = slice((nq + 1 + block) * shard, (nq + 2 + block) * shard)
        bu1[rows_at(at.g * shard, shard), m * one : (m + 1) * one] = flat[src, col : col + one].astype(BF)
        bu2[rows_at(at.g * shard, shard), m * two : (m + 1) * two] = flat[src, col + one : col + share].astype(BF)
    loads[nq + 1 + nu].wait()
    bd1[rows_at(at.g * one, one), :] = flat_h[0:one, :].astype(BF)
    bd2[rows_at(at.g * two, two), :] = flat_h[one:share, :].astype(BF)

    for copy in v_copies:
        copy.wait()
    w = vall.shape[2]
    vecs = jnp.zeros((vall.shape[1], width), F32)
    for j in range(ng):
        row = lax.broadcasted_iota(jnp.int32, (w, width), 0)
        col = lax.broadcasted_iota(jnp.int32, (w, width), 1)
        vecs = vecs + dot(vall[j].astype(BF), jnp.where(col == row + j * w, 1.0, 0.0).astype(BF))
    vec_out[...] = vecs

    x_load.wait()
    lanes = width // 128

    def spread(ref):
        for j in range(lanes):
            xf[j, 0 : length * images, :] = ref[:, j * 128 : (j + 1) * 128].astype(F32)

    def image_of(i):
        return jnp.concatenate([xf[j, pl.ds(i, full, stride=images), :] for j in range(lanes)], 1)

    xf[:, length * images :, :] = jnp.zeros((lanes, (full - length) * images, 128), F32)
    spread(xs)

    def norm_image(i, _):
        im = rows_at(i * full, full)
        x = image_of(i)
        h[im, :] = x
        normed, _r = normalize(x)
        a1o[im, :] = (normed * vec_out[4:5, :] + vec_out[5:6, :]).astype(BF)
        return 0

    lax.fori_loop(0, images, norm_image, 0)
    a1_copy = pltpu.make_async_copy(a1o, a1_out, out_sem.at[0])
    a1_copy.start()
    cot_load.wait()
    spread(cs)

    def cot_image(i, _):
        dm[rows_at(i * full, full), :] = image_of(i).astype(BF)
        return 0

    g_q.pass_on()
    for gather in (g_o, g_u1, g_d1):
        gather.start()
    lax.fori_loop(0, images, cot_image, 0)
    dm_copy = pltpu.make_async_copy(dm, dm_out, out_sem.at[1])
    dm_copy.start()
    g_q.settle()
    g_q.finish()
    wq_copy = pltpu.make_async_copy(bq, wq_out, out_sem.at[2])
    wq_copy.start()

    zero = jnp.zeros((1, width), F32)
    biases = [vec_out[0:1, :], zero, vec_out[1:2, :]]
    block = images * full // 2

    def project(i, _):
        im = rows_at(i * block, block)
        a1 = a1o[im, :]
        for n in range(3):
            cols = slice(n * width, (n + 1) * width)
            qkv[im, cols] = (dot(a1, bq[:, cols]) + biases[n]).astype(BF)
        return 0

    lax.fori_loop(0, 2, project, 0)
    qkv_copy = pltpu.make_async_copy(qkv, qkv_out, out_sem.at[3])
    qkv_copy.start()
    a1_copy.wait()

    low_half = lax.broadcasted_iota(jnp.int32, (full, 128), 1) < HEAD_DIM
    key_bias = jnp.where(lax.broadcasted_iota(jnp.int32, (1, full), 1) < length, 0.0, -1e30).astype(F32)
    ones = jnp.ones((full, 128), BF)

    def when(i, index, *steps):
        @pl.when(i == index)
        def _():
            for step in steps:
                step()

    def attend(i, _):
        when(i, 0, g_o.pass_on)
        when(i, 2, g_o.settle, g_u1.pass_on)
        when(i, 6, g_u1.settle, g_d1.pass_on, g_u2.start, g_d2.start)
        im = rows_at(i * full, full)
        for p in range(HEADS // 2):
            col = p * 128
            q = qkv[im, col : col + 128] * jnp.asarray(HEAD_DIM**-0.5, BF)
            k = qkv[im, col + width : col + width + 128]
            v = jnp.concatenate([qkv[im, col + 2 * width : col + 2 * width + 128], ones], axis=1)
            heads = []
            for hd in range(2):
                mine = low_half if hd == 0 else ~low_half
                s = dot_t(jnp.where(mine, q, jnp.zeros_like(q)), k) + key_bias
                e = jnp.exp(s - jnp.max(s, -1, keepdims=True)).astype(BF)
                both = dot(e, v)
                heads.append(both[:, :128] / both[:, 128:])
            a1o[im, col : col + 128] = jnp.where(low_half, heads[0], heads[1]).astype(BF)
        return 0

    lax.fori_loop(0, images, attend, 0)
    o_copy = pltpu.make_async_copy(a1o, o_out, out_sem.at[4])
    o_copy.start()
    g_o.finish()
    wo_copy = pltpu.make_async_copy(bo, wo_out, out_sem.at[5])
    wo_copy.start()
    qkv_copy.wait()

    def middle(i, _):
        im = rows_at(i * block, block)
        hidden = h[im, :] + dot(a1o[im, :], bo[...]) + vec_out[2:3, :]
        h[im, :] = hidden
        normed, _r = normalize(hidden)
        qkv[im, 0:width] = (normed * vec_out[6:7, :] + vec_out[7:8, :]).astype(BF)
        acc[im, :] = jnp.zeros((block, width), F32)
        da[im, :] = jnp.zeros((block, width), F32)
        return 0

    lax.fori_loop(0, 2, middle, 0)
    a2_copy = pltpu.make_async_copy(qkv.at[:, 0:width], a2_out, out_sem.at[6])
    h_copy = pltpu.make_async_copy(h, h_out, out_sem.at[7])
    a2_copy.start()
    h_copy.start()
    g_d1.settle()
    a2t[...] = qkv[:, 0:width].T
    g_u1.finish()
    g_d1.finish()

    bias = unit_bias(vec_out, ng, share, 0, one)
    ft = tile_of(ng * one)
    tiles = ng * one // ft
    slots = [(ref, n * width) for ref in (xs, cs) for n in range(2)]
    acc_copy = pltpu.make_async_copy(acc, acc_out, out_sem.at[8])
    da_copy = pltpu.make_async_copy(da, da_out, out_sem.at[9])
    pending = []
    for t in range(tiles):
        if t == 1:
            g_u2.pass_on()
            g_d2.pass_on()
        if t >= 2:
            for copy in pending[2 * (t - 2) : 2 * (t - 1)]:
                copy.wait()
        gd_slot, gu_slot = [ref.at[start : start + width] for ref, start in slots[2 * (t % 2) : 2 * (t % 2) + 2]]
        gd_slot, gu_slot = gd_slot.at[0:ft], gu_slot.at[:, 0:ft]
        last = t == tiles - 1
        mlp_tile(
            t, ft, 2, qkv.at[:, 0:width], a2t, dm, bu1, bd1, bias, acc, da,
            qkv.at[:, width : 2 * width], qkv.at[:, 2 * width : 3 * width], sums.at[:, 0:ft], gd_slot, gu_slot, gbu_out,
            (acc_copy.start, da_copy.start, g_u2.settle, g_d2.settle) if last else (),
        )
        units = slice(t * ft, (t + 1) * ft)
        pending.append(pltpu.make_async_copy(gd_slot, gd_out.at[units, :], g_sem.at[0, t]))
        pending.append(pltpu.make_async_copy(gu_slot, gu_out.at[:, units], g_sem.at[1, t]))
        for copy in pending[-2:]:
            copy.start()
    g_u2.finish()
    g_d2.finish()
    u2_copy = pltpu.make_async_copy(bu2, u2_out, out_sem.at[10])
    d2_copy = pltpu.make_async_copy(bd2, d2_out, out_sem.at[11])
    u2_copy.start()
    d2_copy.start()
    for gather in gathers:
        gather.close()
    for copy in pending[-4:] + [dm_copy, wq_copy, o_copy, wo_copy, a2_copy, h_copy, acc_copy, da_copy, u2_copy, d2_copy]:
        copy.wait()


def unit_bias(vec_ref, ng, share, start, size):
    width = vec_ref.shape[1]
    parts = []
    for m in range(ng):
        row, col = divmod(m * share + start, width)
        parts.append(vec_ref[8 + row : 9 + row, col : col + size])
    return jnp.concatenate(parts, 1)


def run_forward(ng, nr, full, tokens, cotangent, w_qkv, w_out, w_up, w_down, vectors):
    images, length, width = tokens.shape
    ff = w_up.shape[1]
    share, one, two = strips(ng, ff)
    f1, f2 = ng * one, ng * two
    any_spec = pl.BlockSpec(memory_space=pl.ANY)
    vmem = pl.BlockSpec(memory_space=pltpu.VMEM)
    dma = pltpu.SemaphoreType.DMA
    rows_like = (images * full, width)
    flat = (length * images, width)
    ft = tile_of(f1)

    def bf(*shape):
        return jax.ShapeDtypeStruct(shape, BF)

    def f32(*shape):
        return jax.ShapeDtypeStruct(shape, F32)

    n_loads = w_qkv.shape[1] // width + ff // width + 2
    return pl.pallas_call(
        functools.partial(forward, ng, nr // 2, length),
        out_shape=(
            bf(width, 3 * width), bf(width, width), bf(width, f2), bf(f2, width), f32(vectors.shape[0], width),
            bf(*rows_like), bf(images * full, 3 * width), bf(*rows_like), bf(*rows_like), bf(*rows_like),
            f32(*rows_like), f32(*rows_like), f32(*rows_like), bf(f1, width), bf(width, f1), f32(1, f1),
        ),
        in_specs=[any_spec] * 7,
        out_specs=(any_spec,) * 4 + (vmem,) + (any_spec,) * 10 + (vmem,),
        scratch_shapes=[
            pltpu.VMEM(flat, BF),
            pltpu.VMEM(flat, BF),
            pltpu.VMEM(rows_like, F32),
            pltpu.VMEM(rows_like, F32),
            pltpu.VMEM(rows_like, F32),
            pltpu.VMEM((width, 3 * width), BF),
            pltpu.VMEM((width, width), BF),
            pltpu.VMEM((width, f1), BF),
            pltpu.VMEM((f1, width), BF),
            pltpu.VMEM((width, f2), BF),
            pltpu.VMEM((f2, width), BF),
            pltpu.VMEM(vectors.shape, F32),
            pltpu.VMEM((ng,) + vectors.shape, F32),
            pltpu.VMEM(rows_like, BF),
            pltpu.VMEM((images * full, 3 * width), BF),
            pltpu.VMEM(rows_like, BF),
            pltpu.VMEM((width, images * full), BF),
            pltpu.VMEM((8, width), F32),
            pltpu.VMEM((width // 128, images * full, 128), F32),
            dma((n_loads,)),
            dma,
            dma((2,)),
            dma((ng - 1,)),
            dma((ng - 1,)),
            dma((12,)),
            dma((2, f1 // ft)),
        ]
        + gather_sems(ng) * 6,
        compiler_params=params(64, collective_id=0, has_side_effects=True),
    )(
        tokens.transpose(1, 0, 2).reshape(flat), cotangent.transpose(1, 0, 2).reshape(flat),
        w_qkv, w_out, w_up, w_down, vectors,
    )


class Early:
    def __init__(self, at, src, load, refs):
        self.at, self.src, self.mine = at, src, None
        if load:
            self.mine, refs = refs[0], refs[1:]
        self.rc, self.rx, self.tz, self.m_sem, self.c_send, self.c_recv, self.x_send, self.x_recv = refs[:8]
        self.rest = refs[8:]
        self.half = self.rc.shape[1]

    def load_copy(self, m):
        start = m * 2 * self.half + self.at.c * self.half
        return pltpu.make_async_copy(self.src.at[rows_at(start, self.half), :], self.mine.at[m], self.m_sem.at[m])

    def core_copy(self, m):
        start = m * 2 * self.half + (1 - self.at.c) * self.half
        return remote(self.src.at[rows_at(start, self.half), :], self.rc.at[m], self.c_send.at[m], self.c_recv.at[m], self.at.sib)

    def group_copy(self, k):
        return remote(self.rc.at[flip(self.at.g, k)], self.rx.at[k - 1], self.x_send.at[k - 1], self.x_recv.at[k - 1], self.at.group(k))

    def start_core(self):
        for m in range(self.at.ng):
            self.core_copy(m).start()
        if self.mine is not None:
            for m in range(self.at.ng):
                self.load_copy(m).start()

    def start_group(self):
        at, h = self.at, self.half
        for m in range(at.ng):
            self.core_copy(m).wait_recv()
            if self.mine is not None:
                self.load_copy(m).wait()
        for k in list(range(1, at.ng)) + [0]:
            m = flip(at.g, k)
            mine = self.src[rows_at(m * 2 * h + at.c * h, h), :] if self.mine is None else self.mine[m]
            self.rc[m] = (mine.astype(F32) + self.rc[m].astype(F32)).astype(BF)
            if k:
                self.group_copy(k).start()

    def collect(self):
        at = self.at
        for k in range(1, at.ng):
            self.group_copy(k).wait_recv()
        total = self.rc[at.g].astype(F32)
        for k in range(at.ng - 1):
            total = total + self.rx[k].astype(F32)
        p = self.half // at.nz
        for j in range(at.nz):
            self.tz[j] = total[j * p : (j + 1) * p].astype(BF)

    def close(self):
        for k in range(1, self.at.ng):
            self.group_copy(k).wait_send()
        for m in range(self.at.ng):
            self.core_copy(m).wait_send()


class Late:
    def __init__(self, at, tz, refs, out):
        self.at, self.tz, self.out = at, tz, out
        (self.rz, self.y, self.z_send, self.z_recv, self.a_send, self.a_recv, self.f_send, self.f_recv, self.o_sem) = refs[:9]
        self.rest = refs[9:]

    def chip_copy(self, j):
        return remote(self.tz.at[flip(self.at.z, j)], self.rz.at[j - 1], self.z_send.at[j - 1], self.z_recv.at[j - 1], self.at.chip(j))

    def back_copy(self, j, mine=True):
        place = self.out.at[self.at.c, self.at.z if mine else flip(self.at.z, j)]
        return remote(self.y, place, self.a_send.at[j - 1], self.a_recv.at[j - 1], self.at.chip(j))

    def last_copy(self, j, mine=True):
        place = self.out.at[self.at.c if mine else 1 - self.at.c, flip(self.at.z, j)]
        return remote(self.y if j == 0 else place, place, self.f_send.at[j], self.f_recv.at[j], self.at.sib)

    def keep_copy(self):
        return pltpu.make_async_copy(self.y, self.out.at[self.at.c, self.at.z], self.o_sem)

    def start_chips(self):
        for j in range(1, self.at.nz):
            self.chip_copy(j).start()

    def start_back(self):
        at = self.at
        for j in range(1, at.nz):
            self.chip_copy(j).wait_recv()
        total = self.tz[at.z].astype(F32)
        for j in range(at.nz - 1):
            total = total + self.rz[j].astype(F32)
        self.y[...] = total.astype(BF)
        for j in range(1, at.nz):
            self.back_copy(j).start()
        self.last_copy(0).start()
        self.keep_copy().start()

    def start_last(self):
        for j in range(1, self.at.nz):
            self.back_copy(j, mine=False).wait_recv()
            self.last_copy(j).start()

    def finish(self):
        at = self.at
        for j in range(at.nz):
            self.last_copy(j, mine=False).wait_recv()
            self.last_copy(j).wait_send()
        for j in range(1, at.nz):
            self.back_copy(j).wait_send()
            self.chip_copy(j).wait_send()
        self.keep_copy().wait()


def early_scratch(ng, nz, half, cols, load):
    dma = pltpu.SemaphoreType.DMA
    shapes = [pltpu.VMEM((ng, half, cols), BF)] if load else []
    shapes += [
        pltpu.VMEM((ng, half, cols), BF),
        pltpu.VMEM((ng - 1, half, cols), BF),
        pltpu.VMEM((nz, half // nz, cols), BF),
    ]
    return shapes + [dma((m,)) for m in (ng, ng, ng, ng - 1, ng - 1)]


def late_scratch(nz, half, cols):
    dma = pltpu.SemaphoreType.DMA
    p = half // nz
    shapes = [pltpu.VMEM((nz - 1, p, cols), BF), pltpu.VMEM((p, cols), BF)]
    for m in (nz - 1, nz - 1, nz):
        shapes += [dma((m,)), dma((m,))]
    return shapes + [dma]


def turn(ng, nz, length, *refs):
    at = Places(ng, nz)
    (a2_hbm, dm_hbm, h_hbm, acc_hbm, da_hbm, o_hbm, wo_hbm, wu_hbm, wd_hbm, gd1_hbm, gu1_hbm, vec_ref,
     out_out, dh_out, do_out, gd_out, gu_out, go_out, gbu_out, sum_out, td_out, tu_out,
     a2, a2t, dm, h, acc, da, o, wo, wu, wd, work, sums, out_s, go_s, slot_a, slot_b, slot_c, slot_d,
     blk_sem, big_sem, out_sem, g_sem, im_sem) = refs[:45]
    early_d = Early(at, gd1_hbm, True, refs[45:])
    early_u = Early(at, gu1_hbm, True, early_d.rest)
    rows, width = h.shape
    images = out_s.shape[0]
    full = rows // images
    half = rows // 2

    def block_copy(j, i):
        src, dst = ((a2_hbm, a2), (dm_hbm, dm), (acc_hbm, acc), (da_hbm, da))[j]
        part = rows_at(i * half, half)
        return pltpu.make_async_copy(src.at[part, :], dst.at[part, :], blk_sem.at[j, i])

    def big_copy(j):
        src, dst = ((wu_hbm, wu), (wd_hbm, wd), (h_hbm, h), (o_hbm, o), (wo_hbm, wo))[j]
        return pltpu.make_async_copy(src, dst, big_sem.at[j])

    block_copy(0, 0).start()
    big_copy(0).start()
    block_copy(1, 0).start()
    big_copy(1).start()
    for j, i in ((0, 1), (2, 0), (3, 0), (1, 1), (2, 1), (3, 1)):
        block_copy(j, i).start()
    for j in range(2, 5):
        big_copy(j).start()
    at.greet(True, False)
    early_d.start_core()
    early_u.start_core()
    for j, i in ((0, 0), (1, 0), (0, 1), (1, 1)):
        block_copy(j, i).wait()
    for j in range(2):
        big_copy(j).wait()
    a2t[...] = a2[...].T

    ff = wu.shape[1]
    share = ff // ng + gd1_hbm.shape[0] // ng
    bias = unit_bias(vec_ref, ng, share, gd1_hbm.shape[0] // ng, ff // ng)
    ft = tile_of(ff)
    tiles = ff // ft
    slots = ((slot_a, slot_b), (slot_c, slot_d))
    pending = []

    def sums_here(i):
        block_copy(2, i).wait()
        block_copy(3, i).wait()

    for t in range(tiles):
        if t >= 2:
            for copy in pending[2 * (t - 2) : 2 * (t - 1)]:
                copy.wait()
        gd_slot, gu_slot = slots[t % 2][0].at[0:ft], slots[t % 2][1].at[:, 0:ft]
        mlp_tile(
            t, ft, 2, a2, a2t, dm, wu, wd, bias, acc, da, work.at[:, 0:width], work.at[:, width : 2 * width],
            sums.at[:, 0:ft], gd_slot, gu_slot, gbu_out,
            (early_d.start_group, early_u.start_group) if t == 0 else (),
            sums_here if t == 0 else lambda i: None,
        )
        units = slice(t * ft, (t + 1) * ft)
        pending.append(pltpu.make_async_copy(gd_slot, gd_out.at[units, :], g_sem.at[0, t]))
        pending.append(pltpu.make_async_copy(gu_slot, gu_out.at[:, units], g_sem.at[1, t]))
        for copy in pending[-2:]:
            copy.start()

    for j in range(2, 5):
        big_copy(j).wait()
    sum_out[...] = jnp.zeros_like(sum_out)

    def out_copy(i):
        return pltpu.make_async_copy(out_s.at[i], out_out.at[i], im_sem.at[i])

    def post(b, _):
        im = rows_at(b * 2 * full, 2 * full)
        hidden = h[im, :]
        result = (hidden + acc[im, :] + vec_ref[3:4, :]).astype(BF).reshape(2, full, width)
        for i in range(2):
            out_s[b * 2 + i] = result[i, :length, :]
            out_copy(b * 2 + i).start()
        cot = dm[im, :].astype(F32)
        normed, rstd = normalize(hidden)
        grad = da[im, :]
        dh = cot + norm_back(grad, normed, rstd, vec_ref[6:7, :])
        h[im, :] = dh
        dz = dh.astype(BF)
        work[im, 0:width] = dz
        work[im, width : 2 * width] = dot_t(dz, wo[...]).astype(BF)
        for j, term in enumerate((dz.astype(F32), cot, grad * normed, grad)):
            sum_out[j : j + 1, :] += jnp.sum(term, 0, keepdims=True)
        return 0

    lax.fori_loop(0, images // 2, post, 0)
    dh_copy = pltpu.make_async_copy(h, dh_out, out_sem.at[0])
    do_copy = pltpu.make_async_copy(work.at[:, width : 2 * width], do_out, out_sem.at[1])
    dh_copy.start()
    do_copy.start()
    go_s[...] = dot(o[...].T, work[:, 0:width]).astype(BF)
    go_copy = pltpu.make_async_copy(go_s, go_out, out_sem.at[2])
    go_copy.start()
    early_d.collect()
    td_copy = pltpu.make_async_copy(early_d.tz, td_out, out_sem.at[3])
    td_copy.start()
    early_u.collect()
    tu_copy = pltpu.make_async_copy(early_u.tz, tu_out, out_sem.at[4])
    tu_copy.start()
    early_d.close()
    early_u.close()
    for copy in pending[-4:] + [dh_copy, do_copy, go_copy, td_copy, tu_copy]:
        copy.wait()
    for i in range(images):
        out_copy(i).wait()


def run_turn(ng, nr, cotangent, a2, dm, h, acc, da, o, wo, wu, wd, gd1, gu1, vecs):
    images, length, width = cotangent.shape
    nz = nr // 2
    rows = h.shape[0]
    ff = wu.shape[1]
    ft = tile_of(ff)
    any_spec = pl.BlockSpec(memory_space=pl.ANY)
    vmem = pl.BlockSpec(memory_space=pltpu.VMEM)
    dma = pltpu.SemaphoreType.DMA
    sizes = [(g.shape[0] // ng // 2, g.shape[1]) for g in (gd1, gu1)]

    def bf(*shape):
        return jax.ShapeDtypeStruct(shape, BF)

    def f32(*shape):
        return jax.ShapeDtypeStruct(shape, F32)

    scratch = [
        pltpu.VMEM((rows, width), BF),
        pltpu.VMEM((width, rows), BF),
        pltpu.VMEM((rows, width), BF),
        pltpu.VMEM((rows, width), F32),
        pltpu.VMEM((rows, width), F32),
        pltpu.VMEM((rows, width), F32),
        pltpu.VMEM((rows, width), BF),
        pltpu.VMEM((width, width), BF),
        pltpu.VMEM(wu.shape, BF),
        pltpu.VMEM(wd.shape, BF),
        pltpu.VMEM((rows, 2 * width), BF),
        pltpu.VMEM((8, width), F32),
        pltpu.VMEM(cotangent.shape, BF),
        pltpu.VMEM((width, width), BF),
        pltpu.VMEM((ft, width), BF),
        pltpu.VMEM((width, ft), BF),
        pltpu.VMEM((ft, width), BF),
        pltpu.VMEM((width, ft), BF),
        dma((4, 2)),
        dma((5,)),
        dma((5,)),
        dma((2, ff // ft)),
        dma((images,)),
    ]
    for hh, w in sizes:
        scratch += early_scratch(ng, nz, hh, w, True)
    return pl.pallas_call(
        functools.partial(turn, ng, nz, length),
        out_shape=(
            bf(*cotangent.shape), f32(rows, width), bf(rows, width), bf(ff, width), bf(width, ff), bf(width, width),
            f32(1, ff), f32(8, width),
        ) + tuple(bf(nz, hh // nz, w) for hh, w in sizes),
        in_specs=[any_spec] * 11 + [vmem],
        out_specs=(any_spec,) * 6 + (vmem, vmem, any_spec, any_spec),
        scratch_shapes=scratch,
        compiler_params=params(64, collective_id=1, has_side_effects=True),
    )(a2, dm, h, acc, da, o, wo, wu, wd, gd1, gu1, vecs)


def vector_sum(at, v_s, landed, sems):
    v_g, v_z, v_c = landed
    g_send, g_recv, z_send, z_recv, c_send, c_recv = sems

    def copies(level):
        if level == 0:
            return [remote(v_s.at[0], v_g.at[k - 1], g_send.at[k - 1], g_recv.at[k - 1], at.group(k)) for k in range(1, at.ng)]
        if level == 1:
            return [remote(v_s.at[1], v_z.at[j - 1], z_send.at[j - 1], z_recv.at[j - 1], at.chip(j)) for j in range(1, at.nz)]
        return [remote(v_s.at[2], v_c.at[0], c_send.at[0], c_recv.at[0], at.sib)]

    def start(level):
        for copy in copies(level):
            copy.start()

    def add(level):
        for copy in copies(level):
            copy.wait()
        total = v_s[level]
        buf = (v_g, v_z, v_c)[level]
        for j in range(buf.shape[0]):
            total = total + buf[j]
        v_s[level + 1] = total

    return start, add


def vector_scratch(ng, nz, shape):
    dma = pltpu.SemaphoreType.DMA
    shapes = [pltpu.VMEM((4,) + shape, F32)]
    shapes += [pltpu.VMEM((m,) + shape, F32) for m in (ng - 1, nz - 1, 1)]
    for m in (ng - 1, nz - 1, 1):
        shapes += [dma((m,)), dma((m,))]
    return shapes


PAIRS_A, PAIRS_B = (0, 1, 2, 3), (4, 5)


def backward(ng, nz, length, *refs):
    at = Places(ng, nz)
    (gd_hbm, gu_hbm, go_hbm, td1_hbm, tu1_hbm, qkv_hbm, do_hbm, o_hbm, a1_hbm, wq_hbm, x_hbm, dh_hbm, vec_ref, sum_ref, gbu1_ref, gbu2_ref,
     ig_out, td1_out, tu1_out, td_out, tu_out, to_out, ta_out, tb_out, vec_out,
     qkv_s, do_s, o_s, a1_s, a1t, wq_s, x_s, dh_s, xpad, inner_s, ga_s, gb_s, im_sem, big_sem, ig_sem, tz_d1, tz_u1, t_sem) = refs[:43]
    rest = refs[43:]
    early, late = [], []
    for src, load in ((gd_hbm, True), (gu_hbm, True), (go_hbm, True), (ga_s, False), (gb_s, False)):
        early.append(Early(at, src, load, rest))
        rest = early[-1].rest
    pieces = [tz_d1, tz_u1] + [e.tz for e in early]
    for tz, total in zip(pieces, (td1_out, tu1_out, td_out, tu_out, to_out, ta_out, tb_out)):
        late.append(Late(at, tz, rest, total))
        rest = late[-1].rest
    down, up, out, qa, qb = early
    down1_l, up1_l, down_l, up_l, out_l, qa_l, qb_l = late
    v_s = rest[0]
    v_start, v_add = vector_sum(at, v_s, rest[1:4], rest[4:10])

    images = x_s.shape[0]
    rows, width = do_s.shape
    full = rows // images
    scale = HEAD_DIM**-0.5

    def image_copies(i):
        return [
            pltpu.make_async_copy(src.at[rows_at(i * full, full), :], dst.at[rows_at(i * full, full), :], im_sem.at[j, i])
            for j, (src, dst) in enumerate(((qkv_hbm, qkv_s), (do_hbm, do_s), (o_hbm, o_s)))
        ]

    def big_copy(j):
        src, dst = ((a1_hbm, a1_s), (wq_hbm, wq_s), (x_hbm, x_s), (dh_hbm, dh_s))[j]
        return pltpu.make_async_copy(src, dst, big_sem.at[j])

    for i in range(images):
        for copy in image_copies(i):
            copy.start()
    for j in range(4):
        big_copy(j).start()
    tz_copies = [pltpu.make_async_copy(td1_hbm, tz_d1, t_sem.at[0]), pltpu.make_async_copy(tu1_hbm, tz_u1, t_sem.at[1])]
    for copy in tz_copies:
        copy.start()
    at.greet(True, True)
    for copy, reducer in zip(tz_copies, (down1_l, up1_l)):
        copy.wait()
        reducer.start_chips()
    down.start_core()
    up.start_core()
    out.start_core()

    cut = length // 16 * 16
    low_half = lax.broadcasted_iota(jnp.int32, (full, 128), 1) < HEAD_DIM
    pick = lax.broadcasted_iota(jnp.int32, (16, width), 1) // HEAD_DIM == lax.broadcasted_iota(jnp.int32, (16, width), 0)
    pick = jnp.where(pick, 1.0, 0.0).astype(BF)
    live = lax.broadcasted_iota(jnp.int32, (full - cut, full), 0) < length - cut

    def attend_back(i, pairs):
        im = rows_at(i * full, full)
        for p in pairs:
            col = p * 128
            q = qkv_s[im, col : col + 128] * jnp.asarray(scale, BF)
            k = qkv_s[im, col + width : col + width + 128]
            v = qkv_s[im, col + 2 * width : col + 2 * width + 128]
            do = do_s[im, col : col + 128]
            kt = k.T
            dq, dk, dv = [], None, None
            for h in range(2):
                mine = low_half if h == 0 else ~low_half
                qm = jnp.where(mine, q, jnp.zeros_like(q))
                dom = jnp.where(mine, do, jnp.zeros_like(do))
                s = dot_t(k, qm)
                s = jnp.concatenate([s[:cut], jnp.where(live, s[cut:], -1e30)], 0)
                e = jnp.exp(s - jnp.max(s, 0, keepdims=True))
                probs = e * (1.0 / jnp.sum(e, 0, keepdims=True))
                ds = (probs * (dot_t(v, dom) - inner_s[i, 2 * p + h : 2 * p + h + 1, :])).astype(BF)
                dv_h, dk_h = dot(probs.astype(BF), dom), dot(ds, qm)
                dv = dv_h if dv is None else dv + dv_h
                dk = dk_h if dk is None else dk + dk_h
                dq.append(dot(kt[HEAD_DIM * h : HEAD_DIM * (h + 1), :], ds))
            dq = (jnp.concatenate(dq, 0) * scale).astype(BF).T
            qkv_s[im, col : col + 128] = dq
            qkv_s[im, col + width : col + width + 128] = dk.astype(BF)
            qkv_s[im, col + 2 * width : col + 2 * width + 128] = dv.astype(BF)

    def when(i, index, *steps):
        @pl.when(i == index)
        def _():
            for step in steps:
                step()

    def first_pass(i, _):
        for copy in image_copies(i):
            copy.wait()
        when(i, 2, down.start_group)
        when(i, 4, up.start_group, down1_l.start_back)
        when(i, 5, out.start_group)
        when(i, 7, up1_l.start_back)
        im = rows_at(i * full, full)
        prod = do_s[im, :].astype(F32) * o_s[im, :].astype(F32)
        high = prod.astype(BF)
        inner_s[i] = dot_t(pick, high) + dot_t(pick, (prod - high.astype(F32)).astype(BF))
        attend_back(i, PAIRS_A)
        return 0

    def weight_grad(pairs, g_ref):
        start, stop = pairs[0] * 128, pairs[-1] * 128 + 128
        wide = stop - start
        for n in range(3):
            dp = qkv_s[:, n * width + start : n * width + stop]
            g_ref[:, n * wide : (n + 1) * wide] = dot(a1t[...], dp).astype(BF)
            if n != 1:
                row = 0 if n == 0 else 1
                v_s[0, row : row + 1, start:stop] = dot(jnp.ones((16, rows), BF), dp)[0:1]

    lax.fori_loop(0, images, first_pass, 0)
    big_copy(0).wait()
    a1t[...] = a1_s[...].T
    weight_grad(PAIRS_A, ga_s)
    qa.start_core()

    def second_pass(i, _):
        when(i, 0, down1_l.start_last)
        when(i, 2, down.collect, down_l.start_chips)
        when(i, 3, qa.start_group)
        when(i, 5, up1_l.start_last)
        attend_back(i, PAIRS_B)
        return 0

    lax.fori_loop(0, images, second_pass, 0)
    weight_grad(PAIRS_B, gb_s)
    qb.start_core()
    down_l.start_back()

    for j in range(1, 4):
        big_copy(j).wait()
    v_s[0, 2:4, :] = sum_ref[0:2, :]
    v_s[0, 4:6, :] = jnp.zeros((2, width), F32)
    v_s[0, 6:8, :] = sum_ref[2:4, :]
    one, two = gbu1_ref.shape[1] // ng, gbu2_ref.shape[1] // ng
    for m in range(ng):
        row, col = divmod(m * (one + two), width)
        v_s[0, 8 + row : 9 + row, col : col + one] = gbu1_ref[0:1, m * one : (m + 1) * one]
        v_s[0, 8 + row : 9 + row, col + one : col + one + two] = gbu2_ref[0:1, m * two : (m + 1) * two]

    def input_copy(i):
        return pltpu.make_async_copy(x_s.at[i], ig_out.at[i], ig_sem.at[i])

    def input_pass(b, _):
        first = b * 2
        when(b, 1, qb.start_group)
        when(b, 3, down_l.start_last)
        im = rows_at(first * full, 2 * full)
        da = dot_t(qkv_s[im, :], wq_s[...])
        normed, rstd = normalize(pad_images(x_s.at[pl.ds(first, 2)], xpad))
        grad = dh_s[im, :] + norm_back(da, normed, rstd, vec_ref[4:5, :])
        grad = grad.astype(BF).reshape(2, full, width)
        for i in range(2):
            x_s[first + i] = grad[i, :length, :]
            input_copy(first + i).start()
        v_s[0, 4:5, :] += jnp.sum(da * normed, 0, keepdims=True)
        v_s[0, 5:6, :] += jnp.sum(da, 0, keepdims=True)
        return 0

    lax.fori_loop(0, images // 2, input_pass, 0)
    v_start(0)
    up.collect()
    up_l.start_chips()
    v_add(0)
    v_start(1)
    out.collect()
    out_l.start_chips()
    v_add(1)
    v_start(2)
    up_l.start_back()
    qa.collect()
    qa_l.start_chips()
    out_l.start_back()
    v_add(2)
    vec_out[...] = v_s[3]
    qb.collect()
    qb_l.start_chips()
    qa_l.start_back()
    up_l.start_last()
    out_l.start_last()
    qb_l.start_back()
    qa_l.start_last()
    qb_l.start_last()
    for reducer in early:
        reducer.close()
    for reducer in late:
        reducer.finish()
    for i in range(images):
        input_copy(i).wait()


def run_backward(ng, nr, grads, firsts, qkv, do, attended, a1, wq, tokens, dh, vecs, sums, g_bu):
    images, length, width = tokens.shape
    full = dh.shape[0] // images
    nz = nr // 2
    any_spec = pl.BlockSpec(memory_space=pl.ANY)
    vmem = pl.BlockSpec(memory_space=pltpu.VMEM)
    dma = pltpu.SemaphoreType.DMA
    cols_a, cols_b = 3 * 128 * len(PAIRS_A), 3 * 128 * len(PAIRS_B)
    sizes = [(g.shape[0] // ng // 2, g.shape[1]) for g in grads]
    sizes += [(width // ng // 2, cols_a), (width // ng // 2, cols_b)]
    all_sizes = [(t.shape[0] * t.shape[1], t.shape[2]) for t in firsts] + sizes
    total_shapes = [(2, nz, h // nz, w) for h, w in all_sizes]
    vec_shape = vecs.shape
    scratch = [
        pltpu.VMEM(qkv.shape, BF),
        pltpu.VMEM(do.shape, BF),
        pltpu.VMEM(attended.shape, BF),
        pltpu.VMEM(a1.shape, BF),
        pltpu.VMEM((width, images * full), BF),
        pltpu.VMEM(wq.shape, BF),
        pltpu.VMEM(tokens.shape, BF),
        pltpu.VMEM(dh.shape, F32),
        pltpu.VMEM((2, full, width), F32),
        pltpu.VMEM((images, 16, full), F32),
        pltpu.VMEM((width, cols_a), BF),
        pltpu.VMEM((width, cols_b), BF),
        dma((3, images)),
        dma((4,)),
        dma((images,)),
        pltpu.VMEM(firsts[0].shape, BF),
        pltpu.VMEM(firsts[1].shape, BF),
        dma((2,)),
    ]
    for i, (h, w) in enumerate(sizes):
        scratch += early_scratch(ng, nz, h, w, i < 3)
    for h, w in all_sizes:
        scratch += late_scratch(nz, h, w)
    scratch += vector_scratch(ng, nz, vec_shape)
    res = pl.pallas_call(
        functools.partial(backward, ng, nz, length),
        out_shape=(jax.ShapeDtypeStruct(tokens.shape, BF),)
        + tuple(jax.ShapeDtypeStruct(s, BF) for s in total_shapes)
        + (jax.ShapeDtypeStruct(vec_shape, F32),),
        in_specs=[any_spec] * 12 + [vmem] * 4,
        out_specs=(any_spec,) * 8 + (vmem,),
        scratch_shapes=scratch,
        compiler_params=params(62, collective_id=2, has_side_effects=True),
    )(*grads, *firsts, qkv, do, attended, a1, wq, tokens, dh, vecs, sums, *g_bu)
    totals = [t.reshape(2 * h, w).astype(F32) for t, (h, w) in zip(res[1:8], all_sizes)]
    wide_a, wide_b = cols_a // 3, cols_b // 3
    down1, up1, down, up, out, qa, qb = totals
    down = jnp.concatenate([down1, down], 0)
    one, two = up1.shape[1] // ng, up.shape[1] // ng
    parts = []
    for m in range(ng):
        parts += [up1[:, m * one : (m + 1) * one], up[:, m * two : (m + 1) * two]]
    up = jnp.concatenate(parts, 1)
    parts = []
    for n in range(3):
        parts += [qa[:, n * wide_a : (n + 1) * wide_a], qb[:, n * wide_b : (n + 1) * wide_b]]
    return res[0], [down, up, out, jnp.concatenate(parts, 1)], res[8]


def adamw_update(weight, first_moment, second, gradient, step_rate, decay_coef):
    first_new = beta_one * first_moment + (1.0 - beta_one) * gradient
    second_new = beta_two * second + (1.0 - beta_two) * gradient * gradient
    fix_one = 1.0 - beta_one**STEP
    fix_two = 1.0 - beta_two**STEP
    weight_new = weight - step_rate * (
        first_new / fix_one / (jnp.sqrt(second_new / fix_two) + adam_eps) + decay_coef * weight
    )
    return (first_new, second_new, weight_new)


def per_device(
    ng, nr, tokens, cotangent, w_qkv, m_qkv, v_qkv, w_out, m_out, v_out, w_up, m_up, v_up,
    w_down, m_down, v_down, vectors, m_vectors, v_vectors,
):
    length = tokens.shape[1]
    full = -(-length // 16) * 16
    (wq, wo, u2, d2, vecs, a1, qkv, attended, a2, dm, h, acc, da, gd1, gu1, gbu1) = run_forward(
        ng, nr, full, tokens, cotangent, w_qkv, w_out, w_up, w_down, vectors
    )
    output, dh, do, gd2, gu2, g_out, gbu2, sums, td1, tu1 = run_turn(
        ng, nr, cotangent, a2, dm, h, acc, da, attended, wo, u2, d2, gd1, gu1, vecs
    )
    input_grad, totals, vec_total = run_backward(
        ng, nr, (gd2, gu2, g_out), (td1, tu1), qkv, do, attended, a1, wq, tokens, dh, vecs, sums, (gbu1, gbu2)
    )
    own = vectors.shape[1]
    vec_total = lax.dynamic_slice_in_dim(vec_total, lax.axis_index("group") * own, own, 1)
    states = (
        (w_qkv, m_qkv, v_qkv, totals[3], 0.1, 0.05),
        (w_out, m_out, v_out, totals[2], 0.1, 0.05),
        (w_up, m_up, v_up, totals[1], 0.1, 0.05),
        (w_down, m_down, v_down, totals[0], 0.1, 0.05),
        (vectors, m_vectors, v_vectors, vec_total, 0.8, 0.0),
    )
    outcome = [output, input_grad]
    for weight, first_moment, second, gradient, rate, decay in states:
        first_new, second_new, weight_new = adamw_update(weight, first_moment, second, gradient, rate, decay)
        outcome.extend([gradient, first_new, second_new, weight_new])
    return tuple(outcome)


def solution(mesh):
    ng, nr = mesh.shape["group"], mesh.shape["replica"]
    tokens_spec = P(("replica", "group"), None, None)
    rows_spec, cols_spec = P("group", None), P(None, "group")
    in_specs = (tokens_spec,) * 2 + (rows_spec,) * 12 + (cols_spec,) * 3
    out_specs = (tokens_spec,) * 2 + (rows_spec,) * 16 + (cols_spec,) * 4
    return jax.shard_map(
        functools.partial(per_device, ng, nr), mesh=mesh, in_specs=in_specs, out_specs=out_specs, check_vma=False
    )
```

```python
import functools

import jax
import jax.numpy as jnp
from jax import lax
from jax.experimental import pallas as pl
from jax.experimental.pallas import tpu as pltpu
from jax.sharding import PartitionSpec as P

F32 = jnp.float32
BF = jnp.bfloat16
HEADS = 12
HEAD_DIM = 64
STEP = 10
MIB = 2**20
MESH = pl.DeviceIdType.MESH

norm_eps = 1e-06
beta_one = 0.9
beta_two = 0.999
adam_eps = 1e-08


def dot(a, b):
    return jnp.dot(a, b, preferred_element_type=F32)


def dot_t(a, b):
    return lax.dot_general(a, b, (((1,), (1,)), ((), ())), preferred_element_type=F32)


def flip(index, mask):
    out, bit = index, 1
    while bit <= mask:
        if mask & bit:
            out = out + bit * (1 - 2 * lax.rem(lax.div(index, bit), 2))
        bit *= 2
    return out


def rows_at(start, size):
    return pl.ds(pl.multiple_of(start, 16), size)


def normalize(hidden):
    centered = hidden - jnp.mean(hidden, -1, keepdims=True)
    rstd = lax.rsqrt(jnp.mean(centered * centered, -1, keepdims=True) + norm_eps)
    return centered * rstd, rstd


def norm_back(grad, normed, rstd, gain):
    e = grad * gain
    mean_e = jnp.mean(e, -1, keepdims=True)
    mean_en = jnp.mean(e * normed, -1, keepdims=True)
    return (e - mean_e - normed * mean_en) * rstd


def gelu_parts(u):
    d = 1.0 + (0.3275911 * 0.7071067811865476) * jnp.abs(u)
    t = pl.reciprocal(d, approx=True)
    t = t * (2.0 - d * t)
    e = jnp.exp2(u * u * (-0.5 * 1.4426950408889634))
    poly = ((0.5307027145 * t - 0.7265760135) * t + 0.7107068705) * t - 0.142248368
    q = (poly * t + 0.127414796) * t * e
    phi = jnp.where(u > 0, 1.0 - q, q)
    return u * phi, phi + (u * 0.3989422804014327) * e


def params(mib=58, **kw):
    return pltpu.CompilerParams(vmem_limit_bytes=mib * MIB, **kw)


class Places:
    def __init__(self, ng, nz):
        self.ng, self.nz = ng, nz
        self.r, self.g = lax.axis_index("replica"), lax.axis_index("group")
        self.c, self.z = lax.rem(self.r, 2), lax.div(self.r, 2)
        self.sib = {"replica": flip(self.r, 1), "group": self.g}

    def group(self, k):
        return {"replica": self.r, "group": flip(self.g, k)}

    def chip(self, j):
        return {"replica": flip(self.r, 2 * j), "group": self.g}

    def greet(self, group, chips):
        barrier = pltpu.get_barrier_semaphore()
        targets = [self.sib]
        if group:
            targets += [self.group(k) for k in range(1, self.ng)]
        if chips:
            targets += [self.chip(j) for j in range(1, self.nz)]
        for target in targets:
            pl.semaphore_signal(barrier, inc=1, device_id=target, device_id_type=MESH)
        pl.semaphore_wait(barrier, len(targets))


def remote(src, dst, send, recv, target):
    return pltpu.make_async_remote_copy(src, dst, send, recv, device_id=target, device_id_type=MESH)


class Gather:
    def __init__(self, at, buf, sems):
        self.at, self.buf = at, buf
        self.x_send, self.x_recv, self.f_send, self.f_recv = sems
        self.half = buf.shape[0] // at.ng // 2
        self.relay = at.ng == 4

    def rows(self, k, c, lower=None):
        start, size = flip(self.at.g, k) * 2 * self.half + c * self.half, self.half
        if lower is not None:
            size = self.half // 2
            start = start + (0 if lower else size)
        return self.buf.at[rows_at(start, size), :]

    def direct(self, k):
        part = self.rows(0, self.at.c)
        return remote(part, part, self.x_send.at[k - 1], self.x_recv.at[k - 1], self.at.group(k))

    def relayed(self, k):
        part = self.rows(k, self.at.c, k == 1)
        return remote(part, part, self.x_send.at[1 + k], self.x_recv.at[1 + k], self.at.group(3 - k))

    def relayed_in(self, k):
        part = self.rows(3, self.at.c, k == 1)
        return remote(part, part, self.x_send.at[1 + k], self.x_recv.at[1 + k], self.at.group(3 - k))

    def across(self, k):
        part = self.rows(k, self.at.c)
        return remote(part, part, self.f_send.at[k - 1], self.f_recv.at[k - 1], self.at.sib)

    def across_in(self, k):
        part = self.rows(k, 1 - self.at.c)
        return remote(part, part, self.f_send.at[k - 1], self.f_recv.at[k - 1], self.at.sib)

    def near(self):
        return (1, 2) if self.relay else range(1, self.at.ng)

    def start(self):
        for k in self.near():
            self.direct(k).start()

    def pass_on(self):
        for k in self.near():
            self.direct(k).wait_recv()
            if self.relay:
                self.relayed(k).start()
            self.across(k).start()

    def settle(self):
        if self.relay:
            for k in (1, 2):
                self.relayed_in(k).wait_recv()
            self.across(3).start()

    def finish(self):
        for k in range(1, self.at.ng):
            self.across_in(k).wait_recv()

    def close(self):
        for k in self.near():
            self.direct(k).wait_send()
            if self.relay:
                self.relayed(k).wait_send()
        for k in range(1, self.at.ng):
            self.across(k).wait_send()


def gather_sems(ng):
    dma = pltpu.SemaphoreType.DMA
    n = 4 if ng == 4 else ng - 1
    return [dma((n,)), dma((n,)), dma((ng - 1,)), dma((ng - 1,))]


def strips(ng, ff):
    share = ff // ng
    one = -(-share // 256) * 128
    return share, one, share - one


def tile_of(size):
    return 768 if size % 768 == 0 else 512


def mlp_tile(t, ft, blocks, a2, a2t, dm, wu, wd, bias, da_acc, act_s, du_s, gd_slot, gu_slot, gbu, before=(), ready=lambda i: None):
    units = slice(t * ft, (t + 1) * ft)
    rows, width = da_acc.shape[0] // blocks, da_acc.shape[1]

    def body(i, _):
        im = rows_at(i * rows, rows)
        u = dot(a2[im, :], wu[:, units]) + bias[:, units]
        da = dot_t(dm[im, :], wd[units, :])
        act, slope = gelu_parts(u)
        act = act.astype(BF)
        du = (da * slope).astype(BF)
        act_s[im, 0:ft] = act
        du_s[im, 0:ft] = du
        ready(i)
        da_acc[im, :] += dot_t(du, wu[:, units])
        return 0

    lax.fori_loop(0, blocks, body, 0)
    for step in before:
        step()
    gd_slot[...] = dot(act_s[:, 0:ft].T, dm[...]).astype(BF)
    both = dot(a2t[...], du_s[:, 0:ft])
    gu_slot[...] = both[0:width].astype(BF)
    gbu[:, 0:ft] = both[width : width + 1]


def forward(ng, nz, length, *refs):
    at = Places(ng, nz)
    (x_hbm, cot_hbm, wq_hbm, wo_hbm, wu_hbm, wd_hbm, vec_hbm,
     wq_out, wo_out, u2_out, d2_out, vec_out, a1_out, qkv_out, o_out, a2_out, dm_out, h_out, act_out, d1_out, da_out, gd_out, gu_out, x_out, gbu_out,
     xs, cs, acc, da, h, bq, bo, bu1, bd1, bu2, bd2, vec_s, vall, a1o, qkv, dm, a2t, xf, gbu,
     w_sem, v_sem, in_sem, v_send, v_recv, out_sem, g_sem, a_sem) = refs[:52]
    width = h.shape[1]
    blocks_q = [bq.at[:, n * width : (n + 1) * width] for n in range(bq.shape[1] // width)]
    gt, ft = ng * 128, 512
    tiles, per_gather, per = bu1.shape[1] // gt, gt // ft, ft // 128
    buffers = blocks_q + [bo, bu2, bd2]
    for t in range(tiles):
        buffers += [bu1.at[:, t * gt : (t + 1) * gt], bd1.at[t * gt : (t + 1) * gt, :]]
    gathers = [Gather(at, buf, refs[52 + 4 * i : 56 + 4 * i]) for i, buf in enumerate(buffers)]
    nq = len(blocks_q)
    g_q, (g_o, g_u2, g_d2) = gathers[:nq], gathers[nq : nq + 3]
    g_t = [gathers[nq + 3 + 2 * t : nq + 5 + 2 * t] for t in range(tiles)]
    images = xs.shape[0] // length
    full = h.shape[0] // images
    shard = wq_hbm.shape[0]
    ff = wu_hbm.shape[1]
    share, one, two = strips(ng, ff)
    nq, nu = wq_hbm.shape[1] // width, ff // width

    flat, flat_h = acc, h
    loads = []
    for n in range(nq):
        loads.append((wq_hbm.at[:, n * width : (n + 1) * width], flat.at[n * shard : (n + 1) * shard]))
    loads.append((wo_hbm, flat.at[nq * shard : (nq + 1) * shard]))
    for n in range(nu):
        loads.append((wu_hbm.at[:, n * width : (n + 1) * width], flat.at[(nq + 1 + n) * shard : (nq + 2 + n) * shard]))
    loads.append((wd_hbm, flat_h.at[0:share]))
    loads = [pltpu.make_async_copy(src, dst, w_sem.at[i]) for i, (src, dst) in enumerate(loads)]
    vec_load = pltpu.make_async_copy(vec_hbm, vec_s, v_sem)
    x_load = pltpu.make_async_copy(x_hbm, xs, in_sem.at[0])
    cot_load = pltpu.make_async_copy(cot_hbm, cs, in_sem.at[1])
    vec_load.start()
    for n in range(nq):
        loads[n].start()
    x_load.start()
    for load in loads[nq:]:
        load.start()
    cot_load.start()
    at.greet(True, False)

    vec_load.wait()
    vall[at.g] = vec_s[...].astype(BF).astype(F32)
    v_copies = [remote(vall.at[at.g], vall.at[at.g], v_send.at[k - 1], v_recv.at[k - 1], at.group(k)) for k in range(1, ng)]
    for copy in v_copies:
        copy.start()
    for n in range(nq):
        loads[n].wait()
        blocks_q[n][rows_at(at.g * shard, shard), :] = flat[n * shard : (n + 1) * shard, :].astype(BF)
        g_q[n].start()
    loads[nq].wait()
    bo[rows_at(at.g * shard, shard), :] = flat[nq * shard : (nq + 1) * shard, :].astype(BF)
    for n in range(nu):
        loads[nq + 1 + n].wait()
    for m in range(ng):
        block, col = divmod(m * share, width)
        src = slice((nq + 1 + block) * shard, (nq + 2 + block) * shard)
        for t in range(tiles):
            lanes = slice(t * gt + m * 128, t * gt + (m + 1) * 128)
            bu1[rows_at(at.g * shard, shard), lanes] = flat[src, col + t * 128 : col + (t + 1) * 128].astype(BF)
        bu2[rows_at(at.g * shard, shard), m * two : (m + 1) * two] = flat[src, col + one : col + share].astype(BF)
    loads[nq + 1 + nu].wait()
    for t in range(tiles):
        bd1[rows_at(t * gt + at.g * 128, 128), :] = flat_h[t * 128 : (t + 1) * 128, :].astype(BF)
    bd2[rows_at(at.g * two, two), :] = flat_h[one:share, :].astype(BF)

    for copy in v_copies:
        copy.wait()
    w = vall.shape[2]
    vecs = jnp.zeros((vall.shape[1], width), F32)
    for j in range(ng):
        row = lax.broadcasted_iota(jnp.int32, (w, width), 0)
        col = lax.broadcasted_iota(jnp.int32, (w, width), 1)
        vecs = vecs + dot(vall[j].astype(BF), jnp.where(col == row + j * w, 1.0, 0.0).astype(BF))
    vec_out[...] = vecs

    x_load.wait()
    lanes = width // 128

    def spread(ref):
        for j in range(lanes):
            xf[j, 0 : length * images, :] = ref[:, j * 128 : (j + 1) * 128].astype(F32)

    def image_of(i):
        return jnp.concatenate([xf[j, pl.ds(i, full, stride=images), :] for j in range(lanes)], 1)

    xf[:, length * images :, :] = jnp.zeros((lanes, (full - length) * images, 128), F32)
    spread(xs)

    def norm_image(i, _):
        im = rows_at(i * full, full)
        x = image_of(i)
        h[im, :] = x
        qkv[im, 0:width] = x.astype(BF)
        normed, _r = normalize(x)
        a1o[im, :] = (normed * vec_out[4:5, :] + vec_out[5:6, :]).astype(BF)
        return 0

    lax.fori_loop(0, images, norm_image, 0)
    a1_copy = pltpu.make_async_copy(a1o, a1_out, out_sem.at[0])
    a1_copy.start()
    x_copy = pltpu.make_async_copy(qkv.at[:, 0:width], x_out, out_sem.at[12])
    x_copy.start()
    g_q[0].pass_on()
    cot_load.wait()
    spread(cs)

    def cot_image(i, _):
        dm[rows_at(i * full, full), :] = image_of(i).astype(BF)
        return 0

    lax.fori_loop(0, images, cot_image, 0)
    dm_copy = pltpu.make_async_copy(dm, dm_out, out_sem.at[1])
    dm_copy.start()
    for gather in g_q[1:]:
        gather.pass_on()
    g_q[0].settle()
    g_o.start()
    x_copy.wait()

    def each(group, name):
        for gather in group:
            if isinstance(gather, Gather):
                getattr(gather, name)()
            else:
                each(gather, name)

    zero = jnp.zeros((1, width), F32)
    biases = [vec_out[0:1, :], zero, vec_out[1:2, :]]
    block = images * full // 2

    for n in range(3):
        cols = slice(n * width, (n + 1) * width)
        g_q[n].finish()

        def project(i, _, cols=cols, bias=biases[n]):
            im = rows_at(i * block, block)
            qkv[im, cols] = (dot(a1o[im, :], bq[:, cols]) + bias).astype(BF)
            return 0

        lax.fori_loop(0, 2, project, 0)
        if n == 0:
            g_q[1].settle()
            g_q[2].settle()
            each(g_t[0], "start")
    wq_copy = pltpu.make_async_copy(bq, wq_out, out_sem.at[2])
    wq_copy.start()
    qkv_copy = pltpu.make_async_copy(qkv, qkv_out, out_sem.at[3])
    qkv_copy.start()
    a1_copy.wait()

    low_half = lax.broadcasted_iota(jnp.int32, (full, 128), 1) < HEAD_DIM
    key_bias = jnp.where(lax.broadcasted_iota(jnp.int32, (1, full), 1) < length, 0.0, -1e30).astype(F32)
    ones = jnp.ones((full, 128), BF)

    def when(i, index, *steps):
        @pl.when(i == index)
        def _():
            for step in steps:
                step()

    def attend(i, _):
        when(i, 0, g_o.pass_on)
        when(i, 1, lambda: each(g_t[1], "start"))
        when(i, 2, g_o.settle, lambda: each(g_t[0], "pass_on"))
        when(i, 5, lambda: each(g_t[0], "settle"), lambda: each(g_t[1], "pass_on"), lambda: each(g_t[2:], "start"))
        im = rows_at(i * full, full)
        for p in range(HEADS // 2):
            col = p * 128
            q = qkv[im, col : col + 128] * jnp.asarray(HEAD_DIM**-0.5, BF)
            k = qkv[im, col + width : col + width + 128]
            v = jnp.concatenate([qkv[im, col + 2 * width : col + 2 * width + 128], ones], axis=1)
            heads = []
            for hd in range(2):
                mine = low_half if hd == 0 else ~low_half
                s = dot_t(jnp.where(mine, q, jnp.zeros_like(q)), k) + key_bias
                e = jnp.exp(s - jnp.max(s, -1, keepdims=True)).astype(BF)
                both = dot(e, v)
                heads.append(both[:, :128] / both[:, 128:])
            a1o[im, col : col + 128] = jnp.where(low_half, heads[0], heads[1]).astype(BF)
        return 0

    lax.fori_loop(0, images, attend, 0)
    o_copy = pltpu.make_async_copy(a1o, o_out, out_sem.at[4])
    o_copy.start()
    g_o.finish()
    wo_copy = pltpu.make_async_copy(bo, wo_out, out_sem.at[5])
    wo_copy.start()
    qkv_copy.wait()

    def middle(i, _):
        im = rows_at(i * block, block)
        hidden = h[im, :] + dot(a1o[im, :], bo[...]) + vec_out[2:3, :]
        h[im, :] = hidden
        normed, _r = normalize(hidden)
        qkv[im, 0:width] = (normed * vec_out[6:7, :] + vec_out[7:8, :]).astype(BF)
        da[im, :] = jnp.zeros((block, width), F32)
        return 0

    lax.fori_loop(0, 2, middle, 0)
    a2_copy = pltpu.make_async_copy(qkv.at[:, 0:width], a2_out, out_sem.at[6])
    h_copy = pltpu.make_async_copy(h, h_out, out_sem.at[7])
    a2_copy.start()
    h_copy.start()
    a2t[0:width, :] = qkv[:, 0:width].T
    a2t[width:, :] = jnp.ones_like(a2t[width:, :])
    each(g_t[1], "settle")
    each(g_t[2:], "pass_on")
    each([g_u2, g_d2], "start")

    bias = jnp.concatenate([unit_bias(vec_out, ng, share, t * 128, 128) for t in range(tiles)], 1)
    slots = [(ref, n * width) for ref in (xs, cs) for n in range(2)]
    d1_copy = pltpu.make_async_copy(bd1, d1_out, out_sem.at[8])
    act_s = qkv.at[:, width : width + ft]
    act_copies = [
        pltpu.make_async_copy(act_s, act_out.at[:, ct * ft : (ct + 1) * ft], a_sem.at[ct]) for ct in range(tiles * per_gather)
    ]
    da_copy = pltpu.make_async_copy(da, da_out, out_sem.at[9])
    pending = []
    for ct in range(tiles * per_gather):
        t, sub = divmod(ct, per_gather)
        if sub == 0:
            each(g_t[t], "finish")
        if ct >= 2:
            for copy in pending[2 * per * (ct - 2) : 2 * per * (ct - 1)]:
                copy.wait()
        gd_slot, gu_slot = [ref.at[start : start + width] for ref, start in slots[2 * (ct % 2) : 2 * (ct % 2) + 2]]
        gd_slot, gu_slot = gd_slot.at[0:ft], gu_slot.at[:, 0:ft]
        hooks = [act_copies[ct].start]
        if ct:
            act_copies[ct - 1].wait()
        if ct == 0:
            hooks.append(lambda: each(g_t[2:], "settle"))
        if ct == tiles * per_gather - 2:
            hooks.append(lambda: each([g_u2, g_d2], "pass_on"))
        if ct == tiles * per_gather - 1:
            hooks += [d1_copy.start, da_copy.start, lambda: each([g_u2, g_d2], "settle")]
        mlp_tile(
            ct, ft, 2, qkv.at[:, 0:width], a2t, dm, bu1, bd1, bias, da, act_s, qkv.at[:, 2 * width : 2 * width + ft], gd_slot, gu_slot, gbu,
            hooks,
        )
        for i in range(per):
            start = (sub * per + i) * one + t * 128
            units, part = slice(start, start + 128), slice(i * 128, (i + 1) * 128)
            pending.append(pltpu.make_async_copy(gd_slot.at[part, :], gd_out.at[units, :], g_sem.at[0, ct, i]))
            pending.append(pltpu.make_async_copy(gu_slot.at[:, part], gu_out.at[:, units], g_sem.at[1, ct, i]))
            gbu_out[:, units] = gbu[:, part]
        for copy in pending[-2 * per :]:
            copy.start()
    g_u2.finish()
    g_d2.finish()
    u2_copy = pltpu.make_async_copy(bu2, u2_out, out_sem.at[10])
    d2_copy = pltpu.make_async_copy(bd2, d2_out, out_sem.at[11])
    u2_copy.start()
    d2_copy.start()
    for gather in gathers:
        gather.close()
    for copy in pending[-4 * per :] + [dm_copy, wq_copy, o_copy, wo_copy, a2_copy, h_copy, d1_copy, da_copy, act_copies[-1], u2_copy, d2_copy]:
        copy.wait()


def unit_bias(vec_ref, ng, share, start, size):
    width = vec_ref.shape[1]
    parts = []
    for m in range(ng):
        row, col = divmod(m * share + start, width)
        parts.append(vec_ref[8 + row : 9 + row, col : col + size])
    return jnp.concatenate(parts, 1)


def run_forward(ng, nr, full, tokens, cotangent, w_qkv, w_out, w_up, w_down, vectors):
    images, length, width = tokens.shape
    ff = w_up.shape[1]
    share, one, two = strips(ng, ff)
    f1, f2 = ng * one, ng * two
    any_spec = pl.BlockSpec(memory_space=pl.ANY)
    vmem = pl.BlockSpec(memory_space=pltpu.VMEM)
    dma = pltpu.SemaphoreType.DMA
    rows_like = (images * full, width)
    flat = (length * images, width)
    ft = 512

    def bf(*shape):
        return jax.ShapeDtypeStruct(shape, BF)

    def f32(*shape):
        return jax.ShapeDtypeStruct(shape, F32)

    n_loads = w_qkv.shape[1] // width + ff // width + 2
    return pl.pallas_call(
        functools.partial(forward, ng, nr // 2, length),
        out_shape=(
            bf(width, 3 * width), bf(width, width), bf(width, f2), bf(f2, width), f32(vectors.shape[0], width),
            bf(*rows_like), bf(images * full, 3 * width), bf(*rows_like), bf(*rows_like), bf(*rows_like),
            f32(*rows_like), bf(images * full, f1), bf(f1, width), f32(*rows_like), bf(f1, width), bf(width, f1), bf(*rows_like), f32(1, f1),
        ),
        in_specs=[any_spec] * 7,
        out_specs=(any_spec,) * 4 + (vmem,) + (any_spec,) * 12 + (vmem,),
        scratch_shapes=[
            pltpu.VMEM(flat, BF),
            pltpu.VMEM(flat, BF),
            pltpu.VMEM(rows_like, F32),
            pltpu.VMEM(rows_like, F32),
            pltpu.VMEM(rows_like, F32),
            pltpu.VMEM((width, 3 * width), BF),
            pltpu.VMEM((width, width), BF),
            pltpu.VMEM((width, f1), BF),
            pltpu.VMEM((f1, width), BF),
            pltpu.VMEM((width, f2), BF),
            pltpu.VMEM((f2, width), BF),
            pltpu.VMEM(vectors.shape, F32),
            pltpu.VMEM((ng,) + vectors.shape, F32),
            pltpu.VMEM(rows_like, BF),
            pltpu.VMEM((images * full, 3 * width), BF),
            pltpu.VMEM(rows_like, BF),
            pltpu.VMEM((width + 16, images * full), BF),
            pltpu.VMEM((width // 128, images * full, 128), F32),
            pltpu.VMEM((1, ft), F32),
            dma((n_loads,)),
            dma,
            dma((2,)),
            dma((ng - 1,)),
            dma((ng - 1,)),
            dma((13,)),
            dma((2, f1 // ft, ft // 128)),
            dma((f1 // ft,)),
        ]
        + gather_sems(ng) * (3 + w_qkv.shape[1] // width + 2 * (f1 // (ng * 128))),
        compiler_params=params(64, collective_id=0, has_side_effects=True),
    )(
        tokens.transpose(1, 0, 2).reshape(flat), cotangent.transpose(1, 0, 2).reshape(flat),
        w_qkv, w_out, w_up, w_down, vectors,
    )


class Early:
    def __init__(self, at, src, load, refs):
        self.at, self.src, self.mine = at, src, None
        if load:
            self.mine, refs = refs[0], refs[1:]
        self.rc, self.rx, self.tz, self.m_sem, self.c_send, self.c_recv, self.x_send, self.x_recv = refs[:8]
        self.rest = refs[8:]
        self.half = self.rc.shape[1]
        self.two = at.ng == 4

    def load_copy(self, m):
        start = m * 2 * self.half + self.at.c * self.half
        return pltpu.make_async_copy(self.src.at[rows_at(start, self.half), :], self.mine.at[m], self.m_sem.at[m])

    def core_copy(self, m):
        start = m * 2 * self.half + (1 - self.at.c) * self.half
        return remote(self.src.at[rows_at(start, self.half), :], self.rc.at[m], self.c_send.at[m], self.c_recv.at[m], self.at.sib)

    def group_copy(self, k):
        return remote(self.rc.at[flip(self.at.g, k)], self.rx.at[k - 1], self.x_send.at[k - 1], self.x_recv.at[k - 1], self.at.group(k))

    def rows(self, k):
        return slice(0, self.half // 2) if k == 1 else slice(self.half // 2, self.half)

    def first_copy(self, k, own):
        part = self.rc.at[flip(self.at.g, k if own else 3), self.rows(k), :]
        slot = 2 * (k - 1) + (0 if own else 1)
        return remote(part, self.rx.at[slot], self.x_send.at[slot], self.x_recv.at[slot], self.at.group(k))

    def second_copy(self, k):
        part = self.rc.at[flip(self.at.g, k), self.rows(3 - k), :]
        return remote(part, self.rx.at[3 + k], self.x_send.at[3 + k], self.x_recv.at[3 + k], self.at.group(k))

    def start_core(self):
        for m in range(self.at.ng):
            self.core_copy(m).start()
        if self.mine is not None:
            for m in range(self.at.ng):
                self.load_copy(m).start()

    def start_group(self):
        at, h = self.at, self.half
        for m in range(at.ng):
            self.core_copy(m).wait_recv()
            if self.mine is not None:
                self.load_copy(m).wait()
        order = (3, 1, 2, 0) if self.two else list(range(1, at.ng)) + [0]
        for k in order:
            m = flip(at.g, k)
            mine = self.src[rows_at(m * 2 * h + at.c * h, h), :] if self.mine is None else self.mine[m]
            self.rc[m] = (mine.astype(F32) + self.rc[m].astype(F32)).astype(BF)
            if self.two and k == 3:
                self.first_copy(1, False).start()
                self.first_copy(2, False).start()
            elif self.two and k:
                self.first_copy(k, True).start()
            elif k:
                self.group_copy(k).start()

    def turn_group(self):
        if not self.two:
            return
        for k in (1, 2):
            self.first_copy(k, False).wait_recv()
            m, sl = flip(self.at.g, 3 - k), self.rows(k)
            self.rc[m, sl, :] = (self.rc[m, sl, :].astype(F32) + self.rx[2 * (k - 1) + 1].astype(F32)).astype(BF)
            self.second_copy(3 - k).start()

    def collect(self):
        at = self.at
        if self.two:
            parts = []
            for k in (1, 2):
                self.first_copy(k, True).wait_recv()
                self.second_copy(3 - k).wait_recv()
                part = self.rc[at.g, self.rows(k), :].astype(F32) + self.rx[2 * (k - 1)].astype(F32)
                parts.append(part + self.rx[3 + 3 - k].astype(F32))
            total = jnp.concatenate(parts, 0)
        else:
            for k in range(1, at.ng):
                self.group_copy(k).wait_recv()
            total = self.rc[at.g].astype(F32)
            for k in range(at.ng - 1):
                total = total + self.rx[k].astype(F32)
        p = self.half // at.nz
        for j in range(at.nz):
            self.tz[j] = total[j * p : (j + 1) * p].astype(BF)

    def close(self):
        if self.two:
            for k in (1, 2):
                self.first_copy(k, True).wait_send()
                self.first_copy(k, False).wait_send()
                self.second_copy(k).wait_send()
        else:
            for k in range(1, self.at.ng):
                self.group_copy(k).wait_send()
        for m in range(self.at.ng):
            self.core_copy(m).wait_send()


class Late:
    def __init__(self, at, tz, refs, out):
        self.at, self.tz, self.out = at, tz, out
        self.steps = at.nz.bit_length() - 1
        (self.rz, self.y, self.z_send, self.z_recv, self.a_send, self.a_recv, self.f_send, self.f_recv, self.o_sem) = refs[:9]
        self.rest = refs[9:]

    def bit(self, k):
        return lax.rem(lax.div(self.at.z, 2**k), 2)

    def base(self, k, size):
        start = 0
        for i in range(k):
            start = start + self.bit(i) * (self.at.nz // 2 ** (i + 1))
        return start + self.bit(k) * size, start + (1 - self.bit(k)) * size

    def half_copy(self, k):
        size = self.at.nz // 2 ** (k + 1)
        landing = self.rz.at[pl.ds(size - 1, size)]
        return remote(self.tz.at[pl.ds(self.base(k, size)[1], size)], landing, self.z_send.at[k], self.z_recv.at[k], self.at.chip(2**k))

    def place(self, mask):
        start = 0
        for i in range(self.steps):
            b = 1 - self.bit(i) if mask & 2**i else self.bit(i)
            start = start + b * (self.at.nz // 2 ** (i + 1))
        return start

    def back_copy(self, k, mask):
        place = self.out.at[self.at.c, self.place(mask)]
        slot = (mask ^ 2**k) - 1
        return remote(self.y if mask == 0 else place, place, self.a_send.at[slot], self.a_recv.at[slot], self.at.chip(2**k))

    def back_in(self, mask):
        place = self.out.at[self.at.c, self.place(mask)]
        return remote(self.y, place, self.a_send.at[mask - 1], self.a_recv.at[mask - 1], self.at.chip(mask))

    def last_copy(self, mask, mine=True):
        place = self.out.at[self.at.c if mine else 1 - self.at.c, self.place(mask)]
        return remote(self.y if mask == 0 else place, place, self.f_send.at[mask], self.f_recv.at[mask], self.at.sib)

    def keep_copy(self):
        return pltpu.make_async_copy(self.y, self.out.at[self.at.c, self.place(0)], self.o_sem)

    def start_halves(self):
        self.half_copy(0).start()

    def add_half(self, k):
        size = self.at.nz // 2 ** (k + 1)
        self.half_copy(k).wait_recv()
        kept = self.base(k, size)[0]
        for i in range(size):
            total = (self.tz[kept + i].astype(F32) + self.rz[size - 1 + i].astype(F32)).astype(BF)
            if size == 1:
                self.y[...] = total
            else:
                self.tz[kept + i] = total
        if size > 1:
            self.half_copy(k + 1).start()
            return
        for j in reversed(range(self.steps)):
            self.back_copy(j, 0).start()
        self.last_copy(0).start()
        self.keep_copy().start()

    def spread(self, k):
        for mask in range(0, self.at.nz, 2 ** (k + 1)):
            got = mask ^ 2**k
            self.back_in(got).wait_recv()
            for j in reversed(range(k)):
                self.back_copy(j, got).start()
            self.last_copy(got).start()

    def stages(self):
        out = [self.start_halves]
        out += [functools.partial(self.add_half, k) for k in range(self.steps)]
        return out + [functools.partial(self.spread, k) for k in reversed(range(self.steps))]

    def finish(self):
        at = self.at
        for mask in range(at.nz):
            self.last_copy(mask, mine=False).wait_recv()
            self.last_copy(mask).wait_send()
        for k in range(self.steps):
            self.half_copy(k).wait_send()
            for mask in range(0, at.nz, 2 ** (k + 1)):
                self.back_copy(k, mask).wait_send()
        self.keep_copy().wait()


class LateDirect:
    def __init__(self, at, tz, refs, out):
        self.at, self.tz, self.out = at, tz, out
        (self.rz, self.y, self.z_send, self.z_recv, self.a_send, self.a_recv, self.f_send, self.f_recv, self.o_sem) = refs[:9]
        self.rest = refs[9:]

    def chip_copy(self, j):
        return remote(self.tz.at[flip(self.at.z, j)], self.rz.at[j - 1], self.z_send.at[j - 1], self.z_recv.at[j - 1], self.at.chip(j))

    def back_copy(self, j, mine=True):
        place = self.out.at[self.at.c, self.at.z if mine else flip(self.at.z, j)]
        return remote(self.y, place, self.a_send.at[j - 1], self.a_recv.at[j - 1], self.at.chip(j))

    def last_copy(self, j, mine=True):
        place = self.out.at[self.at.c if mine else 1 - self.at.c, flip(self.at.z, j)]
        return remote(self.y if j == 0 else place, place, self.f_send.at[j], self.f_recv.at[j], self.at.sib)

    def keep_copy(self):
        return pltpu.make_async_copy(self.y, self.out.at[self.at.c, self.at.z], self.o_sem)

    def start_halves(self):
        for j in reversed(range(1, self.at.nz)):
            self.chip_copy(j).start()

    def start_back(self):
        at = self.at
        for j in range(1, at.nz):
            self.chip_copy(j).wait_recv()
        total = self.tz[at.z].astype(F32)
        for j in range(at.nz - 1):
            total = total + self.rz[j].astype(F32)
        self.y[...] = total.astype(BF)
        for j in reversed(range(1, at.nz)):
            self.back_copy(j).start()
        self.last_copy(0).start()
        self.keep_copy().start()

    def start_last(self):
        for j in range(1, self.at.nz):
            self.back_copy(j, mine=False).wait_recv()
            self.last_copy(j).start()

    def stages(self):
        return [self.start_halves, self.start_back, self.start_last]

    def finish(self):
        at = self.at
        for j in range(at.nz):
            self.last_copy(j, mine=False).wait_recv()
            self.last_copy(j).wait_send()
        for j in range(1, at.nz):
            self.back_copy(j).wait_send()
            self.chip_copy(j).wait_send()
        self.keep_copy().wait()


def early_scratch(ng, nz, half, cols, load):
    dma = pltpu.SemaphoreType.DMA
    landing, n = ((6, half // 2, cols), 6) if ng == 4 else ((ng - 1, half, cols), ng - 1)
    shapes = [pltpu.VMEM((ng, half, cols), BF)] if load else []
    shapes += [pltpu.VMEM((ng, half, cols), BF), pltpu.VMEM(landing, BF), pltpu.VMEM((nz, half // nz, cols), BF)]
    return shapes + [dma((m,)) for m in (ng, ng, ng, n, n)]


def late_scratch(nz, half, cols):
    dma = pltpu.SemaphoreType.DMA
    p = half // nz
    steps = nz.bit_length() - 1
    shapes = [pltpu.VMEM((nz - 1, p, cols), BF), pltpu.VMEM((p, cols), BF)]
    for m in (nz - 1, nz - 1, nz):
        shapes += [dma((m,)), dma((m,))]
    return shapes + [dma]


def turn(ng, nz, *refs):
    at = Places(ng, nz)
    (a2_hbm, dm_hbm, h_hbm, da_hbm, o_hbm, wo_hbm, wu_hbm, wd_hbm, gd1_hbm, gu1_hbm, vec_ref,
     act_out, dh_out, do_out, gd_out, gu_out, go_out, gbu_out, sum_out, td_out, tu_out,
     a2, a2t, dm, h, da, o, wo, wu, wd, work, go_s, slot_a, slot_b, slot_c, slot_d,
     blk_sem, big_sem, out_sem, g_sem, a_sem) = refs[:41]
    early_d = Early(at, gd1_hbm, True, refs[41:])
    early_u = Early(at, gu1_hbm, True, early_d.rest)
    rows, width = h.shape
    half = rows // 2

    def block_copy(j, i):
        src, dst = ((a2_hbm, a2), (dm_hbm, dm), (da_hbm, da))[j]
        part = rows_at(i * half, half)
        return pltpu.make_async_copy(src.at[part, :], dst.at[part, :], blk_sem.at[j, i])

    def big_copy(j):
        src, dst = ((wu_hbm, wu), (wd_hbm, wd), (h_hbm, h), (o_hbm, o), (wo_hbm, wo))[j]
        return pltpu.make_async_copy(src, dst, big_sem.at[j])

    block_copy(0, 0).start()
    big_copy(0).start()
    block_copy(1, 0).start()
    big_copy(1).start()
    for j, i in ((0, 1), (1, 1), (2, 0), (2, 1)):
        block_copy(j, i).start()
    for j in range(2, 5):
        big_copy(j).start()
    at.greet(True, False)
    early_d.start_core()
    early_u.start_core()
    for j, i in ((0, 0), (1, 0), (0, 1), (1, 1)):
        block_copy(j, i).wait()
    for j in range(2):
        big_copy(j).wait()
    a2t[0:width, :] = a2[...].T
    a2t[width:, :] = jnp.ones_like(a2t[width:, :])

    ff = wu.shape[1]
    share = ff // ng + gd1_hbm.shape[0] // ng
    bias = unit_bias(vec_ref, ng, share, gd1_hbm.shape[0] // ng, ff // ng)
    ft = tile_of(ff)
    tiles = ff // ft
    slots = ((slot_a, slot_b), (slot_c, slot_d))
    pending = []

    def sums_here(i):
        block_copy(2, i).wait()

    act_copies = [
        pltpu.make_async_copy(work.at[:, 0:ft], act_out.at[:, t * ft : (t + 1) * ft], a_sem.at[t]) for t in range(tiles)
    ]
    for t in range(tiles):
        if t:
            act_copies[t - 1].wait()
        if t >= 2:
            for copy in pending[2 * (t - 2) : 2 * (t - 1)]:
                copy.wait()
        gd_slot, gu_slot = slots[t % 2][0].at[0:ft], slots[t % 2][1].at[:, 0:ft]
        mlp_tile(
            t, ft, 2, a2, a2t, dm, wu, wd, bias, da, work.at[:, 0:width], work.at[:, width : 2 * width],
            gd_slot, gu_slot, gbu_out.at[:, t * ft : (t + 1) * ft],
            (act_copies[t].start,)
            + ((early_d.start_group, early_u.start_group) if t == 0 else (early_d.turn_group, early_u.turn_group) if t == 1 else ()),
            sums_here if t == 0 else lambda i: None,
        )
        units = slice(t * ft, (t + 1) * ft)
        pending.append(pltpu.make_async_copy(gd_slot, gd_out.at[units, :], g_sem.at[0, t]))
        pending.append(pltpu.make_async_copy(gu_slot, gu_out.at[:, units], g_sem.at[1, t]))
        for copy in pending[-2:]:
            copy.start()

    for j in range(2, 5):
        big_copy(j).wait()
    sum_out[...] = jnp.zeros_like(sum_out)

    act_copies[-1].wait()

    def post(b, _):
        im = rows_at(b * (rows // 4), rows // 4)
        hidden = h[im, :]
        cot = dm[im, :].astype(F32)
        normed, rstd = normalize(hidden)
        grad = da[im, :]
        dh = cot + norm_back(grad, normed, rstd, vec_ref[6:7, :])
        h[im, :] = dh
        dz = dh.astype(BF)
        work[im, 0:width] = dz
        work[im, width : 2 * width] = dot_t(dz, wo[...]).astype(BF)
        for j, term in enumerate((dz.astype(F32), cot, grad * normed, grad)):
            sum_out[j : j + 1, :] += jnp.sum(term, 0, keepdims=True)
        return 0

    lax.fori_loop(0, 4, post, 0)
    dh_copy = pltpu.make_async_copy(h, dh_out, out_sem.at[0])
    do_copy = pltpu.make_async_copy(work.at[:, width : 2 * width], do_out, out_sem.at[1])
    dh_copy.start()
    do_copy.start()
    go_s[...] = dot(o[...].T, work[:, 0:width]).astype(BF)
    go_copy = pltpu.make_async_copy(go_s, go_out, out_sem.at[2])
    go_copy.start()
    early_d.collect()
    td_copy = pltpu.make_async_copy(early_d.tz, td_out, out_sem.at[3])
    td_copy.start()
    early_u.collect()
    tu_copy = pltpu.make_async_copy(early_u.tz, tu_out, out_sem.at[4])
    tu_copy.start()
    early_d.close()
    early_u.close()
    for copy in pending[-4:] + [dh_copy, do_copy, go_copy, td_copy, tu_copy]:
        copy.wait()


def run_turn(ng, nr, a2, dm, h, da, o, wo, wu, wd, gd1, gu1, vecs):
    nz = nr // 2
    rows, width = h.shape
    ff = wu.shape[1]
    ft = tile_of(ff)
    any_spec = pl.BlockSpec(memory_space=pl.ANY)
    vmem = pl.BlockSpec(memory_space=pltpu.VMEM)
    dma = pltpu.SemaphoreType.DMA
    sizes = [(g.shape[0] // ng // 2, g.shape[1]) for g in (gd1, gu1)]

    def bf(*shape):
        return jax.ShapeDtypeStruct(shape, BF)

    def f32(*shape):
        return jax.ShapeDtypeStruct(shape, F32)

    scratch = [
        pltpu.VMEM((rows, width), BF),
        pltpu.VMEM((width + 16, rows), BF),
        pltpu.VMEM((rows, width), BF),
        pltpu.VMEM((rows, width), F32),
        pltpu.VMEM((rows, width), F32),
        pltpu.VMEM((rows, width), BF),
        pltpu.VMEM((width, width), BF),
        pltpu.VMEM(wu.shape, BF),
        pltpu.VMEM(wd.shape, BF),
        pltpu.VMEM((rows, 2 * width), BF),
        pltpu.VMEM((width, width), BF),
        pltpu.VMEM((ft, width), BF),
        pltpu.VMEM((width, ft), BF),
        pltpu.VMEM((ft, width), BF),
        pltpu.VMEM((width, ft), BF),
        dma((3, 2)),
        dma((5,)),
        dma((5,)),
        dma((2, ff // ft)),
        dma((ff // ft,)),
    ]
    for hh, w in sizes:
        scratch += early_scratch(ng, nz, hh, w, True)
    return pl.pallas_call(
        functools.partial(turn, ng, nz),
        out_shape=(
            bf(rows, ff), f32(rows, width), bf(rows, width), bf(ff, width), bf(width, ff), bf(width, width),
            f32(1, ff), f32(8, width),
        ) + tuple(bf(nz, hh // nz, w) for hh, w in sizes),
        in_specs=[any_spec] * 10 + [vmem],
        out_specs=(any_spec,) * 6 + (vmem, vmem, any_spec, any_spec),
        scratch_shapes=scratch,
        compiler_params=params(64, collective_id=1, has_side_effects=True),
    )(a2, dm, h, da, o, wo, wu, wd, gd1, gu1, vecs)


def vector_sum(at, v_s, landed, sems):
    v_g, v_z, v_c = landed
    g_send, g_recv, z_send, z_recv, c_send, c_recv = sems

    def copies(level):
        if level == 0:
            return [remote(v_s.at[0], v_g.at[k - 1], g_send.at[k - 1], g_recv.at[k - 1], at.group(k)) for k in range(1, at.ng)]
        if level == 1:
            return [remote(v_s.at[1], v_z.at[j - 1], z_send.at[j - 1], z_recv.at[j - 1], at.chip(j)) for j in range(1, at.nz)]
        return [remote(v_s.at[2], v_c.at[0], c_send.at[0], c_recv.at[0], at.sib)]

    def start(level):
        for copy in copies(level):
            copy.start()

    def add(level):
        for copy in copies(level):
            copy.wait()
        total = v_s[level]
        buf = (v_g, v_z, v_c)[level]
        for j in range(buf.shape[0]):
            total = total + buf[j]
        v_s[level + 1] = total

    return start, add


def vector_scratch(ng, nz, shape):
    dma = pltpu.SemaphoreType.DMA
    shapes = [pltpu.VMEM((4,) + shape, F32)]
    shapes += [pltpu.VMEM((m,) + shape, F32) for m in (ng - 1, nz - 1, 1)]
    for m in (ng - 1, nz - 1, 1):
        shapes += [dma((m,)), dma((m,))]
    return shapes


PAIRS_A, PAIRS_B = (0, 1, 2, 3), (4, 5)


def act_pieces(n1, n2, width):
    out = []
    for j in range((n1 + n2) // width):
        cuts = [j * width] + ([n1] if j * width < n1 < (j + 1) * width else []) + [(j + 1) * width]
        out += [(j, start, stop) for start, stop in zip(cuts, cuts[1:])]
    return out


def plan(early, late):
    steps = [chunk.stages() for chunk in late[:2]]
    for first, second in zip(early, late[2:]):

        def join(first=first, second=second):
            first.collect()
            second.start_halves()

        steps.append([first.start_core, first.start_group, first.turn_group, join] + second.stages()[1:])
    return steps


def backward(ng, nz, length, *refs):
    at = Places(ng, nz)
    (gd_hbm, gu_hbm, go_hbm, td1_hbm, tu1_hbm, qkv_hbm, do_hbm, o_hbm, a1_hbm, wq_hbm, x_hbm, dh_hbm, h_hbm, act1_hbm, act2_hbm, d1_hbm, d2_hbm, vec_ref, sum_ref, gbu1_ref, gbu2_ref,
     ig_out, out_out, td1_out, tu1_out, td_out, tu_out, to_out, ta_out, tb_out, vec_out,
     qkv_s, do_s, o_s, a1_s, a1t, wq_s, x_s, dh_s, inner_s, ga_s, gb_s, w_s, stage, im_sem, big_sem, ig_sem, tz_d1, tz_u1, t_sem, h_sem, act_sem) = refs[:52]
    rest = refs[52:]
    early, late = [], []
    for src, load in ((gd_hbm, True), (gu_hbm, True), (go_hbm, True), (ga_s, False), (gb_s, False)):
        early.append(Early(at, src, load, rest))
        rest = early[-1].rest
    pieces = [tz_d1, tz_u1] + [e.tz for e in early]
    for tz, total in zip(pieces, (td1_out, tu1_out, td_out, tu_out, to_out, ta_out, tb_out)):
        kind = LateDirect if len(late) >= 5 else Late
        late.append(kind(at, tz, rest, total))
        rest = late[-1].rest
    v_s = rest[0]
    v_start, v_add = vector_sum(at, v_s, rest[1:4], rest[4:10])

    images = ig_sem.shape[0] // 2
    rows, width = do_s.shape
    full = rows // images
    scale = HEAD_DIM**-0.5

    def image_copies(i):
        return [
            pltpu.make_async_copy(src.at[rows_at(i * full, full), :], dst.at[rows_at(i * full, full), :], im_sem.at[j, i])
            for j, (src, dst) in enumerate(((qkv_hbm, qkv_s), (do_hbm, do_s), (o_hbm, o_s)))
        ]

    def big_copy(j):
        src, dst = ((a1_hbm, a1_s), (wq_hbm, wq_s), (x_hbm, x_s), (dh_hbm, dh_s), (d1_hbm, w_s.at[0 : d1_hbm.shape[0], :]), (d2_hbm, w_s.at[d1_hbm.shape[0] :, :]))[j]
        return pltpu.make_async_copy(src, dst, big_sem.at[j])

    for i in range(images):
        for copy in image_copies(i):
            copy.start()
    tz_copies = [pltpu.make_async_copy(td1_hbm, tz_d1, t_sem.at[0]), pltpu.make_async_copy(tu1_hbm, tz_u1, t_sem.at[1])]
    for copy in tz_copies:
        copy.start()
    at.greet(True, True)
    d1, u1, d2, u2, go, ga, gb = (iter(steps) for steps in plan(early, late))

    def advance(*chunks):
        for chunk in chunks:
            next(chunk)()

    for copy, chunk in zip(tz_copies, (d1, u1)):
        copy.wait()
        advance(chunk)
    advance(d2, u2, go)

    cut = length // 16 * 16
    low_half = lax.broadcasted_iota(jnp.int32, (full, 128), 1) < HEAD_DIM
    pick = lax.broadcasted_iota(jnp.int32, (16, width), 1) // HEAD_DIM == lax.broadcasted_iota(jnp.int32, (16, width), 0)
    pick = jnp.where(pick, 1.0, 0.0).astype(BF)
    live = lax.broadcasted_iota(jnp.int32, (full - cut, full), 0) < length - cut

    def attend_back(i, pairs):
        im = rows_at(i * full, full)
        for p in pairs:
            col = p * 128
            q = qkv_s[im, col : col + 128] * jnp.asarray(scale, BF)
            k = qkv_s[im, col + width : col + width + 128]
            v = qkv_s[im, col + 2 * width : col + 2 * width + 128]
            do = do_s[im, col : col + 128]
            kt = k.T
            dq, dk, dv = [], None, None
            for h in range(2):
                mine = low_half if h == 0 else ~low_half
                qm = jnp.where(mine, q, jnp.zeros_like(q))
                dom = jnp.where(mine, do, jnp.zeros_like(do))
                s = dot_t(k, qm)
                s = jnp.concatenate([s[:cut], jnp.where(live, s[cut:], -1e30)], 0)
                e = jnp.exp(s - jnp.max(s, 0, keepdims=True))
                probs = e * (1.0 / jnp.sum(e, 0, keepdims=True))
                ds = (probs * (dot_t(v, dom) - inner_s[i, 2 * p + h : 2 * p + h + 1, :])).astype(BF)
                dv_h, dk_h = dot(probs.astype(BF), dom), dot(ds, qm)
                dv = dv_h if dv is None else dv + dv_h
                dk = dk_h if dk is None else dk + dk_h
                dq.append(dot(kt[HEAD_DIM * h : HEAD_DIM * (h + 1), :], ds))
            dq = (jnp.concatenate(dq, 0) * scale).astype(BF).T
            qkv_s[im, col : col + 128] = dq
            qkv_s[im, col + width : col + width + 128] = dk.astype(BF)
            qkv_s[im, col + 2 * width : col + 2 * width + 128] = dv.astype(BF)

    def act_copies(b):
        n1, n2 = d1_hbm.shape[0], d2_hbm.shape[0]
        out = []
        for j, start, stop in act_pieces(n1, n2, width):
            src, first = (act1_hbm, start) if start < n1 else (act2_hbm, start - n1)
            src = src.at[rows_at(b * 2 * full, 2 * full), first : first + stop - start]
            col = start - j * width
            dst = (do_s, o_s)[b % 2].at[j * 2 * full : (j + 1) * 2 * full, col : col + stop - start]
            out.append(pltpu.make_async_copy(src, dst, act_sem.at[b % 2, len(out)]))
        return out

    def act_start(b):
        for copy in act_copies(b):
            copy.start()

    def when(i, index, *chunks):
        @pl.when(i == index)
        def _():
            advance(*chunks)

    def first_pass(i, _):
        for copy in image_copies(i):
            copy.wait()
        when(i, 1, d2)
        when(i, 2, d1)
        when(i, 3, u2, u1)
        when(i, 4, go, d1)
        when(i, 5, d2, u1)
        when(i, 6, d1)
        when(i, 7, u1)

        @pl.when(i == 3)
        def _():
            for j in range(6):
                big_copy(j).start()

        im = rows_at(i * full, full)
        prod = do_s[im, :].astype(F32) * o_s[im, :].astype(F32)
        high = prod.astype(BF)
        inner_s[i] = dot_t(pick, high) + dot_t(pick, (prod - high.astype(F32)).astype(BF))
        attend_back(i, PAIRS_A)
        return 0

    def weight_grad(pairs, g_ref):
        start, stop = pairs[0] * 128, pairs[-1] * 128 + 128
        wide = stop - start
        for n in range(3):
            dp = qkv_s[:, n * width + start : n * width + stop]
            both = dot(a1t[...], dp)
            g_ref[:, n * wide : (n + 1) * wide] = both[0:width].astype(BF)
            if n != 1:
                row = 0 if n == 0 else 1
                v_s[0, row : row + 1, start:stop] = both[width : width + 1]

    lax.fori_loop(0, images, first_pass, 0)
    big_copy(0).wait()
    a1t[0:width, :] = a1_s[...].T
    a1t[width:, :] = jnp.ones_like(a1t[width:, :])
    weight_grad(PAIRS_A, ga_s)
    advance(ga, d2, u2, go, d1, u1)

    def second_pass(i, _):
        when(i, 2, ga)
        when(i, 3, u2)
        when(i, 4, d2)
        when(i, 5, go)
        when(i, 6, u2)
        attend_back(i, PAIRS_B)
        return 0

    lax.fori_loop(0, images, second_pass, 0)
    weight_grad(PAIRS_B, gb_s)
    advance(gb, ga, go, d2)

    for j in range(1, 6):
        big_copy(j).wait()
    act_start(0)
    act_start(1)
    v_s[0, 2:4, :] = sum_ref[0:2, :]
    v_s[0, 4:6, :] = jnp.zeros((2, width), F32)
    v_s[0, 6:8, :] = sum_ref[2:4, :]
    one, two = gbu1_ref.shape[1] // ng, gbu2_ref.shape[1] // ng
    for m in range(ng):
        row, col = divmod(m * (one + two), width)
        v_s[0, 8 + row : 9 + row, col : col + one] = gbu1_ref[0:1, m * one : (m + 1) * one]
        v_s[0, 8 + row : 9 + row, col + one : col + one + two] = gbu2_ref[0:1, m * two : (m + 1) * two]

    def input_copy(i):
        return pltpu.make_async_copy(stage.at[i], ig_out.at[i], ig_sem.at[i])

    def output_copy(i):
        return pltpu.make_async_copy(stage.at[i], out_out.at[i], ig_sem.at[images + i])

    def hidden_copy(b):
        part = rows_at(b * 2 * full, 2 * full)
        return pltpu.make_async_copy(h_hbm.at[part, :], dh_s.at[part, :], h_sem.at[b])

    def input_pass(b, _):
        first = b * 2
        when(b, 1, gb, u2)
        when(b, 2, ga, go)
        when(b, 3, gb, d2, u2)
        im = rows_at(first * full, 2 * full)
        da = dot_t(qkv_s[im, :], wq_s[...])
        normed, rstd = normalize(x_s[im, :].astype(F32))
        grad = dh_s[im, :] + norm_back(da, normed, rstd, vec_ref[4:5, :])
        grad = grad.astype(BF).reshape(2, full, width)
        for i in range(2):
            stage[first + i] = grad[i, :length, :]
            input_copy(first + i).start()
        v_s[0, 4:5, :] += jnp.sum(da * normed, 0, keepdims=True)
        v_s[0, 5:6, :] += jnp.sum(da, 0, keepdims=True)
        return 0

    lax.fori_loop(0, images // 2, input_pass, 0)
    for b in range(images // 2):
        hidden_copy(b).start()
    for i in range(images):
        input_copy(i).wait()

    def output_pass(b):
        act = (do_s, o_s)[b % 2]
        for copy in act_copies(b):
            copy.wait()
        hidden_copy(b).wait()
        im = rows_at(b * 2 * full, 2 * full)
        total = dh_s[im, :] + vec_ref[3:4, :]
        for j in range(w_s.shape[0] // width):
            total = total + dot(act[j * 2 * full : (j + 1) * 2 * full, :], w_s[j * width : (j + 1) * width, :])
        total = total.astype(BF).reshape(2, full, width)
        for i in range(2):
            stage[2 * b + i] = total[i, :length, :]
            output_copy(2 * b + i).start()
        if b + 2 < images // 2:
            act_start(b + 2)

    v_start(0)
    advance(gb, go)
    output_pass(0)
    advance(ga, d2, u2)
    v_add(0)
    v_start(1)
    output_pass(1)
    advance(gb, go)
    output_pass(2)
    v_add(1)
    v_start(2)
    advance(ga)
    output_pass(3)
    advance(gb)
    v_add(2)
    vec_out[...] = v_s[3]
    for chunk in (d1, u1, d2, u2, go, ga, gb):
        for step in chunk:
            step()
    for reducer in early:
        reducer.close()
    for reducer in late:
        reducer.finish()
    for i in range(images):
        output_copy(i).wait()


def run_backward(ng, nr, images, length, grads, firsts, qkv, do, attended, a1, wq, tokens, dh, h, acts, downs, vecs, sums, g_bu):
    width = tokens.shape[1]
    full = dh.shape[0] // images
    nz = nr // 2
    any_spec = pl.BlockSpec(memory_space=pl.ANY)
    vmem = pl.BlockSpec(memory_space=pltpu.VMEM)
    dma = pltpu.SemaphoreType.DMA
    cols_a, cols_b = 3 * 128 * len(PAIRS_A), 3 * 128 * len(PAIRS_B)
    sizes = [(g.shape[0] // ng // 2, g.shape[1]) for g in grads]
    sizes += [(width // ng // 2, cols_a), (width // ng // 2, cols_b)]
    all_sizes = [(t.shape[0] * t.shape[1], t.shape[2]) for t in firsts] + sizes
    total_shapes = [(2, nz, h // nz, w) for h, w in all_sizes]
    vec_shape = vecs.shape
    scratch = [
        pltpu.VMEM(qkv.shape, BF),
        pltpu.VMEM(do.shape, BF),
        pltpu.VMEM(attended.shape, BF),
        pltpu.VMEM(a1.shape, BF),
        pltpu.VMEM((width + 16, images * full), BF),
        pltpu.VMEM(wq.shape, BF),
        pltpu.VMEM(tokens.shape, BF),
        pltpu.VMEM(dh.shape, F32),
        pltpu.VMEM((images, 16, full), F32),
        pltpu.VMEM((width, cols_a), BF),
        pltpu.VMEM((width, cols_b), BF),
        pltpu.VMEM((downs[0].shape[0] + downs[1].shape[0], width), BF),
        pltpu.VMEM((images, length, width), BF),
        dma((3, images)),
        dma((6,)),
        dma((2 * images,)),
        pltpu.VMEM(firsts[0].shape, BF),
        pltpu.VMEM(firsts[1].shape, BF),
        dma((2,)),
        dma((images // 2,)),
        dma((2, len(act_pieces(downs[0].shape[0], downs[1].shape[0], width)))),
    ]
    for i, (hh, w) in enumerate(sizes):
        scratch += early_scratch(ng, nz, hh, w, i < 3)
    for hh, w in all_sizes:
        scratch += late_scratch(nz, hh, w)
    scratch += vector_scratch(ng, nz, vec_shape)
    res = pl.pallas_call(
        functools.partial(backward, ng, nz, length),
        out_shape=(jax.ShapeDtypeStruct((images, length, width), BF),) * 2
        + tuple(jax.ShapeDtypeStruct(s, BF) for s in total_shapes)
        + (jax.ShapeDtypeStruct(vec_shape, F32),),
        in_specs=[any_spec] * 17 + [vmem] * 4,
        out_specs=(any_spec,) * 9 + (vmem,),
        scratch_shapes=scratch,
        compiler_params=params(62, collective_id=2, has_side_effects=True),
    )(*grads, *firsts, qkv, do, attended, a1, wq, tokens, dh, h, *acts, *downs, vecs, sums, *g_bu)
    return res[0], res[1], res[2:9], res[9]


def whole_totals(ng, width, totals):
    down1, up1, down, up, out, qa, qb = [t.reshape(-1, t.shape[3]).astype(F32) for t in totals]
    down = jnp.concatenate([down1, down], 0)
    one, two = up1.shape[1] // ng, up.shape[1] // ng
    parts = []
    for m in range(ng):
        parts += [up1[:, m * one : (m + 1) * one], up[:, m * two : (m + 1) * two]]
    up = jnp.concatenate(parts, 1)
    wide_a, wide_b = qa.shape[1] // 3, qb.shape[1] // 3
    parts = []
    for n in range(3):
        parts += [qa[:, n * wide_a : (n + 1) * wide_a], qb[:, n * wide_b : (n + 1) * wide_b]]
    return [jnp.concatenate(parts, 1), out, up, down]


def rows_of(ref, cols):
    return ref[:, :, cols].reshape(ref.shape[0] * ref.shape[1], -1)


def adam_block(ng, *refs):
    vec = refs[7]
    states, results = refs[8:23], refs[23:]

    def update(index, place, gradient, rate, decay):
        w, m, v = (ref[place] for ref in states[3 * index : 3 * index + 3])
        first, second, new = adamw_update(w, m, v, gradient, rate, decay)
        for ref, value in zip(results[4 * index : 4 * index + 4], (gradient, first, second, new)):
            ref[place] = value

    qa, qb, out, up1, up2, down1, down2 = (ref.at[0] for ref in refs[:7])
    wide_a, wide_b = qa.shape[2] // 3, qb.shape[2] // 3
    for n in range(3):
        start = n * (wide_a + wide_b)
        update(0, (slice(None), slice(start, start + wide_a)), rows_of(qa, slice(n * wide_a, (n + 1) * wide_a)).astype(F32), 0.1, 0.05)
        start += wide_a
        update(0, (slice(None), slice(start, start + wide_b)), rows_of(qb, slice(n * wide_b, (n + 1) * wide_b)).astype(F32), 0.1, 0.05)
    update(1, ..., rows_of(out, slice(None)).astype(F32), 0.1, 0.05)
    strip = up1.shape[2] // ng
    for m in range(ng):
        for j, ref in enumerate((up1, up2)):
            start = (2 * m + j) * strip
            update(2, (slice(None), slice(start, start + strip)), rows_of(ref, slice(m * strip, (m + 1) * strip)).astype(F32), 0.1, 0.05)
    for j, ref in enumerate((down1, down2)):
        update(3, j, rows_of(ref, slice(None)).astype(F32), 0.1, 0.05)

    @pl.when(pl.program_id(0) == 0)
    def _():
        g = lax.axis_index("group")
        own = states[12].shape[1]
        total = jnp.zeros(states[12].shape, F32)
        for j in range(ng):
            total = total + jnp.where(g == j, vec[:, j * own : (j + 1) * own], 0.0)
        update(4, ..., total, 0.8, 0.0)


def run_adam(ng, totals, vec_total, states):
    down1, up1, down2, up2, out, qa, qb = totals
    nz, p = out.shape[1], out.shape[2]
    take = 2

    def piece(t):
        return pl.BlockSpec((1, take) + t.shape[2:], lambda i: (i // (nz // take), i % (nz // take), 0, 0))

    def block(index, state):
        if index == 3:
            return pl.BlockSpec((2, take * down1.shape[2], state.shape[2]), lambda i: (0, i, 0))
        if index == 4:
            return pl.BlockSpec(state.shape, lambda i: (0, 0))
        return pl.BlockSpec((take * p, state.shape[1]), lambda i: (i, 0))

    pieces = [qa, qb, out, up1, up2, down1, down2]
    states = list(states)
    down_shape = states[9].shape
    states[9:12] = [s.reshape(2, down_shape[0] // 2, down_shape[1]) for s in states[9:12]]
    specs = [block(i // 3, s) for i, s in enumerate(states)]
    out_specs, out_shapes = [], []
    for index in range(5):
        out_specs += [specs[3 * index]] * 4
        out_shapes += [jax.ShapeDtypeStruct(states[3 * index].shape, F32)] * 4
    res = pl.pallas_call(
        functools.partial(adam_block, ng),
        grid=(2 * nz // take,),
        out_shape=tuple(out_shapes),
        in_specs=[piece(t) for t in pieces] + [pl.BlockSpec(vec_total.shape, lambda i: (0, 0))] + specs,
        out_specs=tuple(out_specs),
        compiler_params=params(),
    )(*pieces, vec_total, *states)
    res = list(res)
    res[12:16] = [r.reshape(down_shape) for r in res[12:16]]
    return res


def adamw_update(weight, first_moment, second, gradient, step_rate, decay_coef):
    first_new = beta_one * first_moment + (1.0 - beta_one) * gradient
    second_new = beta_two * second + (1.0 - beta_two) * gradient * gradient
    fix_one = 1.0 - beta_one**STEP
    fix_two = 1.0 - beta_two**STEP
    weight_new = weight - step_rate * (
        first_new / fix_one / (jnp.sqrt(second_new / fix_two) + adam_eps) + decay_coef * weight
    )
    return (first_new, second_new, weight_new)


def per_device(
    ng, nr, tokens, cotangent, w_qkv, m_qkv, v_qkv, w_out, m_out, v_out, w_up, m_up, v_up,
    w_down, m_down, v_down, vectors, m_vectors, v_vectors,
):
    images, length, width = tokens.shape
    full = -(-length // 16) * 16
    (wq, wo, u2, d2, vecs, a1, qkv, attended, a2, dm, h, act1, d1, da, gd1, gu1, x, gbu1) = run_forward(
        ng, nr, full, tokens, cotangent, w_qkv, w_out, w_up, w_down, vectors
    )
    act2, dh, do, gd2, gu2, g_out, gbu2, sums, td1, tu1 = run_turn(
        ng, nr, a2, dm, h, da, attended, wo, u2, d2, gd1, gu1, vecs
    )
    input_grad, output, totals, vec_total = run_backward(
        ng, nr, images, length, (gd2, gu2, g_out), (td1, tu1), qkv, do, attended, a1, wq, x, dh, h, (act1, act2), (d1, d2),
        vecs, sums, (gbu1, gbu2),
    )
    states = (
        w_qkv, m_qkv, v_qkv, w_out, m_out, v_out, w_up, m_up, v_up, w_down, m_down, v_down, vectors, m_vectors, v_vectors,
    )
    outcome = [output, input_grad]
    if td1.shape == totals[2].shape[1:] and totals[4].shape[2] % 8 == 0:
        return tuple(outcome + run_adam(ng, totals, vec_total, states))
    own = vectors.shape[1]
    gradients = whole_totals(ng, width, totals)
    gradients.append(lax.dynamic_slice_in_dim(vec_total, lax.axis_index("group") * own, own, 1))
    for index, gradient in enumerate(gradients):
        rate, decay = (0.8, 0.0) if index == 4 else (0.1, 0.05)
        outcome.append(gradient)
        outcome.extend(adamw_update(*states[3 * index : 3 * index + 3], gradient, rate, decay))
    return tuple(outcome)


def solution(mesh):
    ng, nr = mesh.shape["group"], mesh.shape["replica"]
    tokens_spec = P(("replica", "group"), None, None)
    rows_spec, cols_spec = P("group", None), P(None, "group")
    in_specs = (tokens_spec,) * 2 + (rows_spec,) * 12 + (cols_spec,) * 3
    out_specs = (tokens_spec,) * 2 + (rows_spec,) * 16 + (cols_spec,) * 4
    return jax.shard_map(
        functools.partial(per_device, ng, nr), mesh=mesh, in_specs=in_specs, out_specs=out_specs, check_vma=False
    )
```

```python
import functools

import jax
import jax.numpy as jnp
from jax import lax
from jax.experimental import pallas as pl
from jax.experimental.pallas import tpu as pltpu
from jax.sharding import PartitionSpec as P

F32 = jnp.float32
BF = jnp.bfloat16
HEADS = 12
HEAD_DIM = 64
STEP = 10
MIB = 2**20
MESH = pl.DeviceIdType.MESH

norm_eps = 1e-06
beta_one = 0.9
beta_two = 0.999
adam_eps = 1e-08


def dot(a, b):
    return jnp.dot(a, b, preferred_element_type=F32)


def dot_t(a, b):
    return lax.dot_general(a, b, (((1,), (1,)), ((), ())), preferred_element_type=F32)


def dot_tn(a, b):
    return lax.dot_general(a, b, (((0,), (0,)), ((), ())), preferred_element_type=F32)


def flip(index, mask):
    out, bit = index, 1
    while bit <= mask:
        if mask & bit:
            out = out + bit * (1 - 2 * lax.rem(lax.div(index, bit), 2))
        bit *= 2
    return out


def rows_at(start, size):
    return pl.ds(pl.multiple_of(start, 16), size)


def normalize(hidden):
    centered = hidden - jnp.mean(hidden, -1, keepdims=True)
    rstd = lax.rsqrt(jnp.mean(centered * centered, -1, keepdims=True) + norm_eps)
    return centered * rstd, rstd


def norm_back(grad, normed, rstd, gain):
    e = grad * gain
    mean_e = jnp.mean(e, -1, keepdims=True)
    mean_en = jnp.mean(e * normed, -1, keepdims=True)
    return (e - mean_e - normed * mean_en) * rstd


def gelu_parts(u):
    d = 1.0 + (0.3275911 * 0.7071067811865476) * jnp.abs(u)
    t = pl.reciprocal(d, approx=True)
    t = t * (2.0 - d * t)
    e = jnp.exp2(u * u * (-0.5 * 1.4426950408889634))
    poly = ((0.5307027145 * t - 0.7265760135) * t + 0.7107068705) * t - 0.142248368
    q = (poly * t + 0.127414796) * t * e
    phi = jnp.where(u > 0, 1.0 - q, q)
    return u * phi, phi + (u * 0.3989422804014327) * e


def params(mib=58, **kw):
    return pltpu.CompilerParams(vmem_limit_bytes=mib * MIB, **kw)


class Places:
    def __init__(self, ng, nz):
        self.ng, self.nz = ng, nz
        self.r, self.g = lax.axis_index("replica"), lax.axis_index("group")
        self.c, self.z = lax.rem(self.r, 2), lax.div(self.r, 2)
        self.sib = {"replica": flip(self.r, 1), "group": self.g}

    def group(self, k):
        return {"replica": self.r, "group": flip(self.g, k)}

    def chip(self, j):
        return {"replica": flip(self.r, 2 * j), "group": self.g}

    def greet(self, group, chips):
        barrier = pltpu.get_barrier_semaphore()
        targets = [self.sib]
        if group:
            targets += [self.group(k) for k in range(1, self.ng)]
        if chips:
            targets += [self.chip(j) for j in range(1, self.nz)]
        for target in targets:
            pl.semaphore_signal(barrier, inc=1, device_id=target, device_id_type=MESH)
        pl.semaphore_wait(barrier, len(targets))


def remote(src, dst, send, recv, target):
    return pltpu.make_async_remote_copy(src, dst, send, recv, device_id=target, device_id_type=MESH)


class Gather:
    def __init__(self, at, buf, sems):
        self.at, self.buf = at, buf
        self.x_send, self.x_recv, self.f_send, self.f_recv = sems
        self.half = buf.shape[0] // at.ng // 2
        self.relay = at.ng == 4

    def rows(self, k, c, lower=None):
        start, size = flip(self.at.g, k) * 2 * self.half + c * self.half, self.half
        if lower is not None:
            size = self.half // 2
            start = start + (0 if lower else size)
        return self.buf.at[rows_at(start, size), :]

    def direct(self, k):
        part = self.rows(0, self.at.c)
        return remote(part, part, self.x_send.at[k - 1], self.x_recv.at[k - 1], self.at.group(k))

    def relayed(self, k):
        part = self.rows(k, self.at.c, k == 1)
        return remote(part, part, self.x_send.at[1 + k], self.x_recv.at[1 + k], self.at.group(3 - k))

    def relayed_in(self, k):
        part = self.rows(3, self.at.c, k == 1)
        return remote(part, part, self.x_send.at[1 + k], self.x_recv.at[1 + k], self.at.group(3 - k))

    def across(self, k):
        part = self.rows(k, self.at.c)
        return remote(part, part, self.f_send.at[k - 1], self.f_recv.at[k - 1], self.at.sib)

    def across_in(self, k):
        part = self.rows(k, 1 - self.at.c)
        return remote(part, part, self.f_send.at[k - 1], self.f_recv.at[k - 1], self.at.sib)

    def near(self):
        return (1, 2) if self.relay else range(1, self.at.ng)

    def start(self):
        for k in self.near():
            self.direct(k).start()

    def pass_on(self):
        for k in self.near():
            self.direct(k).wait_recv()
            if self.relay:
                self.relayed(k).start()
            self.across(k).start()

    def settle(self):
        if self.relay:
            for k in (1, 2):
                self.relayed_in(k).wait_recv()
            self.across(3).start()

    def finish(self):
        for k in range(1, self.at.ng):
            self.across_in(k).wait_recv()

    def close(self):
        for k in self.near():
            self.direct(k).wait_send()
            if self.relay:
                self.relayed(k).wait_send()
        for k in range(1, self.at.ng):
            self.across(k).wait_send()


def gather_sems(ng):
    dma = pltpu.SemaphoreType.DMA
    n = 4 if ng == 4 else ng - 1
    return [dma((n,)), dma((n,)), dma((ng - 1,)), dma((ng - 1,))]


def strips(ng, ff):
    share = ff // ng
    one = -(-share // 256) * 128
    return share, one, share - one


def tile_of(size):
    return 768 if size % 768 == 0 else 512


def mlp_tile(t, ft, blocks, a2, a2t, dm, wu, wd, bias, da_acc, act_s, du_s, gd_slot, gu_slot, gbu, before=(), ready=lambda i: None):
    units = slice(t * ft, (t + 1) * ft)
    rows, width = da_acc.shape[0] // blocks, da_acc.shape[1]

    def body(i, _):
        im = rows_at(i * rows, rows)
        u = dot(a2[im, :], wu[:, units]) + bias[:, units]
        da = dot_t(dm[im, :], wd[units, :])
        act, slope = gelu_parts(u)
        act = act.astype(BF)
        du = (da * slope).astype(BF)
        act_s[im, 0:ft] = act
        du_s[im, 0:ft] = du
        ready(i)
        da_acc[im, :] += dot_t(du, wu[:, units])
        return 0

    lax.fori_loop(0, blocks, body, 0)
    for step in before:
        step()
    gd_slot[...] = dot(act_s[:, 0:ft].T, dm[...]).astype(BF)
    both = dot(a2t[...], du_s[:, 0:ft])
    gu_slot[...] = both[0:width].astype(BF)
    gbu[:, 0:ft] = both[width : width + 1]


def forward(ng, nz, length, *refs):
    at = Places(ng, nz)
    (x_hbm, cot_hbm, wq_hbm, wo_hbm, wu_hbm, wd_hbm, vec_hbm,
     wq_out, wo_out, u2_out, d2_out, vec_out, a1_out, p_out, qkv_out, o_out, a2_out, dm_out, h_out, act_out, d1_out, da_out, gd_out, gu_out, x_out, gbu_out,
     xs, cs, acc, da, h, bq, bo, bu1, bd1, bu2, bd2, vec_s, vall, a1o, qkv, dm, a2t, xf, gbu,
     w_sem, v_sem, in_sem, v_send, v_recv, out_sem, g_sem, a_sem, p_sem) = refs[:54]
    width = h.shape[1]
    blocks_q = [bq.at[:, n * width : (n + 1) * width] for n in range(bq.shape[1] // width)]
    gt, ft = ng * 128, 512
    tiles, per_gather, per = bu1.shape[1] // gt, gt // ft, ft // 128
    buffers = blocks_q + [bo, bu2, bd2]
    for t in range(tiles):
        buffers += [bu1.at[:, t * gt : (t + 1) * gt], bd1.at[t * gt : (t + 1) * gt, :]]
    gathers = [Gather(at, buf, refs[54 + 4 * i : 58 + 4 * i]) for i, buf in enumerate(buffers)]
    nq = len(blocks_q)
    g_q, (g_o, g_u2, g_d2) = gathers[:nq], gathers[nq : nq + 3]
    g_t = [gathers[nq + 3 + 2 * t : nq + 5 + 2 * t] for t in range(tiles)]
    images = xs.shape[0] // length
    full = h.shape[0] // images
    shard = wq_hbm.shape[0]
    ff = wu_hbm.shape[1]
    share, one, two = strips(ng, ff)
    nq, nu = wq_hbm.shape[1] // width, ff // width

    flat, flat_h = acc, h
    loads = []
    for n in range(nq):
        loads.append((wq_hbm.at[:, n * width : (n + 1) * width], flat.at[n * shard : (n + 1) * shard]))
    loads.append((wo_hbm, flat.at[nq * shard : (nq + 1) * shard]))
    for n in range(nu):
        loads.append((wu_hbm.at[:, n * width : (n + 1) * width], flat.at[(nq + 1 + n) * shard : (nq + 2 + n) * shard]))
    loads.append((wd_hbm, flat_h.at[0:share]))
    loads = [pltpu.make_async_copy(src, dst, w_sem.at[i]) for i, (src, dst) in enumerate(loads)]
    vec_load = pltpu.make_async_copy(vec_hbm, vec_s, v_sem)
    x_load = pltpu.make_async_copy(x_hbm, xs, in_sem.at[0])
    cot_load = pltpu.make_async_copy(cot_hbm, cs, in_sem.at[1])
    vec_load.start()
    for n in range(nq):
        loads[n].start()
    x_load.start()
    for load in loads[nq:]:
        load.start()
    cot_load.start()
    at.greet(True, False)

    vec_load.wait()
    vall[at.g] = vec_s[...].astype(BF).astype(F32)
    v_copies = [remote(vall.at[at.g], vall.at[at.g], v_send.at[k - 1], v_recv.at[k - 1], at.group(k)) for k in range(1, ng)]
    for copy in v_copies:
        copy.start()
    for n in range(nq):
        loads[n].wait()
        blocks_q[n][rows_at(at.g * shard, shard), :] = flat[n * shard : (n + 1) * shard, :].astype(BF)
        if n == 0:
            g_q[0].start()
    loads[nq].wait()
    bo[rows_at(at.g * shard, shard), :] = flat[nq * shard : (nq + 1) * shard, :].astype(BF)
    for n in range(nu):
        loads[nq + 1 + n].wait()
    for m in range(ng):
        block, col = divmod(m * share, width)
        src = slice((nq + 1 + block) * shard, (nq + 2 + block) * shard)
        for t in range(tiles):
            lanes = slice(t * gt + m * 128, t * gt + (m + 1) * 128)
            bu1[rows_at(at.g * shard, shard), lanes] = flat[src, col + t * 128 : col + (t + 1) * 128].astype(BF)
        bu2[rows_at(at.g * shard, shard), m * two : (m + 1) * two] = flat[src, col + one : col + share].astype(BF)
    loads[nq + 1 + nu].wait()
    for t in range(tiles):
        bd1[rows_at(t * gt + at.g * 128, 128), :] = flat_h[t * 128 : (t + 1) * 128, :].astype(BF)
    bd2[rows_at(at.g * two, two), :] = flat_h[one:share, :].astype(BF)

    for copy in v_copies:
        copy.wait()
    w = vall.shape[2]
    vecs = jnp.zeros((vall.shape[1], width), F32)
    for j in range(ng):
        row = lax.broadcasted_iota(jnp.int32, (w, width), 0)
        col = lax.broadcasted_iota(jnp.int32, (w, width), 1)
        vecs = vecs + dot(vall[j].astype(BF), jnp.where(col == row + j * w, 1.0, 0.0).astype(BF))
    vec_out[...] = vecs

    x_load.wait()
    lanes = width // 128

    def spread(ref):
        for j in range(lanes):
            xf[j, 0 : length * images, :] = ref[:, j * 128 : (j + 1) * 128].astype(F32)

    def image_of(i):
        return jnp.concatenate([xf[j, pl.ds(i, full, stride=images), :] for j in range(lanes)], 1)

    xf[:, length * images :, :] = jnp.zeros((lanes, (full - length) * images, 128), F32)
    spread(xs)

    def when(i, index, *steps):
        @pl.when(i == index)
        def _():
            for step in steps:
                step()

    def norm_image(i, _):
        when(i, 2, g_q[1].start)
        when(i, 5, g_q[2].start)
        when(i, images - 1, g_q[0].pass_on)
        im = rows_at(i * full, full)
        x = image_of(i)
        h[im, :] = x
        qkv[im, 0:width] = x.astype(BF)
        normed, _r = normalize(x)
        a1o[im, :] = (normed * vec_out[4:5, :] + vec_out[5:6, :]).astype(BF)
        return 0

    lax.fori_loop(0, images, norm_image, 0)
    a1_copy = pltpu.make_async_copy(a1o, a1_out, out_sem.at[0])
    a1_copy.start()
    x_copy = pltpu.make_async_copy(qkv.at[:, 0:width], x_out, out_sem.at[12])
    x_copy.start()
    cot_load.wait()
    spread(cs)

    def cot_image(i, _):
        when(i, 2, g_q[1].pass_on)
        when(i, 5, g_q[2].pass_on, g_q[0].settle)
        dm[rows_at(i * full, full), :] = image_of(i).astype(BF)
        return 0

    lax.fori_loop(0, images, cot_image, 0)
    dm_copy = pltpu.make_async_copy(dm, dm_out, out_sem.at[1])
    dm_copy.start()
    g_o.start()
    x_copy.wait()

    def each(group, name):
        for gather in group:
            if isinstance(gather, Gather):
                getattr(gather, name)()
            else:
                each(gather, name)

    zero = jnp.zeros((1, width), F32)
    biases = [vec_out[0:1, :], zero, vec_out[1:2, :]]
    block = images * full // 2

    for n in range(3):
        cols = slice(n * width, (n + 1) * width)
        g_q[n].finish()

        def project(i, _, cols=cols, bias=biases[n]):
            im = rows_at(i * block, block)
            qkv[im, cols] = (dot(a1o[im, :], bq[:, cols]) + bias).astype(BF)
            return 0

        lax.fori_loop(0, 2, project, 0)
        if n == 0:
            g_q[1].settle()
            g_q[2].settle()
            each(g_t[0], "start")
    wq_copy = pltpu.make_async_copy(bq, wq_out, out_sem.at[2])
    wq_copy.start()
    qkv_copy = pltpu.make_async_copy(qkv, qkv_out, out_sem.at[3])
    qkv_copy.start()
    a1_copy.wait()

    low_half = lax.broadcasted_iota(jnp.int32, (full, 128), 1) < HEAD_DIM
    key_bias = jnp.where(lax.broadcasted_iota(jnp.int32, (1, full), 1) < length, 0.0, -1e30).astype(F32)
    ones = jnp.ones((full, 128), BF)
    per_col = HEADS // 3

    def keep(i, buf):
        return [
            pltpu.make_async_copy(
                buf.at[0 : per_col * full, n * 256 : (n + 1) * 256],
                p_out.at[rows_at((i * 3 + n) * per_col * full, per_col * full), :],
                p_sem.at[lax.rem(i, 2), n],
            )
            for n in range(3)
        ]

    def attend(i, buf):
        @pl.when(i >= 2)
        def _():
            for copy in keep(i - 2, buf):
                copy.wait()

        when(i, 0, g_o.pass_on)
        when(i, 1, lambda: each(g_t[1], "start"))
        when(i, 2, g_o.settle, lambda: each(g_t[0], "pass_on"))
        when(i, 5, lambda: each(g_t[0], "settle"), lambda: each(g_t[1], "pass_on"), lambda: each(g_t[2:], "start"))
        im = rows_at(i * full, full)
        for p in range(HEADS // 2):
            col = p * 128
            q = qkv[im, col : col + 128] * jnp.asarray(HEAD_DIM**-0.5, BF)
            k = qkv[im, col + width : col + width + 128]
            v = jnp.concatenate([qkv[im, col + 2 * width : col + 2 * width + 128], ones], axis=1)
            heads = []
            for hd in range(2):
                mine = low_half if hd == 0 else ~low_half
                s = dot_t(jnp.where(mine, q, jnp.zeros_like(q)), k) + key_bias
                e = jnp.exp(s - jnp.max(s, -1, keepdims=True))
                both = dot(e.astype(BF), v)
                scale = 1.0 / both[:, 128:]
                heads.append(both[:, :128] * scale)
                wide = jnp.concatenate([scale, scale[:, : full - 128]], 1)
                hd_all = 2 * p + hd
                place = (hd_all % per_col * full, hd_all // per_col * 256)
                buf[place[0] : place[0] + full, place[1] : place[1] + full] = (e * wide).astype(BF)
            a1o[im, col : col + 128] = jnp.where(low_half, heads[0], heads[1]).astype(BF)
        for copy in keep(i, buf):
            copy.start()

    def attend_two(j, _):
        attend(2 * j, xs)
        attend(2 * j + 1, cs)
        return 0

    lax.fori_loop(0, images // 2, attend_two, 0)
    o_copy = pltpu.make_async_copy(a1o, o_out, out_sem.at[4])
    o_copy.start()
    g_o.finish()
    wo_copy = pltpu.make_async_copy(bo, wo_out, out_sem.at[5])
    wo_copy.start()
    qkv_copy.wait()

    def middle(i, _):
        im = rows_at(i * block, block)
        hidden = h[im, :] + dot(a1o[im, :], bo[...]) + vec_out[2:3, :]
        h[im, :] = hidden
        normed, _r = normalize(hidden)
        qkv[im, 0:width] = (normed * vec_out[6:7, :] + vec_out[7:8, :]).astype(BF)
        da[im, :] = jnp.zeros((block, width), F32)
        return 0

    lax.fori_loop(0, 2, middle, 0)
    a2_copy = pltpu.make_async_copy(qkv.at[:, 0:width], a2_out, out_sem.at[6])
    h_copy = pltpu.make_async_copy(h, h_out, out_sem.at[7])
    a2_copy.start()
    h_copy.start()
    a2t[0:width, :] = qkv[:, 0:width].T
    a2t[width:, :] = jnp.ones_like(a2t[width:, :])
    each(g_t[1], "settle")
    each(g_t[2:], "pass_on")
    each([g_u2, g_d2], "start")

    for i in (images - 2, images - 1):
        for copy in keep(i, (xs, cs)[i % 2]):
            copy.wait()
    bias = jnp.concatenate([unit_bias(vec_out, ng, share, t * 128, 128) for t in range(tiles)], 1)
    slots = [(ref, n * width) for ref in (xs, cs) for n in range(2)]
    d1_copy = pltpu.make_async_copy(bd1, d1_out, out_sem.at[8])
    act_s = qkv.at[:, width : width + ft]
    act_copies = [
        pltpu.make_async_copy(act_s, act_out.at[:, ct * ft : (ct + 1) * ft], a_sem.at[ct]) for ct in range(tiles * per_gather)
    ]
    da_copy = pltpu.make_async_copy(da, da_out, out_sem.at[9])
    pending = []
    for ct in range(tiles * per_gather):
        t, sub = divmod(ct, per_gather)
        if sub == 0:
            each(g_t[t], "finish")
        if ct >= 2:
            for copy in pending[2 * per * (ct - 2) : 2 * per * (ct - 1)]:
                copy.wait()
        gd_slot, gu_slot = [ref.at[start : start + width] for ref, start in slots[2 * (ct % 2) : 2 * (ct % 2) + 2]]
        gd_slot, gu_slot = gd_slot.at[0:ft], gu_slot.at[:, 0:ft]
        hooks = [act_copies[ct].start]
        if ct:
            act_copies[ct - 1].wait()
        if ct == 0:
            hooks.append(lambda: each(g_t[2:], "settle"))
        if ct == tiles * per_gather - 2:
            hooks.append(lambda: each([g_u2, g_d2], "pass_on"))
        if ct == tiles * per_gather - 1:
            hooks += [d1_copy.start, da_copy.start, lambda: each([g_u2, g_d2], "settle")]
        mlp_tile(
            ct, ft, 2, qkv.at[:, 0:width], a2t, dm, bu1, bd1, bias, da, act_s, qkv.at[:, 2 * width : 2 * width + ft], gd_slot, gu_slot, gbu,
            hooks,
        )
        for i in range(per):
            start = (sub * per + i) * one + t * 128
            units, part = slice(start, start + 128), slice(i * 128, (i + 1) * 128)
            pending.append(pltpu.make_async_copy(gd_slot.at[part, :], gd_out.at[units, :], g_sem.at[0, ct, i]))
            pending.append(pltpu.make_async_copy(gu_slot.at[:, part], gu_out.at[:, units], g_sem.at[1, ct, i]))
            gbu_out[:, units] = gbu[:, part]
        for copy in pending[-2 * per :]:
            copy.start()
    g_u2.finish()
    g_d2.finish()
    u2_copy = pltpu.make_async_copy(bu2, u2_out, out_sem.at[10])
    d2_copy = pltpu.make_async_copy(bd2, d2_out, out_sem.at[11])
    u2_copy.start()
    d2_copy.start()
    for gather in gathers:
        gather.close()
    for copy in pending[-4 * per :] + [dm_copy, wq_copy, o_copy, wo_copy, a2_copy, h_copy, d1_copy, da_copy, act_copies[-1], u2_copy, d2_copy]:
        copy.wait()


def unit_bias(vec_ref, ng, share, start, size):
    width = vec_ref.shape[1]
    parts = []
    for m in range(ng):
        row, col = divmod(m * share + start, width)
        parts.append(vec_ref[8 + row : 9 + row, col : col + size])
    return jnp.concatenate(parts, 1)


def run_forward(ng, nr, full, tokens, cotangent, w_qkv, w_out, w_up, w_down, vectors):
    images, length, width = tokens.shape
    ff = w_up.shape[1]
    share, one, two = strips(ng, ff)
    f1, f2 = ng * one, ng * two
    any_spec = pl.BlockSpec(memory_space=pl.ANY)
    vmem = pl.BlockSpec(memory_space=pltpu.VMEM)
    dma = pltpu.SemaphoreType.DMA
    rows_like = (images * full, width)
    flat = (length * images, width)
    ft = 512

    def bf(*shape):
        return jax.ShapeDtypeStruct(shape, BF)

    def f32(*shape):
        return jax.ShapeDtypeStruct(shape, F32)

    n_loads = w_qkv.shape[1] // width + ff // width + 2
    return pl.pallas_call(
        functools.partial(forward, ng, nr // 2, length),
        out_shape=(
            bf(width, 3 * width), bf(width, width), bf(width, f2), bf(f2, width), f32(vectors.shape[0], width),
            bf(*rows_like), bf(images * HEADS * full, 256), bf(images * full, 3 * width), bf(*rows_like), bf(*rows_like), bf(*rows_like),
            f32(*rows_like), bf(images * full, f1), bf(f1, width), f32(*rows_like), bf(f1, width), bf(width, f1), bf(*rows_like), f32(1, f1),
        ),
        in_specs=[any_spec] * 7,
        out_specs=(any_spec,) * 4 + (vmem,) + (any_spec,) * 13 + (vmem,),
        scratch_shapes=[
            pltpu.VMEM(flat, BF),
            pltpu.VMEM(flat, BF),
            pltpu.VMEM(rows_like, F32),
            pltpu.VMEM(rows_like, F32),
            pltpu.VMEM(rows_like, F32),
            pltpu.VMEM((width, 3 * width), BF),
            pltpu.VMEM((width, width), BF),
            pltpu.VMEM((width, f1), BF),
            pltpu.VMEM((f1, width), BF),
            pltpu.VMEM((width, f2), BF),
            pltpu.VMEM((f2, width), BF),
            pltpu.VMEM(vectors.shape, F32),
            pltpu.VMEM((ng,) + vectors.shape, F32),
            pltpu.VMEM(rows_like, BF),
            pltpu.VMEM((images * full, 3 * width), BF),
            pltpu.VMEM(rows_like, BF),
            pltpu.VMEM((width + 16, images * full), BF),
            pltpu.VMEM((width // 128, images * full, 128), F32),
            pltpu.VMEM((1, ft), F32),
            dma((n_loads,)),
            dma,
            dma((2,)),
            dma((ng - 1,)),
            dma((ng - 1,)),
            dma((13,)),
            dma((2, f1 // ft, ft // 128)),
            dma((f1 // ft,)),
            dma((2, 3)),
        ]
        + gather_sems(ng) * (3 + w_qkv.shape[1] // width + 2 * (f1 // (ng * 128))),
        compiler_params=params(64, collective_id=0, has_side_effects=True),
    )(
        tokens.transpose(1, 0, 2).reshape(flat), cotangent.transpose(1, 0, 2).reshape(flat),
        w_qkv, w_out, w_up, w_down, vectors,
    )


class Early:
    def __init__(self, at, src, load, refs):
        self.at, self.src, self.mine = at, src, None
        if load:
            self.mine, refs = refs[0], refs[1:]
        self.rc, self.rx, self.tz, self.m_sem, self.c_send, self.c_recv, self.x_send, self.x_recv = refs[:8]
        self.rest = refs[8:]
        self.half = self.rc.shape[1]
        self.two = at.ng == 4

    def load_copy(self, m):
        start = m * 2 * self.half + self.at.c * self.half
        return pltpu.make_async_copy(self.src.at[rows_at(start, self.half), :], self.mine.at[m], self.m_sem.at[m])

    def core_copy(self, m):
        start = m * 2 * self.half + (1 - self.at.c) * self.half
        return remote(self.src.at[rows_at(start, self.half), :], self.rc.at[m], self.c_send.at[m], self.c_recv.at[m], self.at.sib)

    def group_copy(self, k):
        return remote(self.rc.at[flip(self.at.g, k)], self.rx.at[k - 1], self.x_send.at[k - 1], self.x_recv.at[k - 1], self.at.group(k))

    def rows(self, k):
        return slice(0, self.half // 2) if k == 1 else slice(self.half // 2, self.half)

    def first_copy(self, k, own):
        part = self.rc.at[flip(self.at.g, k if own else 3), self.rows(k), :]
        slot = 2 * (k - 1) + (0 if own else 1)
        return remote(part, self.rx.at[slot], self.x_send.at[slot], self.x_recv.at[slot], self.at.group(k))

    def second_copy(self, k):
        part = self.rc.at[flip(self.at.g, k), self.rows(3 - k), :]
        return remote(part, self.rx.at[3 + k], self.x_send.at[3 + k], self.x_recv.at[3 + k], self.at.group(k))

    def start_core(self):
        for m in range(self.at.ng):
            self.core_copy(m).start()
        if self.mine is not None:
            for m in range(self.at.ng):
                self.load_copy(m).start()

    def start_group(self):
        at, h = self.at, self.half
        for m in range(at.ng):
            self.core_copy(m).wait_recv()
            if self.mine is not None:
                self.load_copy(m).wait()
        order = (3, 1, 2, 0) if self.two else list(range(1, at.ng)) + [0]
        for k in order:
            m = flip(at.g, k)
            mine = self.src[rows_at(m * 2 * h + at.c * h, h), :] if self.mine is None else self.mine[m]
            self.rc[m] = (mine.astype(F32) + self.rc[m].astype(F32)).astype(BF)
            if self.two and k == 3:
                self.first_copy(1, False).start()
                self.first_copy(2, False).start()
            elif self.two and k:
                self.first_copy(k, True).start()
            elif k:
                self.group_copy(k).start()

    def turn_group(self):
        if not self.two:
            return
        for k in (1, 2):
            self.first_copy(k, False).wait_recv()
            m, sl = flip(self.at.g, 3 - k), self.rows(k)
            self.rc[m, sl, :] = (self.rc[m, sl, :].astype(F32) + self.rx[2 * (k - 1) + 1].astype(F32)).astype(BF)
            self.second_copy(3 - k).start()

    def collect(self):
        at = self.at
        if self.two:
            parts = []
            for k in (1, 2):
                self.first_copy(k, True).wait_recv()
                self.second_copy(3 - k).wait_recv()
                part = self.rc[at.g, self.rows(k), :].astype(F32) + self.rx[2 * (k - 1)].astype(F32)
                parts.append(part + self.rx[3 + 3 - k].astype(F32))
            total = jnp.concatenate(parts, 0)
        else:
            for k in range(1, at.ng):
                self.group_copy(k).wait_recv()
            total = self.rc[at.g].astype(F32)
            for k in range(at.ng - 1):
                total = total + self.rx[k].astype(F32)
        p = self.half // at.nz
        for j in range(at.nz):
            self.tz[j] = total[j * p : (j + 1) * p].astype(BF)

    def close(self):
        if self.two:
            for k in (1, 2):
                self.first_copy(k, True).wait_send()
                self.first_copy(k, False).wait_send()
                self.second_copy(k).wait_send()
        else:
            for k in range(1, self.at.ng):
                self.group_copy(k).wait_send()
        for m in range(self.at.ng):
            self.core_copy(m).wait_send()


class Late:
    def __init__(self, at, tz, refs, out, begin=0):
        self.at, self.tz, self.out, self.begin = at, tz, out, begin
        self.steps = at.nz.bit_length() - 1
        (self.rz, self.y, self.z_send, self.z_recv, self.a_send, self.a_recv, self.f_send, self.f_recv, self.o_sem) = refs[:9]
        self.rest = refs[9:]

    def bit(self, k):
        return lax.rem(lax.div(self.at.z, 2**k), 2)

    def base(self, k, size):
        start = 0
        for i in range(k):
            start = start + self.bit(i) * (self.at.nz // 2 ** (i + 1))
        return start + self.bit(k) * size, start + (1 - self.bit(k)) * size

    def half_copy(self, k):
        size = self.at.nz // 2 ** (k + 1)
        landing = self.rz.at[pl.ds(size - 1, size)]
        return remote(self.tz.at[pl.ds(self.base(k, size)[1], size)], landing, self.z_send.at[k], self.z_recv.at[k], self.at.chip(2**k))

    def place(self, mask):
        start = 0
        for i in range(self.steps):
            b = 1 - self.bit(i) if mask & 2**i else self.bit(i)
            start = start + b * (self.at.nz // 2 ** (i + 1))
        return start

    def back_copy(self, k, mask):
        place = self.out.at[self.at.c, self.place(mask)]
        slot = (mask ^ 2**k) - 1
        return remote(self.y if mask == 0 else place, place, self.a_send.at[slot], self.a_recv.at[slot], self.at.chip(2**k))

    def back_in(self, mask):
        place = self.out.at[self.at.c, self.place(mask)]
        return remote(self.y, place, self.a_send.at[mask - 1], self.a_recv.at[mask - 1], self.at.chip(mask))

    def last_copy(self, mask, mine=True):
        place = self.out.at[self.at.c if mine else 1 - self.at.c, self.place(mask)]
        return remote(self.y if mask == 0 else place, place, self.f_send.at[mask], self.f_recv.at[mask], self.at.sib)

    def keep_copy(self):
        return pltpu.make_async_copy(self.y, self.out.at[self.at.c, self.place(0)], self.o_sem)

    def start_halves(self):
        self.half_copy(self.begin).start()

    def add_half(self, k, go_on=True):
        size = self.at.nz // 2 ** (k + 1)
        self.half_copy(k).wait_recv()
        kept = self.base(k, size)[0]
        for i in range(size):
            total = (self.tz[kept + i].astype(F32) + self.rz[size - 1 + i].astype(F32)).astype(BF)
            if size == 1:
                self.y[...] = total
            else:
                self.tz[kept + i] = total
        if size > 1:
            if go_on:
                self.half_copy(k + 1).start()
            return
        for j in reversed(range(self.steps)):
            self.back_copy(j, 0).start()
        self.last_copy(0).start()
        self.keep_copy().start()

    def spread(self, k):
        for mask in range(0, self.at.nz, 2 ** (k + 1)):
            got = mask ^ 2**k
            self.back_in(got).wait_recv()
            for j in reversed(range(k)):
                self.back_copy(j, got).start()
            self.last_copy(got).start()

    def stages(self):
        out = [self.start_halves]
        out += [functools.partial(self.add_half, k) for k in range(self.begin, self.steps)]
        return out + [functools.partial(self.spread, k) for k in reversed(range(self.steps))]

    def finish(self):
        at = self.at
        for mask in range(at.nz):
            self.last_copy(mask, mine=False).wait_recv()
            self.last_copy(mask).wait_send()
        for k in range(self.steps):
            if k >= self.begin:
                self.half_copy(k).wait_send()
            for mask in range(0, at.nz, 2 ** (k + 1)):
                self.back_copy(k, mask).wait_send()
        self.keep_copy().wait()


class LateDirect:
    def __init__(self, at, tz, refs, out):
        self.at, self.tz, self.out = at, tz, out
        (self.rz, self.y, self.z_send, self.z_recv, self.a_send, self.a_recv, self.f_send, self.f_recv, self.o_sem) = refs[:9]
        self.rest = refs[9:]

    def chip_copy(self, j):
        return remote(self.tz.at[flip(self.at.z, j)], self.rz.at[j - 1], self.z_send.at[j - 1], self.z_recv.at[j - 1], self.at.chip(j))

    def back_copy(self, j, mine=True):
        place = self.out.at[self.at.c, self.at.z if mine else flip(self.at.z, j)]
        return remote(self.y, place, self.a_send.at[j - 1], self.a_recv.at[j - 1], self.at.chip(j))

    def last_copy(self, j, mine=True):
        place = self.out.at[self.at.c if mine else 1 - self.at.c, flip(self.at.z, j)]
        return remote(self.y if j == 0 else place, place, self.f_send.at[j], self.f_recv.at[j], self.at.sib)

    def keep_copy(self):
        return pltpu.make_async_copy(self.y, self.out.at[self.at.c, self.at.z], self.o_sem)

    def start_halves(self):
        for j in reversed(range(1, self.at.nz)):
            self.chip_copy(j).start()

    def start_back(self):
        at = self.at
        for j in range(1, at.nz):
            self.chip_copy(j).wait_recv()
        total = self.tz[at.z].astype(F32)
        for j in range(at.nz - 1):
            total = total + self.rz[j].astype(F32)
        self.y[...] = total.astype(BF)
        for j in reversed(range(1, at.nz)):
            self.back_copy(j).start()
        self.last_copy(0).start()
        self.keep_copy().start()

    def start_last(self):
        for j in range(1, self.at.nz):
            self.back_copy(j, mine=False).wait_recv()
            self.last_copy(j).start()

    def stages(self):
        return [self.start_halves, self.start_back, self.start_last]

    def finish(self):
        at = self.at
        for j in range(at.nz):
            self.last_copy(j, mine=False).wait_recv()
            self.last_copy(j).wait_send()
        for j in range(1, at.nz):
            self.back_copy(j).wait_send()
            self.chip_copy(j).wait_send()
        self.keep_copy().wait()


def early_scratch(ng, nz, half, cols, load):
    dma = pltpu.SemaphoreType.DMA
    landing, n = ((6, half // 2, cols), 6) if ng == 4 else ((ng - 1, half, cols), ng - 1)
    shapes = [pltpu.VMEM((ng, half, cols), BF)] if load else []
    shapes += [pltpu.VMEM((ng, half, cols), BF), pltpu.VMEM(landing, BF), pltpu.VMEM((nz, half // nz, cols), BF)]
    return shapes + [dma((m,)) for m in (ng, ng, ng, n, n)]


def late_scratch(nz, half, cols):
    dma = pltpu.SemaphoreType.DMA
    p = half // nz
    steps = nz.bit_length() - 1
    shapes = [pltpu.VMEM((nz - 1, p, cols), BF), pltpu.VMEM((p, cols), BF)]
    for m in (nz - 1, nz - 1, nz):
        shapes += [dma((m,)), dma((m,))]
    return shapes + [dma]


def turn(ng, nz, *refs):
    at = Places(ng, nz)
    (a2_hbm, dm_hbm, h_hbm, da_hbm, o_hbm, wo_hbm, wu_hbm, wd_hbm, gd1_hbm, gu1_hbm, vec_ref,
     act_out, dh_out, do_out, gd_out, gu_out, go_out, gbu_out, sum_out, td_out, tu_out,
     a2, a2t, dm, h, da, o, wo, wu, wd, work, go_s, slot_a, slot_b, slot_c, slot_d,
     blk_sem, big_sem, out_sem, g_sem, a_sem) = refs[:41]
    early_d = Early(at, gd1_hbm, True, refs[41:])
    early_u = Early(at, gu1_hbm, True, early_d.rest)
    late_d = Late(at, early_d.tz, early_u.rest, None)
    late_u = Late(at, early_u.tz, late_d.rest, None)
    rows, width = h.shape
    half = rows // 2

    def block_copy(j, i):
        src, dst = ((a2_hbm, a2), (dm_hbm, dm), (da_hbm, da))[j]
        part = rows_at(i * half, half)
        return pltpu.make_async_copy(src.at[part, :], dst.at[part, :], blk_sem.at[j, i])

    def big_copy(j):
        src, dst = ((wu_hbm, wu), (wd_hbm, wd), (h_hbm, h), (o_hbm, o), (wo_hbm, wo))[j]
        return pltpu.make_async_copy(src, dst, big_sem.at[j])

    block_copy(0, 0).start()
    big_copy(0).start()
    block_copy(1, 0).start()
    big_copy(1).start()
    for j, i in ((0, 1), (1, 1), (2, 0), (2, 1)):
        block_copy(j, i).start()
    for j in range(2, 5):
        big_copy(j).start()
    at.greet(True, True)
    early_d.start_core()
    early_u.start_core()
    for j, i in ((0, 0), (1, 0), (0, 1), (1, 1)):
        block_copy(j, i).wait()
    for j in range(2):
        big_copy(j).wait()
    a2t[0:width, :] = a2[...].T
    a2t[width:, :] = jnp.ones_like(a2t[width:, :])

    ff = wu.shape[1]
    share = ff // ng + gd1_hbm.shape[0] // ng
    bias = unit_bias(vec_ref, ng, share, gd1_hbm.shape[0] // ng, ff // ng)
    ft = tile_of(ff)
    tiles = ff // ft
    slots = ((slot_a, slot_b), (slot_c, slot_d))
    pending = []

    def sums_here(i):
        block_copy(2, i).wait()

        @pl.when(i == 1)
        def _():
            early_d.start_group()

    def sums_there(i):
        @pl.when(i == 1)
        def _():
            early_d.turn_group()

    act_copies = [
        pltpu.make_async_copy(work.at[:, 0:ft], act_out.at[:, t * ft : (t + 1) * ft], a_sem.at[t]) for t in range(tiles)
    ]
    for t in range(tiles):
        if t:
            act_copies[t - 1].wait()
        if t >= 2:
            for copy in pending[2 * (t - 2) : 2 * (t - 1)]:
                copy.wait()
        gd_slot, gu_slot = slots[t % 2][0].at[0:ft], slots[t % 2][1].at[:, 0:ft]
        mlp_tile(
            t, ft, 2, a2, a2t, dm, wu, wd, bias, da, work.at[:, 0:width], work.at[:, width : 2 * width],
            gd_slot, gu_slot, gbu_out.at[:, t * ft : (t + 1) * ft],
            (act_copies[t].start,) + ((early_u.start_group,) if t == 0 else (early_u.turn_group,) if t == 1 else ()),
            sums_here if t == 0 else sums_there if t == 1 else lambda i: None,
        )
        units = slice(t * ft, (t + 1) * ft)
        pending.append(pltpu.make_async_copy(gd_slot, gd_out.at[units, :], g_sem.at[0, t]))
        pending.append(pltpu.make_async_copy(gu_slot, gu_out.at[:, units], g_sem.at[1, t]))
        for copy in pending[-2:]:
            copy.start()

    for j in range(2, 5):
        big_copy(j).wait()
    sum_out[...] = jnp.zeros_like(sum_out)
    early_d.collect()
    late_d.start_halves()

    act_copies[-1].wait()

    def post(b, _):
        @pl.when(b == 1)
        def _():
            early_u.collect()
            late_u.start_halves()

        im = rows_at(b * (rows // 4), rows // 4)
        hidden = h[im, :]
        cot = dm[im, :].astype(F32)
        normed, rstd = normalize(hidden)
        grad = da[im, :]
        dh = cot + norm_back(grad, normed, rstd, vec_ref[6:7, :])
        h[im, :] = dh
        dz = dh.astype(BF)
        work[im, 0:width] = dz
        work[im, width : 2 * width] = dot_t(dz, wo[...]).astype(BF)
        for j, term in enumerate((dz.astype(F32), cot, grad * normed, grad)):
            sum_out[j : j + 1, :] += jnp.sum(term, 0, keepdims=True)
        return 0

    lax.fori_loop(0, 4, post, 0)
    dh_copy = pltpu.make_async_copy(h, dh_out, out_sem.at[0])
    do_copy = pltpu.make_async_copy(work.at[:, width : 2 * width], do_out, out_sem.at[1])
    dh_copy.start()
    do_copy.start()
    go_s[...] = dot(o[...].T, work[:, 0:width]).astype(BF)
    go_copy = pltpu.make_async_copy(go_s, go_out, out_sem.at[2])
    go_copy.start()
    late_d.add_half(0, False)
    td_copy = pltpu.make_async_copy(early_d.tz, td_out, out_sem.at[3])
    td_copy.start()
    late_u.add_half(0, False)
    tu_copy = pltpu.make_async_copy(early_u.tz, tu_out, out_sem.at[4])
    tu_copy.start()
    early_d.close()
    early_u.close()
    late_d.half_copy(0).wait_send()
    late_u.half_copy(0).wait_send()
    for copy in pending[-4:] + [dh_copy, do_copy, go_copy, td_copy, tu_copy]:
        copy.wait()


def run_turn(ng, nr, a2, dm, h, da, o, wo, wu, wd, gd1, gu1, vecs):
    nz = nr // 2
    rows, width = h.shape
    ff = wu.shape[1]
    ft = tile_of(ff)
    any_spec = pl.BlockSpec(memory_space=pl.ANY)
    vmem = pl.BlockSpec(memory_space=pltpu.VMEM)
    dma = pltpu.SemaphoreType.DMA
    sizes = [(g.shape[0] // ng // 2, g.shape[1]) for g in (gd1, gu1)]

    def bf(*shape):
        return jax.ShapeDtypeStruct(shape, BF)

    def f32(*shape):
        return jax.ShapeDtypeStruct(shape, F32)

    scratch = [
        pltpu.VMEM((rows, width), BF),
        pltpu.VMEM((width + 16, rows), BF),
        pltpu.VMEM((rows, width), BF),
        pltpu.VMEM((rows, width), F32),
        pltpu.VMEM((rows, width), F32),
        pltpu.VMEM((rows, width), BF),
        pltpu.VMEM((width, width), BF),
        pltpu.VMEM(wu.shape, BF),
        pltpu.VMEM(wd.shape, BF),
        pltpu.VMEM((rows, 2 * width), BF),
        pltpu.VMEM((width, width), BF),
        pltpu.VMEM((ft, width), BF),
        pltpu.VMEM((width, ft), BF),
        pltpu.VMEM((ft, width), BF),
        pltpu.VMEM((width, ft), BF),
        dma((3, 2)),
        dma((5,)),
        dma((5,)),
        dma((2, ff // ft)),
        dma((ff // ft,)),
    ]
    for hh, w in sizes:
        scratch += early_scratch(ng, nz, hh, w, True)
    for hh, w in sizes:
        scratch += late_scratch(nz, hh, w)
    return pl.pallas_call(
        functools.partial(turn, ng, nz),
        out_shape=(
            bf(rows, ff), f32(rows, width), bf(rows, width), bf(ff, width), bf(width, ff), bf(width, width),
            f32(1, ff), f32(8, width),
        ) + tuple(bf(nz, hh // nz, w) for hh, w in sizes),
        in_specs=[any_spec] * 10 + [vmem],
        out_specs=(any_spec,) * 6 + (vmem, vmem, any_spec, any_spec),
        scratch_shapes=scratch,
        compiler_params=params(64, collective_id=1, has_side_effects=True),
    )(a2, dm, h, da, o, wo, wu, wd, gd1, gu1, vecs)


def vector_sum(at, v_s, landed, sems):
    v_g, v_z, v_c = landed
    g_send, g_recv, z_send, z_recv, c_send, c_recv = sems

    def copies(level):
        if level == 0:
            return [remote(v_s.at[0], v_g.at[k - 1], g_send.at[k - 1], g_recv.at[k - 1], at.group(k)) for k in range(1, at.ng)]
        if level == 1:
            return [remote(v_s.at[1], v_z.at[j - 1], z_send.at[j - 1], z_recv.at[j - 1], at.chip(j)) for j in range(1, at.nz)]
        return [remote(v_s.at[2], v_c.at[0], c_send.at[0], c_recv.at[0], at.sib)]

    def start(level):
        for copy in copies(level):
            copy.start()

    def add(level):
        for copy in copies(level):
            copy.wait()
        total = v_s[level]
        buf = (v_g, v_z, v_c)[level]
        for j in range(buf.shape[0]):
            total = total + buf[j]
        v_s[level + 1] = total

    return start, add


def vector_scratch(ng, nz, shape):
    dma = pltpu.SemaphoreType.DMA
    shapes = [pltpu.VMEM((4,) + shape, F32)]
    shapes += [pltpu.VMEM((m,) + shape, F32) for m in (ng - 1, nz - 1, 1)]
    for m in (ng - 1, nz - 1, 1):
        shapes += [dma((m,)), dma((m,))]
    return shapes


PAIRS_A, PAIRS_B = (0, 1, 2, 3), (4, 5)


def act_pieces(n1, n2, width):
    out = []
    for j in range((n1 + n2) // width):
        cuts = [j * width] + ([n1] if j * width < n1 < (j + 1) * width else []) + [(j + 1) * width]
        out += [(j, start, stop) for start, stop in zip(cuts, cuts[1:])]
    return out


def plan(early, late):
    steps = [chunk.stages() for chunk in late[:2]]
    for first, second in zip(early, late[2:]):

        def join(first=first, second=second):
            first.collect()
            second.start_halves()

        steps.append([first.start_core, first.start_group, first.turn_group, join] + second.stages()[1:])
    return steps


def backward(ng, nz, length, *refs):
    at = Places(ng, nz)
    (gd_hbm, gu_hbm, go_hbm, td1_hbm, tu1_hbm, p_hbm, qkv_hbm, do_hbm, o_hbm, a1_hbm, wq_hbm, x_hbm, dh_hbm, h_hbm, act1_hbm, act2_hbm, d1_hbm, d2_hbm, vec_ref, sum_ref, gbu1_ref, gbu2_ref,
     ig_out, out_out, td1_out, tu1_out, td_out, tu_out, to_out, ta_out, tb_out, vec_out,
     qkv_s, do_s, o_s, a1_s, a1t, wq_s, x_s, dh_s, p_s, inner_s, ga_s, gb_s, w_s, stage, im_sem, big_sem, ig_sem, tz_d1, tz_u1, t_sem, h_sem, act_sem, down_sem, p_sem) = refs[:56]
    rest = refs[56:]
    early, late = [], []
    for src, load in ((gd_hbm, True), (gu_hbm, True), (go_hbm, True), (ga_s, False), (gb_s, False)):
        early.append(Early(at, src, load, rest))
        rest = early[-1].rest
    pieces = [tz_d1, tz_u1] + [e.tz for e in early]
    for tz, total in zip(pieces, (td1_out, tu1_out, td_out, tu_out, to_out, ta_out, tb_out)):
        kind = LateDirect if len(late) >= 5 else Late
        late.append(kind(at, tz, rest, total, *((1,) if len(late) < 2 else ())))
        rest = late[-1].rest
    v_s = rest[0]
    v_start, v_add = vector_sum(at, v_s, rest[1:4], rest[4:10])

    images = ig_sem.shape[0] // 2
    rows, width = do_s.shape
    full = rows // images
    scale = HEAD_DIM**-0.5

    def image_copies(i):
        return [
            pltpu.make_async_copy(src.at[rows_at(i * full, full), :], dst.at[rows_at(i * full, full), :], im_sem.at[j, i])
            for j, (src, dst) in enumerate(((qkv_hbm, qkv_s), (do_hbm, do_s), (o_hbm, o_s)))
        ]

    def big_copy(j):
        src, dst = ((a1_hbm, a1_s), (wq_hbm, wq_s), (x_hbm, x_s), (dh_hbm, dh_s))[j]
        return pltpu.make_async_copy(src, dst, big_sem.at[j])

    def probs_copy(i, pairs):
        count = 2 * len(pairs) * full
        src = p_hbm.at[rows_at((i * HEADS + 2 * pairs[0]) * full, count), :]
        slot = lax.rem(i, 2)
        return pltpu.make_async_copy(src, p_s.at[slot, 0:count, :], p_sem.at[slot])

    tz_copies = [pltpu.make_async_copy(td1_hbm, tz_d1, t_sem.at[0]), pltpu.make_async_copy(tu1_hbm, tz_u1, t_sem.at[1])]
    for copy in tz_copies:
        copy.start()
    for copy in image_copies(0) + image_copies(1):
        copy.start()
    probs_copy(0, PAIRS_A).start()
    at.greet(True, True)
    d1, u1, d2, u2, go, ga, gb = (iter(steps) for steps in plan(early, late))

    def advance(*chunks):
        for chunk in chunks:
            next(chunk)()

    advance(d2)
    for copy, chunk in zip(tz_copies, (d1, u1)):
        copy.wait()
        advance(chunk)
    advance(u2, go)

    low_half = lax.broadcasted_iota(jnp.int32, (full, 128), 1) < HEAD_DIM
    pick = lax.broadcasted_iota(jnp.int32, (width, 128), 0) // HEAD_DIM == lax.broadcasted_iota(jnp.int32, (width, 128), 1)
    pick = jnp.where(pick, 1.0, 0.0).astype(BF)

    def attend_back(i, pairs):
        @pl.when(i + 1 < images)
        def _():
            probs_copy(i + 1, pairs).start()

        im = rows_at(i * full, full)
        probs_copy(i, pairs).wait()
        slot = lax.rem(i, 2)
        for p in pairs:
            col = p * 128
            q = qkv_s[im, col : col + 128] * jnp.asarray(scale, BF)
            k = qkv_s[im, col + width : col + width + 128]
            v = qkv_s[im, col + 2 * width : col + 2 * width + 128]
            do = do_s[im, col : col + 128]
            zero = jnp.zeros_like(q)
            dom = jnp.concatenate([jnp.where(low_half, do, zero), jnp.where(low_half, zero, do)], 0)
            qm = jnp.concatenate([jnp.where(low_half, q, zero), jnp.where(low_half, zero, q)], 0)
            start = 2 * (p - pairs[0]) * full
            probs = p_s[slot, start : start + 2 * full, 0:full]
            inner = jnp.concatenate([inner_s[im, 2 * p : 2 * p + 1], inner_s[im, 2 * p + 1 : 2 * p + 2]], 0)
            ds = (probs.astype(F32) * (dot_t(dom, v) - inner)).astype(BF)
            dq = dot(ds, k)
            qkv_s[im, col : col + 128] = (jnp.where(low_half, dq[:full], dq[full:]) * scale).astype(BF)
            qkv_s[im, col + width : col + width + 128] = dot_tn(ds, qm).astype(BF)
            qkv_s[im, col + 2 * width : col + 2 * width + 128] = dot_tn(probs, dom).astype(BF)

    half_rows = rows // 2
    act_bufs = (do_s, o_s, a1_s, x_s)

    def act_copies(chunk):
        n1, n2 = d1_hbm.shape[0], d2_hbm.shape[0]
        out = []
        for n, (j, start, stop) in enumerate(act_pieces(n1, n2, width)):
            if j == chunk:
                src, first = (act1_hbm, start) if start < n1 else (act2_hbm, start - n1)
                col = start - j * width
                src, dst = src.at[:, first : first + stop - start], act_bufs[j].at[:, col : col + stop - start]
                out.append(pltpu.make_async_copy(src, dst, act_sem.at[n]))
        return out

    down_bufs = [w_s.at[0:width, :], w_s.at[width : 2 * width, :], a1t.at[0:width, 0:width], a1t.at[0:width, width : 2 * width]]

    def down_copies(chunk):
        n1, n2 = d1_hbm.shape[0], d2_hbm.shape[0]
        out = []
        for n, (j, start, stop) in enumerate(act_pieces(n1, n2, width)):
            if j == chunk:
                src, first = (d1_hbm, start) if start < n1 else (d2_hbm, start - n1)
                row = start - j * width
                src, dst = src.at[first : first + stop - start, :], down_bufs[j].at[row : row + stop - start, :]
                out.append(pltpu.make_async_copy(src, dst, down_sem.at[n]))
        return out

    def down_start(chunk):
        for copy in down_copies(chunk):
            copy.start()

    def act_start(bufs, first):
        for j in range(first, first + len(bufs)):
            for copy in act_copies(j):
                copy.start()

    def act_wait(chunk):
        for copy in act_copies(chunk) + down_copies(chunk):
            copy.wait()

    def when(i, index, *chunks):
        @pl.when(i == index)
        def _():
            advance(*chunks)

    def first_pass(i, _):
        for copy in image_copies(i):
            copy.wait()

        @pl.when(i + 2 < images)
        def _():
            for copy in image_copies(i + 2):
                copy.start()

        when(i, 2, d2)
        when(i, 3, u2, d1)
        when(i, 4, go, u1)
        when(i, 6, d2, d1)
        when(i, 7, u1)

        @pl.when(i == 3)
        def _():
            for j in range(4):
                big_copy(j).start()
            for j in range(2):
                down_start(j)

        im = rows_at(i * full, full)
        prod = do_s[im, :].astype(F32) * o_s[im, :].astype(F32)
        high = prod.astype(BF)
        inner_s[im, :] = dot(high, pick) + dot((prod - high.astype(F32)).astype(BF), pick)
        attend_back(i, PAIRS_A)
        return 0

    def weight_grad(pairs, g_ref, steps=()):
        start, stop = pairs[0] * 128, pairs[-1] * 128 + 128
        wide = stop - start
        for n in range(3):
            if n == 1:
                advance(*steps)
            dp = qkv_s[:, n * width + start : n * width + stop]
            both = dot(a1t[...], dp)
            g_ref[:, n * wide : (n + 1) * wide] = both[0:width].astype(BF)
            if n != 1:
                row = 0 if n == 0 else 1
                v_s[0, row : row + 1, start:stop] = both[width : width + 1]

    lax.fori_loop(0, images, first_pass, 0)
    probs_copy(0, PAIRS_B).start()
    big_copy(0).wait()
    a1t[0:width, :] = a1_s[...].T
    a1t[width:, :] = jnp.ones_like(a1t[width:, :])
    weight_grad(PAIRS_A, ga_s, (d2, u2))
    advance(ga, d2, go, d1, u1)

    def second_pass(i, _):
        when(i, 1, u2)
        when(i, 3, ga, go)
        when(i, 4, d2)
        when(i, 6, u2)
        when(i, 7, go)
        attend_back(i, PAIRS_B)
        return 0

    lax.fori_loop(0, images, second_pass, 0)
    weight_grad(PAIRS_B, gb_s)
    advance(gb, ga, d2, u2)

    for j in range(1, 4):
        big_copy(j).wait()
    act_start(act_bufs[:3], 0)
    for j in range(2, len(act_bufs)):
        down_start(j)
    v_s[0, 2:4, :] = sum_ref[0:2, :]
    v_s[0, 4:6, :] = jnp.zeros((2, width), F32)
    v_s[0, 6:8, :] = sum_ref[2:4, :]
    one, two = gbu1_ref.shape[1] // ng, gbu2_ref.shape[1] // ng
    for m in range(ng):
        row, col = divmod(m * (one + two), width)
        v_s[0, 8 + row : 9 + row, col : col + one] = gbu1_ref[0:1, m * one : (m + 1) * one]
        v_s[0, 8 + row : 9 + row, col + one : col + one + two] = gbu2_ref[0:1, m * two : (m + 1) * two]

    def input_copy(i):
        return pltpu.make_async_copy(stage.at[i], ig_out.at[i], ig_sem.at[i])

    def output_copy(i):
        return pltpu.make_async_copy(stage.at[i], out_out.at[i], ig_sem.at[images + i])

    h_copy = pltpu.make_async_copy(h_hbm, dh_s, h_sem.at[0])

    def input_pass(b, _):
        first = b * 2
        when(b, 0, go)
        when(b, 1, gb, d2)
        when(b, 2, ga, u2)
        when(b, 3, gb, go)
        im = rows_at(first * full, 2 * full)
        da = dot_t(qkv_s[im, :], wq_s[...])
        normed, rstd = normalize(x_s[im, :].astype(F32))
        grad = dh_s[im, :] + norm_back(da, normed, rstd, vec_ref[4:5, :])
        grad = grad.astype(BF).reshape(2, full, width)
        for i in range(2):
            stage[first + i] = grad[i, :length, :]
            input_copy(first + i).start()
        v_s[0, 4:5, :] += jnp.sum(da * normed, 0, keepdims=True)
        v_s[0, 5:6, :] += jnp.sum(da, 0, keepdims=True)
        return 0

    lax.fori_loop(0, images // 2, input_pass, 0)
    h_copy.start()
    act_start(act_bufs[3:], 3)
    for i in range(images):
        input_copy(i).wait()

    def output_pass(b, steps):
        im = rows_at(b * half_rows, half_rows)
        for j, buf in enumerate(act_bufs):
            dh_s[im, :] += dot(buf[im, :], down_bufs[j][...])
            if j == 1:
                advance(*steps)
        for i in range(images // 2):
            at_image = b * (images // 2) + i
            image = dh_s[rows_at(at_image * full, full), :] + vec_ref[3:4, :]
            stage[at_image] = image.astype(BF)[:length]
            output_copy(at_image).start()

    v_start(0)
    advance(gb)
    for j in range(len(act_bufs)):
        act_wait(j)
    h_copy.wait()
    output_pass(0, (ga, u2))
    v_add(0)
    v_start(1)
    advance(gb)
    output_pass(1, (go,))
    v_add(1)
    v_start(2)
    advance(ga)
    advance(gb)
    v_add(2)
    vec_out[...] = v_s[3]
    for chunk in (d1, u1, d2, u2, go, ga, gb):
        for step in chunk:
            step()
    for reducer in early:
        reducer.close()
    for reducer in late:
        reducer.finish()
    for i in range(images):
        output_copy(i).wait()


def run_backward(ng, nr, images, length, grads, firsts, probs, qkv, do, attended, a1, wq, tokens, dh, h, acts, downs, vecs, sums, g_bu):
    width = tokens.shape[1]
    full = dh.shape[0] // images
    nz = nr // 2
    any_spec = pl.BlockSpec(memory_space=pl.ANY)
    vmem = pl.BlockSpec(memory_space=pltpu.VMEM)
    dma = pltpu.SemaphoreType.DMA
    cols_a, cols_b = 3 * 128 * len(PAIRS_A), 3 * 128 * len(PAIRS_B)
    sizes = [(g.shape[0] // ng // 2, g.shape[1]) for g in grads]
    sizes += [(width // ng // 2, cols_a), (width // ng // 2, cols_b)]
    all_sizes = [(t.shape[0] * t.shape[1], t.shape[2]) for t in firsts] + sizes
    total_shapes = [(2, nz, h // nz, w) for h, w in all_sizes]
    vec_shape = vecs.shape
    scratch = [
        pltpu.VMEM(qkv.shape, BF),
        pltpu.VMEM(do.shape, BF),
        pltpu.VMEM(attended.shape, BF),
        pltpu.VMEM(a1.shape, BF),
        pltpu.VMEM((width + 16, images * full), BF),
        pltpu.VMEM(wq.shape, BF),
        pltpu.VMEM(tokens.shape, BF),
        pltpu.VMEM(dh.shape, F32),
        pltpu.VMEM((2, 2 * len(PAIRS_A) * full, 256), BF),
        pltpu.VMEM((images * full, 128), F32),
        pltpu.VMEM((width, cols_a), BF),
        pltpu.VMEM((width, cols_b), BF),
        pltpu.VMEM((2 * width, width), BF),
        pltpu.VMEM((images, length, width), BF),
        dma((3, images)),
        dma((6,)),
        dma((2 * images,)),
        pltpu.VMEM(firsts[0].shape, BF),
        pltpu.VMEM(firsts[1].shape, BF),
        dma((2,)),
        dma((1,)),
        dma((len(act_pieces(downs[0].shape[0], downs[1].shape[0], width)))),
        dma((len(act_pieces(downs[0].shape[0], downs[1].shape[0], width)))),
        dma((2,)),
    ]
    for i, (hh, w) in enumerate(sizes):
        scratch += early_scratch(ng, nz, hh, w, i < 3)
    for hh, w in all_sizes:
        scratch += late_scratch(nz, hh, w)
    scratch += vector_scratch(ng, nz, vec_shape)
    res = pl.pallas_call(
        functools.partial(backward, ng, nz, length),
        out_shape=(jax.ShapeDtypeStruct((images, length, width), BF),) * 2
        + tuple(jax.ShapeDtypeStruct(s, BF) for s in total_shapes)
        + (jax.ShapeDtypeStruct(vec_shape, F32),),
        in_specs=[any_spec] * 18 + [vmem] * 4,
        out_specs=(any_spec,) * 9 + (vmem,),
        scratch_shapes=scratch,
        compiler_params=params(62, collective_id=2, has_side_effects=True),
    )(*grads, *firsts, probs, qkv, do, attended, a1, wq, tokens, dh, h, *acts, *downs, vecs, sums, *g_bu)
    return res[0], res[1], res[2:9], res[9]


def whole_totals(ng, width, totals):
    down1, up1, down, up, out, qa, qb = [t.reshape(-1, t.shape[3]).astype(F32) for t in totals]
    down = jnp.concatenate([down1, down], 0)
    one, two = up1.shape[1] // ng, up.shape[1] // ng
    parts = []
    for m in range(ng):
        parts += [up1[:, m * one : (m + 1) * one], up[:, m * two : (m + 1) * two]]
    up = jnp.concatenate(parts, 1)
    wide_a, wide_b = qa.shape[1] // 3, qb.shape[1] // 3
    parts = []
    for n in range(3):
        parts += [qa[:, n * wide_a : (n + 1) * wide_a], qb[:, n * wide_b : (n + 1) * wide_b]]
    return [jnp.concatenate(parts, 1), out, up, down]


def rows_of(ref, cols):
    return ref[:, :, cols].reshape(ref.shape[0] * ref.shape[1], -1)


def adam_block(ng, *refs):
    vec = refs[7]
    states, results = refs[8:23], refs[23:]

    def update(index, place, gradient, rate, decay):
        w, m, v = (ref[place] for ref in states[3 * index : 3 * index + 3])
        first, second, new = adamw_update(w, m, v, gradient, rate, decay)
        for ref, value in zip(results[4 * index : 4 * index + 4], (gradient, first, second, new)):
            ref[place] = value

    qa, qb, out, up1, up2, down1, down2 = (ref.at[0] for ref in refs[:7])
    wide_a, wide_b = qa.shape[2] // 3, qb.shape[2] // 3
    for n in range(3):
        start = n * (wide_a + wide_b)
        update(0, (slice(None), slice(start, start + wide_a)), rows_of(qa, slice(n * wide_a, (n + 1) * wide_a)).astype(F32), 0.1, 0.05)
        start += wide_a
        update(0, (slice(None), slice(start, start + wide_b)), rows_of(qb, slice(n * wide_b, (n + 1) * wide_b)).astype(F32), 0.1, 0.05)
    update(1, ..., rows_of(out, slice(None)).astype(F32), 0.1, 0.05)
    strip = up1.shape[2] // ng
    for m in range(ng):
        for j, ref in enumerate((up1, up2)):
            start = (2 * m + j) * strip
            update(2, (slice(None), slice(start, start + strip)), rows_of(ref, slice(m * strip, (m + 1) * strip)).astype(F32), 0.1, 0.05)
    for j, ref in enumerate((down1, down2)):
        update(3, j, rows_of(ref, slice(None)).astype(F32), 0.1, 0.05)

    @pl.when(pl.program_id(0) == 0)
    def _():
        g = lax.axis_index("group")
        own = states[12].shape[1]
        total = jnp.zeros(states[12].shape, F32)
        for j in range(ng):
            total = total + jnp.where(g == j, vec[:, j * own : (j + 1) * own], 0.0)
        update(4, ..., total, 0.8, 0.0)


def run_adam(ng, totals, vec_total, states):
    down1, up1, down2, up2, out, qa, qb = totals
    nz, p = out.shape[1], out.shape[2]
    take = 2

    def piece(t):
        return pl.BlockSpec((1, take) + t.shape[2:], lambda i: (i // (nz // take), i % (nz // take), 0, 0))

    def block(index, state):
        if index == 3:
            return pl.BlockSpec((2, take * down1.shape[2], state.shape[2]), lambda i: (0, i, 0))
        if index == 4:
            return pl.BlockSpec(state.shape, lambda i: (0, 0))
        return pl.BlockSpec((take * p, state.shape[1]), lambda i: (i, 0))

    pieces = [qa, qb, out, up1, up2, down1, down2]
    states = list(states)
    down_shape = states[9].shape
    states[9:12] = [s.reshape(2, down_shape[0] // 2, down_shape[1]) for s in states[9:12]]
    specs = [block(i // 3, s) for i, s in enumerate(states)]
    out_specs, out_shapes = [], []
    for index in range(5):
        out_specs += [specs[3 * index]] * 4
        out_shapes += [jax.ShapeDtypeStruct(states[3 * index].shape, F32)] * 4
    res = pl.pallas_call(
        functools.partial(adam_block, ng),
        grid=(2 * nz // take,),
        out_shape=tuple(out_shapes),
        in_specs=[piece(t) for t in pieces] + [pl.BlockSpec(vec_total.shape, lambda i: (0, 0))] + specs,
        out_specs=tuple(out_specs),
        compiler_params=params(),
    )(*pieces, vec_total, *states)
    res = list(res)
    res[12:16] = [r.reshape(down_shape) for r in res[12:16]]
    return res


def adamw_update(weight, first_moment, second, gradient, step_rate, decay_coef):
    first_new = beta_one * first_moment + (1.0 - beta_one) * gradient
    second_new = beta_two * second + (1.0 - beta_two) * gradient * gradient
    fix_one = 1.0 - beta_one**STEP
    fix_two = 1.0 - beta_two**STEP
    weight_new = weight - step_rate * (
        first_new / fix_one / (jnp.sqrt(second_new / fix_two) + adam_eps) + decay_coef * weight
    )
    return (first_new, second_new, weight_new)


def per_device(
    ng, nr, tokens, cotangent, w_qkv, m_qkv, v_qkv, w_out, m_out, v_out, w_up, m_up, v_up,
    w_down, m_down, v_down, vectors, m_vectors, v_vectors,
):
    images, length, width = tokens.shape
    full = -(-length // 16) * 16
    (wq, wo, u2, d2, vecs, a1, probs, qkv, attended, a2, dm, h, act1, d1, da, gd1, gu1, x, gbu1) = run_forward(
        ng, nr, full, tokens, cotangent, w_qkv, w_out, w_up, w_down, vectors
    )
    act2, dh, do, gd2, gu2, g_out, gbu2, sums, td1, tu1 = run_turn(
        ng, nr, a2, dm, h, da, attended, wo, u2, d2, gd1, gu1, vecs
    )
    input_grad, output, totals, vec_total = run_backward(
        ng, nr, images, length, (gd2, gu2, g_out), (td1, tu1), probs, qkv, do, attended, a1, wq, x, dh, h, (act1, act2), (d1, d2),
        vecs, sums, (gbu1, gbu2),
    )
    states = (
        w_qkv, m_qkv, v_qkv, w_out, m_out, v_out, w_up, m_up, v_up, w_down, m_down, v_down, vectors, m_vectors, v_vectors,
    )
    outcome = [output, input_grad]
    if td1.shape == totals[2].shape[1:] and totals[4].shape[2] % 8 == 0:
        return tuple(lax.optimization_barrier(outcome + run_adam(ng, totals, vec_total, states)))
    own = vectors.shape[1]
    gradients = whole_totals(ng, width, totals)
    gradients.append(lax.dynamic_slice_in_dim(vec_total, lax.axis_index("group") * own, own, 1))
    for index, gradient in enumerate(gradients):
        rate, decay = (0.8, 0.0) if index == 4 else (0.1, 0.05)
        outcome.append(gradient)
        outcome.extend(adamw_update(*states[3 * index : 3 * index + 3], gradient, rate, decay))
    return tuple(outcome)


def solution(mesh):
    ng, nr = mesh.shape["group"], mesh.shape["replica"]
    tokens_spec = P(("replica", "group"), None, None)
    rows_spec, cols_spec = P("group", None), P(None, "group")
    in_specs = (tokens_spec,) * 2 + (rows_spec,) * 12 + (cols_spec,) * 3
    out_specs = (tokens_spec,) * 2 + (rows_spec,) * 16 + (cols_spec,) * 4
    return jax.shard_map(
        functools.partial(per_device, ng, nr), mesh=mesh, in_specs=in_specs, out_specs=out_specs, check_vma=False
    )
```

```python
import functools

import jax
import jax.numpy as jnp
from jax import lax
from jax.experimental import pallas as pl
from jax.experimental.pallas import tpu as pltpu
from jax.sharding import PartitionSpec as P

F32 = jnp.float32
BF = jnp.bfloat16
HEADS = 12
HEAD_DIM = 64
STEP = 10
MIB = 2**20
MESH = pl.DeviceIdType.MESH

norm_eps = 1e-06
beta_one = 0.9
beta_two = 0.999
adam_eps = 1e-08


def dot(a, b):
    return jnp.dot(a, b, preferred_element_type=F32)


def dot_t(a, b):
    return lax.dot_general(a, b, (((1,), (1,)), ((), ())), preferred_element_type=F32)


def dot_tn(a, b):
    return lax.dot_general(a, b, (((0,), (0,)), ((), ())), preferred_element_type=F32)


def flip(index, mask):
    out, bit = index, 1
    while bit <= mask:
        if mask & bit:
            out = out + bit * (1 - 2 * lax.rem(lax.div(index, bit), 2))
        bit *= 2
    return out


def rows_at(start, size):
    return pl.ds(pl.multiple_of(start, 16), size)


def normalize(hidden):
    centered = hidden - jnp.mean(hidden, -1, keepdims=True)
    rstd = lax.rsqrt(jnp.mean(centered * centered, -1, keepdims=True) + norm_eps)
    return centered * rstd, rstd


def norm_back(grad, normed, rstd, gain):
    e = grad * gain
    mean_e = jnp.mean(e, -1, keepdims=True)
    mean_en = jnp.mean(e * normed, -1, keepdims=True)
    return (e - mean_e - normed * mean_en) * rstd


def gelu_parts(u):
    d = 1.0 + (0.3275911 * 0.7071067811865476) * jnp.abs(u)
    t = pl.reciprocal(d, approx=True)
    t = t * (2.0 - d * t)
    e = jnp.exp2(u * u * (-0.5 * 1.4426950408889634))
    poly = ((0.5307027145 * t - 0.7265760135) * t + 0.7107068705) * t - 0.142248368
    q = (poly * t + 0.127414796) * t * e
    phi = jnp.where(u > 0, 1.0 - q, q)
    return u * phi, phi + (u * 0.3989422804014327) * e


def params(mib=58, **kw):
    return pltpu.CompilerParams(vmem_limit_bytes=mib * MIB, **kw)


class Places:
    def __init__(self, ng, nz):
        self.ng, self.nz = ng, nz
        self.r, self.g = lax.axis_index("replica"), lax.axis_index("group")
        self.c, self.z = lax.rem(self.r, 2), lax.div(self.r, 2)
        self.sib = {"replica": flip(self.r, 1), "group": self.g}

    def group(self, k):
        return {"replica": self.r, "group": flip(self.g, k)}

    def chip(self, j):
        return {"replica": flip(self.r, 2 * j), "group": self.g}

    def greet(self, group, chips):
        barrier = pltpu.get_barrier_semaphore()
        targets = [self.sib]
        if group:
            targets += [self.group(k) for k in range(1, self.ng)]
        if chips:
            targets += [self.chip(j) for j in range(1, self.nz)]
        for target in targets:
            pl.semaphore_signal(barrier, inc=1, device_id=target, device_id_type=MESH)
        pl.semaphore_wait(barrier, len(targets))


def remote(src, dst, send, recv, target):
    return pltpu.make_async_remote_copy(src, dst, send, recv, device_id=target, device_id_type=MESH)


class Gather:
    def __init__(self, at, buf, sems):
        self.at, self.buf = at, buf
        self.x_send, self.x_recv, self.f_send, self.f_recv = sems
        self.half = buf.shape[0] // at.ng // 2
        self.relay = at.ng == 4

    def rows(self, k, c, lower=None):
        start, size = flip(self.at.g, k) * 2 * self.half + c * self.half, self.half
        if lower is not None:
            size = self.half // 2
            start = start + (0 if lower else size)
        return self.buf.at[rows_at(start, size), :]

    def direct(self, k):
        part = self.rows(0, self.at.c)
        return remote(part, part, self.x_send.at[k - 1], self.x_recv.at[k - 1], self.at.group(k))

    def relayed(self, k):
        part = self.rows(k, self.at.c, k == 1)
        return remote(part, part, self.x_send.at[1 + k], self.x_recv.at[1 + k], self.at.group(3 - k))

    def relayed_in(self, k):
        part = self.rows(3, self.at.c, k == 1)
        return remote(part, part, self.x_send.at[1 + k], self.x_recv.at[1 + k], self.at.group(3 - k))

    def across(self, k):
        part = self.rows(k, self.at.c)
        return remote(part, part, self.f_send.at[k - 1], self.f_recv.at[k - 1], self.at.sib)

    def across_in(self, k):
        part = self.rows(k, 1 - self.at.c)
        return remote(part, part, self.f_send.at[k - 1], self.f_recv.at[k - 1], self.at.sib)

    def near(self):
        return (1, 2) if self.relay else range(1, self.at.ng)

    def start(self):
        for k in self.near():
            self.direct(k).start()

    def pass_on(self):
        for k in self.near():
            self.direct(k).wait_recv()
            if self.relay:
                self.relayed(k).start()
            self.across(k).start()

    def settle(self):
        if self.relay:
            for k in (1, 2):
                self.relayed_in(k).wait_recv()
            self.across(3).start()

    def finish(self):
        for k in range(1, self.at.ng):
            self.across_in(k).wait_recv()

    def close(self):
        for k in self.near():
            self.direct(k).wait_send()
            if self.relay:
                self.relayed(k).wait_send()
        for k in range(1, self.at.ng):
            self.across(k).wait_send()


def gather_sems(ng):
    dma = pltpu.SemaphoreType.DMA
    n = 4 if ng == 4 else ng - 1
    return [dma((n,)), dma((n,)), dma((ng - 1,)), dma((ng - 1,))]


def strips(ng, ff):
    share = ff // ng
    one = -(-share // 256) * 128
    return share, one, share - one


def tile_of(size):
    return 768 if size % 768 == 0 else 512


def mlp_tile(t, ft, blocks, a2, a2t, dm, wu, wd, bias, da_acc, act_s, du_s, gd_slot, gu_slot, gbu, before=(), ready=lambda i: None):
    units = slice(t * ft, (t + 1) * ft)
    rows, width = da_acc.shape[0] // blocks, da_acc.shape[1]

    def body(i, _):
        im = rows_at(i * rows, rows)
        u = dot(a2[im, :], wu[:, units]) + bias[:, units]
        da = dot_t(dm[im, :], wd[units, :])
        act, slope = gelu_parts(u)
        act = act.astype(BF)
        du = (da * slope).astype(BF)
        act_s[im, 0:ft] = act
        du_s[im, 0:ft] = du
        ready(i)
        da_acc[im, :] += dot_t(du, wu[:, units])
        return 0

    lax.fori_loop(0, blocks, body, 0)
    for step in before:
        step()
    gd_slot[...] = dot(act_s[:, 0:ft].T, dm[...]).astype(BF)
    both = dot(a2t[...], du_s[:, 0:ft])
    gu_slot[...] = both[0:width].astype(BF)
    gbu[:, 0:ft] = both[width : width + 1]


def forward(ng, nz, length, *refs):
    at = Places(ng, nz)
    (x_hbm, cot_hbm, wq_hbm, wo_hbm, wu_hbm, wd_hbm, vec_hbm,
     wq_out, wo_out, u2_out, d2_out, vec_out, a1_out, p_out, qkv_out, o_out, a2_out, dm_out, h_out, act_out, d1_out, da_out, gd_out, gu_out, x_out, gbu_out,
     xs, cs, acc, da, h, bq, bo, bu1, bd1, bu2, bd2, vec_s, vall, a1o, qkv, dm, a2t, xf, gbu,
     w_sem, v_sem, in_sem, v_send, v_recv, out_sem, g_sem, a_sem, p_sem) = refs[:54]
    width = h.shape[1]
    blocks_q = [bq.at[:, n * width : (n + 1) * width] for n in range(bq.shape[1] // width)]
    gt, ft = ng * 128, 512
    tiles, per_gather, per = bu1.shape[1] // gt, gt // ft, ft // 128
    buffers = blocks_q + [bo, bu2, bd2]
    for t in range(tiles):
        buffers += [bu1.at[:, t * gt : (t + 1) * gt], bd1.at[t * gt : (t + 1) * gt, :]]
    gathers = [Gather(at, buf, refs[54 + 4 * i : 58 + 4 * i]) for i, buf in enumerate(buffers)]
    nq = len(blocks_q)
    g_q, (g_o, g_u2, g_d2) = gathers[:nq], gathers[nq : nq + 3]
    g_t = [gathers[nq + 3 + 2 * t : nq + 5 + 2 * t] for t in range(tiles)]
    images = xs.shape[0] // length
    full = h.shape[0] // images
    shard = wq_hbm.shape[0]
    ff = wu_hbm.shape[1]
    share, one, two = strips(ng, ff)
    nq, nu = wq_hbm.shape[1] // width, ff // width

    flat, flat_h = acc, h
    loads = []
    for n in range(nq):
        loads.append((wq_hbm.at[:, n * width : (n + 1) * width], flat.at[n * shard : (n + 1) * shard]))
    loads.append((wo_hbm, flat.at[nq * shard : (nq + 1) * shard]))
    for n in range(nu):
        loads.append((wu_hbm.at[:, n * width : (n + 1) * width], flat.at[(nq + 1 + n) * shard : (nq + 2 + n) * shard]))
    loads.append((wd_hbm, flat_h.at[0:share]))
    loads = [pltpu.make_async_copy(src, dst, w_sem.at[i]) for i, (src, dst) in enumerate(loads)]
    vec_load = pltpu.make_async_copy(vec_hbm, vec_s, v_sem)
    x_load = pltpu.make_async_copy(x_hbm, xs, in_sem.at[0])
    cot_load = pltpu.make_async_copy(cot_hbm, cs, in_sem.at[1])
    vec_load.start()
    for n in range(nq):
        loads[n].start()
    x_load.start()
    for load in loads[nq:]:
        load.start()
    cot_load.start()
    at.greet(True, False)

    vec_load.wait()
    vall[at.g] = vec_s[...].astype(BF).astype(F32)
    v_copies = [remote(vall.at[at.g], vall.at[at.g], v_send.at[k - 1], v_recv.at[k - 1], at.group(k)) for k in range(1, ng)]
    for copy in v_copies:
        copy.start()
    for n in range(nq):
        loads[n].wait()
        blocks_q[n][rows_at(at.g * shard, shard), :] = flat[n * shard : (n + 1) * shard, :].astype(BF)
        if n == 0:
            g_q[0].start()
    loads[nq].wait()
    bo[rows_at(at.g * shard, shard), :] = flat[nq * shard : (nq + 1) * shard, :].astype(BF)
    for n in range(nu):
        loads[nq + 1 + n].wait()
    for m in range(ng):
        block, col = divmod(m * share, width)
        src = slice((nq + 1 + block) * shard, (nq + 2 + block) * shard)
        for t in range(tiles):
            lanes = slice(t * gt + m * 128, t * gt + (m + 1) * 128)
            bu1[rows_at(at.g * shard, shard), lanes] = flat[src, col + t * 128 : col + (t + 1) * 128].astype(BF)
        bu2[rows_at(at.g * shard, shard), m * two : (m + 1) * two] = flat[src, col + one : col + share].astype(BF)
    loads[nq + 1 + nu].wait()
    for t in range(tiles):
        bd1[rows_at(t * gt + at.g * 128, 128), :] = flat_h[t * 128 : (t + 1) * 128, :].astype(BF)
    bd2[rows_at(at.g * two, two), :] = flat_h[one:share, :].astype(BF)

    for copy in v_copies:
        copy.wait()
    w = vall.shape[2]
    vecs = jnp.zeros((vall.shape[1], width), F32)
    for j in range(ng):
        row = lax.broadcasted_iota(jnp.int32, (w, width), 0)
        col = lax.broadcasted_iota(jnp.int32, (w, width), 1)
        vecs = vecs + dot(vall[j].astype(BF), jnp.where(col == row + j * w, 1.0, 0.0).astype(BF))
    vec_out[...] = vecs

    x_load.wait()
    lanes = width // 128

    def spread(ref):
        for j in range(lanes):
            xf[j, 0 : length * images, :] = ref[:, j * 128 : (j + 1) * 128].astype(F32)

    def image_of(i):
        return jnp.concatenate([xf[j, pl.ds(i, full, stride=images), :] for j in range(lanes)], 1)

    xf[:, length * images :, :] = jnp.zeros((lanes, (full - length) * images, 128), F32)
    spread(xs)

    def when(i, index, *steps):
        @pl.when(i == index)
        def _():
            for step in steps:
                step()

    def norm_image(i, _):
        when(i, 2, g_q[1].start)
        when(i, 5, g_q[2].start)
        when(i, images - 1, g_q[0].pass_on)
        im = rows_at(i * full, full)
        x = image_of(i)
        h[im, :] = x
        qkv[im, 0:width] = x.astype(BF)
        normed, _r = normalize(x)
        a1o[im, :] = (normed * vec_out[4:5, :] + vec_out[5:6, :]).astype(BF)
        return 0

    lax.fori_loop(0, images, norm_image, 0)
    a1_copy = pltpu.make_async_copy(a1o, a1_out, out_sem.at[0])
    a1_copy.start()
    x_copy = pltpu.make_async_copy(qkv.at[:, 0:width], x_out, out_sem.at[12])
    x_copy.start()
    cot_load.wait()
    spread(cs)

    def cot_image(i, _):
        when(i, 2, g_q[1].pass_on)
        when(i, 5, g_q[2].pass_on, g_q[0].settle)
        dm[rows_at(i * full, full), :] = image_of(i).astype(BF)
        return 0

    lax.fori_loop(0, images, cot_image, 0)
    dm_copy = pltpu.make_async_copy(dm, dm_out, out_sem.at[1])
    dm_copy.start()
    g_o.start()
    x_copy.wait()

    def each(group, name):
        for gather in group:
            if isinstance(gather, Gather):
                getattr(gather, name)()
            else:
                each(gather, name)

    zero = jnp.zeros((1, width), F32)
    biases = [vec_out[0:1, :], zero, vec_out[1:2, :]]
    block = images * full // 2

    for n in range(3):
        cols = slice(n * width, (n + 1) * width)
        g_q[n].finish()

        def project(i, _, cols=cols, bias=biases[n]):
            im = rows_at(i * block, block)
            qkv[im, cols] = (dot(a1o[im, :], bq[:, cols]) + bias).astype(BF)
            return 0

        lax.fori_loop(0, 2, project, 0)
        if n == 0:
            g_q[1].settle()
            g_q[2].settle()
            each(g_t[0], "start")
    wq_copy = pltpu.make_async_copy(bq, wq_out, out_sem.at[2])
    wq_copy.start()
    qkv_copy = pltpu.make_async_copy(qkv, qkv_out, out_sem.at[3])
    qkv_copy.start()
    a1_copy.wait()

    low_half = lax.broadcasted_iota(jnp.int32, (full, 128), 1) < HEAD_DIM
    key_bias = jnp.where(lax.broadcasted_iota(jnp.int32, (1, full), 1) < length, 0.0, -1e30).astype(F32)
    ones = jnp.ones((full, 128), BF)
    per_col = HEADS // 3

    def keep(i, buf):
        return [
            pltpu.make_async_copy(
                buf.at[0 : per_col * full, n * 256 : (n + 1) * 256],
                p_out.at[rows_at((i * 3 + n) * per_col * full, per_col * full), :],
                p_sem.at[lax.rem(i, 2), n],
            )
            for n in range(3)
        ]

    def attend(i, buf):
        @pl.when(i >= 2)
        def _():
            for copy in keep(i - 2, buf):
                copy.wait()

        when(i, 0, g_o.pass_on)
        when(i, 1, lambda: each(g_t[1], "start"))
        when(i, 2, g_o.settle, lambda: each(g_t[0], "pass_on"))
        when(i, 5, lambda: each(g_t[0], "settle"), lambda: each(g_t[1], "pass_on"), lambda: each(g_t[2:], "start"))
        im = rows_at(i * full, full)
        for p in range(HEADS // 2):
            col = p * 128
            q = qkv[im, col : col + 128] * jnp.asarray(HEAD_DIM**-0.5, BF)
            k = qkv[im, col + width : col + width + 128]
            v = jnp.concatenate([qkv[im, col + 2 * width : col + 2 * width + 128], ones], axis=1)
            heads = []
            for hd in range(2):
                mine = low_half if hd == 0 else ~low_half
                s = dot_t(jnp.where(mine, q, jnp.zeros_like(q)), k) + key_bias
                e = jnp.exp(s - jnp.max(s, -1, keepdims=True))
                both = dot(e.astype(BF), v)
                scale = 1.0 / both[:, 128:]
                heads.append(both[:, :128] * scale)
                wide = jnp.concatenate([scale, scale[:, : full - 128]], 1)
                hd_all = 2 * p + hd
                place = (hd_all % per_col * full, hd_all // per_col * 256)
                buf[place[0] : place[0] + full, place[1] : place[1] + full] = (e * wide).astype(BF)
            a1o[im, col : col + 128] = jnp.where(low_half, heads[0], heads[1]).astype(BF)
        for copy in keep(i, buf):
            copy.start()

    def attend_two(j, _):
        attend(2 * j, xs)
        attend(2 * j + 1, cs)
        return 0

    lax.fori_loop(0, images // 2, attend_two, 0)
    o_copy = pltpu.make_async_copy(a1o, o_out, out_sem.at[4])
    o_copy.start()
    g_o.finish()
    wo_copy = pltpu.make_async_copy(bo, wo_out, out_sem.at[5])
    wo_copy.start()
    qkv_copy.wait()

    def middle(i, _):
        im = rows_at(i * block, block)
        hidden = h[im, :] + dot(a1o[im, :], bo[...]) + vec_out[2:3, :]
        h[im, :] = hidden
        normed, _r = normalize(hidden)
        qkv[im, 0:width] = (normed * vec_out[6:7, :] + vec_out[7:8, :]).astype(BF)
        da[im, :] = jnp.zeros((block, width), F32)
        return 0

    lax.fori_loop(0, 2, middle, 0)
    a2_copy = pltpu.make_async_copy(qkv.at[:, 0:width], a2_out, out_sem.at[6])
    h_copy = pltpu.make_async_copy(h, h_out, out_sem.at[7])
    a2_copy.start()
    h_copy.start()
    a2t[0:width, :] = qkv[:, 0:width].T
    a2t[width:, :] = jnp.ones_like(a2t[width:, :])
    each(g_t[1], "settle")
    each(g_t[2:], "pass_on")
    each([g_u2, g_d2], "start")

    for i in (images - 2, images - 1):
        for copy in keep(i, (xs, cs)[i % 2]):
            copy.wait()
    bias = jnp.concatenate([unit_bias(vec_out, ng, share, t * 128, 128) for t in range(tiles)], 1)
    slots = [(ref, n * width) for ref in (xs, cs) for n in range(2)]
    d1_copy = pltpu.make_async_copy(bd1, d1_out, out_sem.at[8])
    act_s = qkv.at[:, width : width + ft]
    act_copies = [
        pltpu.make_async_copy(act_s, act_out.at[:, ct * ft : (ct + 1) * ft], a_sem.at[ct]) for ct in range(tiles * per_gather)
    ]
    da_copy = pltpu.make_async_copy(da, da_out, out_sem.at[9])
    pending = []
    for ct in range(tiles * per_gather):
        t, sub = divmod(ct, per_gather)
        if sub == 0:
            each(g_t[t], "finish")
        if ct >= 2:
            for copy in pending[2 * per * (ct - 2) : 2 * per * (ct - 1)]:
                copy.wait()
        gd_slot, gu_slot = [ref.at[start : start + width] for ref, start in slots[2 * (ct % 2) : 2 * (ct % 2) + 2]]
        gd_slot, gu_slot = gd_slot.at[0:ft], gu_slot.at[:, 0:ft]
        hooks = [act_copies[ct].start]
        if ct:
            act_copies[ct - 1].wait()
        if ct == 0:
            hooks.append(lambda: each(g_t[2:], "settle"))
        if ct == tiles * per_gather - 2:
            hooks.append(lambda: each([g_u2, g_d2], "pass_on"))
        if ct == tiles * per_gather - 1:
            hooks += [d1_copy.start, da_copy.start, lambda: each([g_u2, g_d2], "settle")]
        mlp_tile(
            ct, ft, 2, qkv.at[:, 0:width], a2t, dm, bu1, bd1, bias, da, act_s, qkv.at[:, 2 * width : 2 * width + ft], gd_slot, gu_slot, gbu,
            hooks,
        )
        for i in range(per):
            start = (sub * per + i) * one + t * 128
            units, part = slice(start, start + 128), slice(i * 128, (i + 1) * 128)
            pending.append(pltpu.make_async_copy(gd_slot.at[part, :], gd_out.at[units, :], g_sem.at[0, ct, i]))
            pending.append(pltpu.make_async_copy(gu_slot.at[:, part], gu_out.at[:, units], g_sem.at[1, ct, i]))
            gbu_out[:, units] = gbu[:, part]
        for copy in pending[-2 * per :]:
            copy.start()
    g_u2.finish()
    g_d2.finish()
    u2_copy = pltpu.make_async_copy(bu2, u2_out, out_sem.at[10])
    d2_copy = pltpu.make_async_copy(bd2, d2_out, out_sem.at[11])
    u2_copy.start()
    d2_copy.start()
    for gather in gathers:
        gather.close()
    for copy in pending[-4 * per :] + [dm_copy, wq_copy, o_copy, wo_copy, a2_copy, h_copy, d1_copy, da_copy, act_copies[-1], u2_copy, d2_copy]:
        copy.wait()


def unit_bias(vec_ref, ng, share, start, size):
    width = vec_ref.shape[1]
    parts = []
    for m in range(ng):
        row, col = divmod(m * share + start, width)
        parts.append(vec_ref[8 + row : 9 + row, col : col + size])
    return jnp.concatenate(parts, 1)


def run_forward(ng, nr, full, tokens, cotangent, w_qkv, w_out, w_up, w_down, vectors):
    images, length, width = tokens.shape
    ff = w_up.shape[1]
    share, one, two = strips(ng, ff)
    f1, f2 = ng * one, ng * two
    any_spec = pl.BlockSpec(memory_space=pl.ANY)
    vmem = pl.BlockSpec(memory_space=pltpu.VMEM)
    dma = pltpu.SemaphoreType.DMA
    rows_like = (images * full, width)
    flat = (length * images, width)
    ft = 512

    def bf(*shape):
        return jax.ShapeDtypeStruct(shape, BF)

    def f32(*shape):
        return jax.ShapeDtypeStruct(shape, F32)

    n_loads = w_qkv.shape[1] // width + ff // width + 2
    return pl.pallas_call(
        functools.partial(forward, ng, nr // 2, length),
        out_shape=(
            bf(width, 3 * width), bf(width, width), bf(width, f2), bf(f2, width), f32(vectors.shape[0], width),
            bf(*rows_like), bf(images * HEADS * full, 256), bf(images * full, 3 * width), bf(*rows_like), bf(*rows_like), bf(*rows_like),
            f32(*rows_like), bf(images * full, f1), bf(f1, width), f32(*rows_like), bf(f1, width), bf(width, f1), bf(*rows_like), f32(1, f1),
        ),
        in_specs=[any_spec] * 7,
        out_specs=(any_spec,) * 4 + (vmem,) + (any_spec,) * 13 + (vmem,),
        scratch_shapes=[
            pltpu.VMEM(flat, BF),
            pltpu.VMEM(flat, BF),
            pltpu.VMEM(rows_like, F32),
            pltpu.VMEM(rows_like, F32),
            pltpu.VMEM(rows_like, F32),
            pltpu.VMEM((width, 3 * width), BF),
            pltpu.VMEM((width, width), BF),
            pltpu.VMEM((width, f1), BF),
            pltpu.VMEM((f1, width), BF),
            pltpu.VMEM((width, f2), BF),
            pltpu.VMEM((f2, width), BF),
            pltpu.VMEM(vectors.shape, F32),
            pltpu.VMEM((ng,) + vectors.shape, F32),
            pltpu.VMEM(rows_like, BF),
            pltpu.VMEM((images * full, 3 * width), BF),
            pltpu.VMEM(rows_like, BF),
            pltpu.VMEM((width + 16, images * full), BF),
            pltpu.VMEM((width // 128, images * full, 128), F32),
            pltpu.VMEM((1, ft), F32),
            dma((n_loads,)),
            dma,
            dma((2,)),
            dma((ng - 1,)),
            dma((ng - 1,)),
            dma((13,)),
            dma((2, f1 // ft, ft // 128)),
            dma((f1 // ft,)),
            dma((2, 3)),
        ]
        + gather_sems(ng) * (3 + w_qkv.shape[1] // width + 2 * (f1 // (ng * 128))),
        compiler_params=params(64, collective_id=0, has_side_effects=True),
    )(
        tokens.transpose(1, 0, 2).reshape(flat), cotangent.transpose(1, 0, 2).reshape(flat),
        w_qkv, w_out, w_up, w_down, vectors,
    )


class Early:
    def __init__(self, at, src, load, refs):
        self.at, self.src, self.mine = at, src, None
        if load:
            self.mine, refs = refs[0], refs[1:]
        self.rc, self.rx, self.tz, self.m_sem, self.c_send, self.c_recv, self.x_send, self.x_recv = refs[:8]
        self.rest = refs[8:]
        self.half = self.rc.shape[1]
        self.two = at.ng == 4

    def load_copy(self, m):
        start = m * 2 * self.half + self.at.c * self.half
        return pltpu.make_async_copy(self.src.at[rows_at(start, self.half), :], self.mine.at[m], self.m_sem.at[m])

    def core_copy(self, m):
        start = m * 2 * self.half + (1 - self.at.c) * self.half
        return remote(self.src.at[rows_at(start, self.half), :], self.rc.at[m], self.c_send.at[m], self.c_recv.at[m], self.at.sib)

    def group_copy(self, k):
        return remote(self.rc.at[flip(self.at.g, k)], self.rx.at[k - 1], self.x_send.at[k - 1], self.x_recv.at[k - 1], self.at.group(k))

    def rows(self, k):
        return slice(0, self.half // 2) if k == 1 else slice(self.half // 2, self.half)

    def first_copy(self, k, own):
        part = self.rc.at[flip(self.at.g, k if own else 3), self.rows(k), :]
        slot = 2 * (k - 1) + (0 if own else 1)
        return remote(part, self.rx.at[slot], self.x_send.at[slot], self.x_recv.at[slot], self.at.group(k))

    def second_copy(self, k):
        part = self.rc.at[flip(self.at.g, k), self.rows(3 - k), :]
        return remote(part, self.rx.at[3 + k], self.x_send.at[3 + k], self.x_recv.at[3 + k], self.at.group(k))

    def start_core(self):
        for m in range(self.at.ng):
            self.core_copy(m).start()
        if self.mine is not None:
            for m in range(self.at.ng):
                self.load_copy(m).start()

    def start_group(self):
        at, h = self.at, self.half
        for m in range(at.ng):
            self.core_copy(m).wait_recv()
            if self.mine is not None:
                self.load_copy(m).wait()
        order = (3, 1, 2, 0) if self.two else list(range(1, at.ng)) + [0]
        for k in order:
            m = flip(at.g, k)
            mine = self.src[rows_at(m * 2 * h + at.c * h, h), :] if self.mine is None else self.mine[m]
            self.rc[m] = (mine.astype(F32) + self.rc[m].astype(F32)).astype(BF)
            if self.two and k == 3:
                self.first_copy(1, False).start()
                self.first_copy(2, False).start()
            elif self.two and k:
                self.first_copy(k, True).start()
            elif k:
                self.group_copy(k).start()

    def turn_group(self):
        if not self.two:
            return
        for k in (1, 2):
            self.first_copy(k, False).wait_recv()
            m, sl = flip(self.at.g, 3 - k), self.rows(k)
            self.rc[m, sl, :] = (self.rc[m, sl, :].astype(F32) + self.rx[2 * (k - 1) + 1].astype(F32)).astype(BF)
            self.second_copy(3 - k).start()

    def collect(self):
        at = self.at
        if self.two:
            parts = []
            for k in (1, 2):
                self.first_copy(k, True).wait_recv()
                self.second_copy(3 - k).wait_recv()
                part = self.rc[at.g, self.rows(k), :].astype(F32) + self.rx[2 * (k - 1)].astype(F32)
                parts.append(part + self.rx[3 + 3 - k].astype(F32))
            total = jnp.concatenate(parts, 0)
        else:
            for k in range(1, at.ng):
                self.group_copy(k).wait_recv()
            total = self.rc[at.g].astype(F32)
            for k in range(at.ng - 1):
                total = total + self.rx[k].astype(F32)
        p = self.half // at.nz
        for j in range(at.nz):
            self.tz[j] = total[j * p : (j + 1) * p].astype(BF)

    def close(self):
        if self.two:
            for k in (1, 2):
                self.first_copy(k, True).wait_send()
                self.first_copy(k, False).wait_send()
                self.second_copy(k).wait_send()
        else:
            for k in range(1, self.at.ng):
                self.group_copy(k).wait_send()
        for m in range(self.at.ng):
            self.core_copy(m).wait_send()


class Late:
    def __init__(self, at, tz, refs, out, begin=0):
        self.at, self.tz, self.out, self.begin = at, tz, out, begin
        self.steps = at.nz.bit_length() - 1
        (self.rz, self.y, self.z_send, self.z_recv, self.a_send, self.a_recv, self.f_send, self.f_recv, self.o_sem) = refs[:9]
        self.rest = refs[9:]

    def bit(self, k):
        return lax.rem(lax.div(self.at.z, 2**k), 2)

    def base(self, k, size):
        start = 0
        for i in range(k):
            start = start + self.bit(i) * (self.at.nz // 2 ** (i + 1))
        return start + self.bit(k) * size, start + (1 - self.bit(k)) * size

    def half_copy(self, k):
        size = self.at.nz // 2 ** (k + 1)
        landing = self.rz.at[pl.ds(size - 1, size)]
        return remote(self.tz.at[pl.ds(self.base(k, size)[1], size)], landing, self.z_send.at[k], self.z_recv.at[k], self.at.chip(2**k))

    def place(self, mask):
        start = 0
        for i in range(self.steps):
            b = 1 - self.bit(i) if mask & 2**i else self.bit(i)
            start = start + b * (self.at.nz // 2 ** (i + 1))
        return start

    def back_copy(self, k, mask):
        place = self.out.at[self.at.c, self.place(mask)]
        slot = (mask ^ 2**k) - 1
        return remote(self.y if mask == 0 else place, place, self.a_send.at[slot], self.a_recv.at[slot], self.at.chip(2**k))

    def back_in(self, mask):
        place = self.out.at[self.at.c, self.place(mask)]
        return remote(self.y, place, self.a_send.at[mask - 1], self.a_recv.at[mask - 1], self.at.chip(mask))

    def last_copy(self, mask, mine=True):
        place = self.out.at[self.at.c if mine else 1 - self.at.c, self.place(mask)]
        return remote(self.y if mask == 0 else place, place, self.f_send.at[mask], self.f_recv.at[mask], self.at.sib)

    def keep_copy(self):
        return pltpu.make_async_copy(self.y, self.out.at[self.at.c, self.place(0)], self.o_sem)

    def start_halves(self):
        self.half_copy(self.begin).start()

    def add_half(self, k, go_on=True):
        size = self.at.nz // 2 ** (k + 1)
        self.half_copy(k).wait_recv()
        kept = self.base(k, size)[0]
        for i in range(size):
            total = (self.tz[kept + i].astype(F32) + self.rz[size - 1 + i].astype(F32)).astype(BF)
            if size == 1:
                self.y[...] = total
            else:
                self.tz[kept + i] = total
        if size > 1:
            if go_on:
                self.half_copy(k + 1).start()
            return
        for j in reversed(range(self.steps)):
            self.back_copy(j, 0).start()
        self.last_copy(0).start()
        self.keep_copy().start()

    def spread(self, k):
        for mask in range(0, self.at.nz, 2 ** (k + 1)):
            got = mask ^ 2**k
            self.back_in(got).wait_recv()
            for j in reversed(range(k)):
                self.back_copy(j, got).start()
            self.last_copy(got).start()

    def stages(self):
        out = [self.start_halves]
        out += [functools.partial(self.add_half, k) for k in range(self.begin, self.steps)]
        return out + [functools.partial(self.spread, k) for k in reversed(range(self.steps))]

    def finish(self):
        at = self.at
        for mask in range(at.nz):
            self.last_copy(mask, mine=False).wait_recv()
            self.last_copy(mask).wait_send()
        for k in range(self.steps):
            if k >= self.begin:
                self.half_copy(k).wait_send()
            for mask in range(0, at.nz, 2 ** (k + 1)):
                self.back_copy(k, mask).wait_send()
        self.keep_copy().wait()


class LateDirect:
    def __init__(self, at, tz, refs, out):
        self.at, self.tz, self.out = at, tz, out
        (self.rz, self.y, self.z_send, self.z_recv, self.a_send, self.a_recv, self.f_send, self.f_recv, self.o_sem) = refs[:9]
        self.rest = refs[9:]

    def chip_copy(self, j):
        return remote(self.tz.at[flip(self.at.z, j)], self.rz.at[j - 1], self.z_send.at[j - 1], self.z_recv.at[j - 1], self.at.chip(j))

    def back_copy(self, j, mine=True):
        place = self.out.at[self.at.c, self.at.z if mine else flip(self.at.z, j)]
        return remote(self.y, place, self.a_send.at[j - 1], self.a_recv.at[j - 1], self.at.chip(j))

    def last_copy(self, j, mine=True):
        place = self.out.at[self.at.c if mine else 1 - self.at.c, flip(self.at.z, j)]
        return remote(self.y if j == 0 else place, place, self.f_send.at[j], self.f_recv.at[j], self.at.sib)

    def keep_copy(self):
        return pltpu.make_async_copy(self.y, self.out.at[self.at.c, self.at.z], self.o_sem)

    def start_halves(self):
        for j in reversed(range(1, self.at.nz)):
            self.chip_copy(j).start()

    def start_back(self):
        at = self.at
        for j in range(1, at.nz):
            self.chip_copy(j).wait_recv()
        total = self.tz[at.z].astype(F32)
        for j in range(at.nz - 1):
            total = total + self.rz[j].astype(F32)
        self.y[...] = total.astype(BF)
        for j in reversed(range(1, at.nz)):
            self.back_copy(j).start()
        self.last_copy(0).start()
        self.keep_copy().start()

    def start_last(self):
        for j in range(1, self.at.nz):
            self.back_copy(j, mine=False).wait_recv()
            self.last_copy(j).start()

    def stages(self):
        return [self.start_halves, self.start_back, self.start_last]

    def finish(self):
        at = self.at
        for j in range(at.nz):
            self.last_copy(j, mine=False).wait_recv()
            self.last_copy(j).wait_send()
        for j in range(1, at.nz):
            self.back_copy(j).wait_send()
            self.chip_copy(j).wait_send()
        self.keep_copy().wait()


def early_scratch(ng, nz, half, cols, load):
    dma = pltpu.SemaphoreType.DMA
    landing, n = ((6, half // 2, cols), 6) if ng == 4 else ((ng - 1, half, cols), ng - 1)
    shapes = [pltpu.VMEM((ng, half, cols), BF)] if load else []
    shapes += [pltpu.VMEM((ng, half, cols), BF), pltpu.VMEM(landing, BF), pltpu.VMEM((nz, half // nz, cols), BF)]
    return shapes + [dma((m,)) for m in (ng, ng, ng, n, n)]


def late_scratch(nz, half, cols):
    dma = pltpu.SemaphoreType.DMA
    p = half // nz
    steps = nz.bit_length() - 1
    shapes = [pltpu.VMEM((nz - 1, p, cols), BF), pltpu.VMEM((p, cols), BF)]
    for m in (nz - 1, nz - 1, nz):
        shapes += [dma((m,)), dma((m,))]
    return shapes + [dma]


def turn(ng, nz, *refs):
    at = Places(ng, nz)
    (a2_hbm, dm_hbm, h_hbm, da_hbm, o_hbm, wo_hbm, wu_hbm, wd_hbm, gd1_hbm, gu1_hbm, vec_ref,
     act_out, dh_out, do_out, gd_out, gu_out, go_out, gbu_out, sum_out, td_out, tu_out,
     a2, a2t, dm, h, da, o, wo, wu, wd, work, go_s, slot_a, slot_b, slot_c, slot_d,
     blk_sem, big_sem, out_sem, g_sem, a_sem) = refs[:41]
    early_d = Early(at, gd1_hbm, True, refs[41:])
    early_u = Early(at, gu1_hbm, True, early_d.rest)
    late_d = Late(at, early_d.tz, early_u.rest, None)
    late_u = Late(at, early_u.tz, late_d.rest, None)
    rows, width = h.shape
    half = rows // 2

    def block_copy(j, i):
        src, dst = ((a2_hbm, a2), (dm_hbm, dm), (da_hbm, da))[j]
        part = rows_at(i * half, half)
        return pltpu.make_async_copy(src.at[part, :], dst.at[part, :], blk_sem.at[j, i])

    def big_copy(j):
        src, dst = ((wu_hbm, wu), (wd_hbm, wd), (h_hbm, h), (o_hbm, o), (wo_hbm, wo))[j]
        return pltpu.make_async_copy(src, dst, big_sem.at[j])

    block_copy(0, 0).start()
    big_copy(0).start()
    block_copy(1, 0).start()
    big_copy(1).start()
    for j, i in ((0, 1), (1, 1), (2, 0), (2, 1)):
        block_copy(j, i).start()
    for j in range(2, 5):
        big_copy(j).start()
    at.greet(True, True)
    early_d.start_core()
    early_u.start_core()
    for j, i in ((0, 0), (1, 0), (0, 1), (1, 1)):
        block_copy(j, i).wait()
    for j in range(2):
        big_copy(j).wait()
    a2t[0:width, :] = a2[...].T
    a2t[width:, :] = jnp.ones_like(a2t[width:, :])

    ff = wu.shape[1]
    share = ff // ng + gd1_hbm.shape[0] // ng
    bias = unit_bias(vec_ref, ng, share, gd1_hbm.shape[0] // ng, ff // ng)
    ft = tile_of(ff)
    tiles = ff // ft
    slots = ((slot_a, slot_b), (slot_c, slot_d))
    pending = []

    def sums_here(i):
        block_copy(2, i).wait()

        @pl.when(i == 1)
        def _():
            early_d.start_group()

    def sums_there(i):
        @pl.when(i == 1)
        def _():
            early_d.turn_group()

    act_copies = [
        pltpu.make_async_copy(work.at[:, 0:ft], act_out.at[:, t * ft : (t + 1) * ft], a_sem.at[t]) for t in range(tiles)
    ]
    for t in range(tiles):
        if t:
            act_copies[t - 1].wait()
        if t >= 2:
            for copy in pending[2 * (t - 2) : 2 * (t - 1)]:
                copy.wait()
        gd_slot, gu_slot = slots[t % 2][0].at[0:ft], slots[t % 2][1].at[:, 0:ft]
        mlp_tile(
            t, ft, 2, a2, a2t, dm, wu, wd, bias, da, work.at[:, 0:width], work.at[:, width : 2 * width],
            gd_slot, gu_slot, gbu_out.at[:, t * ft : (t + 1) * ft],
            (act_copies[t].start,) + ((early_u.start_group,) if t == 0 else (early_u.turn_group,) if t == 1 else ()),
            sums_here if t == 0 else sums_there if t == 1 else lambda i: None,
        )
        units = slice(t * ft, (t + 1) * ft)
        pending.append(pltpu.make_async_copy(gd_slot, gd_out.at[units, :], g_sem.at[0, t]))
        pending.append(pltpu.make_async_copy(gu_slot, gu_out.at[:, units], g_sem.at[1, t]))
        for copy in pending[-2:]:
            copy.start()

    for j in range(2, 5):
        big_copy(j).wait()
    sum_out[...] = jnp.zeros_like(sum_out)
    early_d.collect()
    late_d.start_halves()

    act_copies[-1].wait()

    def post(b, _):
        @pl.when(b == 1)
        def _():
            early_u.collect()
            late_u.start_halves()

        im = rows_at(b * (rows // 4), rows // 4)
        hidden = h[im, :]
        cot = dm[im, :].astype(F32)
        normed, rstd = normalize(hidden)
        grad = da[im, :]
        dh = cot + norm_back(grad, normed, rstd, vec_ref[6:7, :])
        h[im, :] = dh
        dz = dh.astype(BF)
        work[im, 0:width] = dz
        work[im, width : 2 * width] = dot_t(dz, wo[...]).astype(BF)
        for j, term in enumerate((dz.astype(F32), cot, grad * normed, grad)):
            sum_out[j : j + 1, :] += jnp.sum(term, 0, keepdims=True)
        return 0

    lax.fori_loop(0, 4, post, 0)
    dh_copy = pltpu.make_async_copy(h, dh_out, out_sem.at[0])
    do_copy = pltpu.make_async_copy(work.at[:, width : 2 * width], do_out, out_sem.at[1])
    dh_copy.start()
    do_copy.start()
    go_s[...] = dot(o[...].T, work[:, 0:width]).astype(BF)
    go_copy = pltpu.make_async_copy(go_s, go_out, out_sem.at[2])
    go_copy.start()
    late_d.add_half(0, False)
    td_copy = pltpu.make_async_copy(early_d.tz, td_out, out_sem.at[3])
    td_copy.start()
    late_u.add_half(0, False)
    tu_copy = pltpu.make_async_copy(early_u.tz, tu_out, out_sem.at[4])
    tu_copy.start()
    early_d.close()
    early_u.close()
    late_d.half_copy(0).wait_send()
    late_u.half_copy(0).wait_send()
    for copy in pending[-4:] + [dh_copy, do_copy, go_copy, td_copy, tu_copy]:
        copy.wait()


def run_turn(ng, nr, a2, dm, h, da, o, wo, wu, wd, gd1, gu1, vecs):
    nz = nr // 2
    rows, width = h.shape
    ff = wu.shape[1]
    ft = tile_of(ff)
    any_spec = pl.BlockSpec(memory_space=pl.ANY)
    vmem = pl.BlockSpec(memory_space=pltpu.VMEM)
    dma = pltpu.SemaphoreType.DMA
    sizes = [(g.shape[0] // ng // 2, g.shape[1]) for g in (gd1, gu1)]

    def bf(*shape):
        return jax.ShapeDtypeStruct(shape, BF)

    def f32(*shape):
        return jax.ShapeDtypeStruct(shape, F32)

    scratch = [
        pltpu.VMEM((rows, width), BF),
        pltpu.VMEM((width + 16, rows), BF),
        pltpu.VMEM((rows, width), BF),
        pltpu.VMEM((rows, width), F32),
        pltpu.VMEM((rows, width), F32),
        pltpu.VMEM((rows, width), BF),
        pltpu.VMEM((width, width), BF),
        pltpu.VMEM(wu.shape, BF),
        pltpu.VMEM(wd.shape, BF),
        pltpu.VMEM((rows, 2 * width), BF),
        pltpu.VMEM((width, width), BF),
        pltpu.VMEM((ft, width), BF),
        pltpu.VMEM((width, ft), BF),
        pltpu.VMEM((ft, width), BF),
        pltpu.VMEM((width, ft), BF),
        dma((3, 2)),
        dma((5,)),
        dma((5,)),
        dma((2, ff // ft)),
        dma((ff // ft,)),
    ]
    for hh, w in sizes:
        scratch += early_scratch(ng, nz, hh, w, True)
    for hh, w in sizes:
        scratch += late_scratch(nz, hh, w)
    return pl.pallas_call(
        functools.partial(turn, ng, nz),
        out_shape=(
            bf(rows, ff), f32(rows, width), bf(rows, width), bf(ff, width), bf(width, ff), bf(width, width),
            f32(1, ff), f32(8, width),
        ) + tuple(bf(nz, hh // nz, w) for hh, w in sizes),
        in_specs=[any_spec] * 10 + [vmem],
        out_specs=(any_spec,) * 6 + (vmem, vmem, any_spec, any_spec),
        scratch_shapes=scratch,
        compiler_params=params(64, collective_id=1, has_side_effects=True),
    )(a2, dm, h, da, o, wo, wu, wd, gd1, gu1, vecs)


def vector_sum(at, v_s, landed, sems):
    v_g, v_z, v_c = landed
    g_send, g_recv, z_send, z_recv, c_send, c_recv = sems

    def copies(level):
        if level == 0:
            return [remote(v_s.at[0], v_g.at[k - 1], g_send.at[k - 1], g_recv.at[k - 1], at.group(k)) for k in range(1, at.ng)]
        if level == 1:
            return [remote(v_s.at[1], v_z.at[j - 1], z_send.at[j - 1], z_recv.at[j - 1], at.chip(j)) for j in range(1, at.nz)]
        return [remote(v_s.at[2], v_c.at[0], c_send.at[0], c_recv.at[0], at.sib)]

    def start(level):
        for copy in copies(level):
            copy.start()

    def add(level):
        for copy in copies(level):
            copy.wait()
        total = v_s[level]
        buf = (v_g, v_z, v_c)[level]
        for j in range(buf.shape[0]):
            total = total + buf[j]
        v_s[level + 1] = total

    return start, add


def vector_scratch(ng, nz, shape):
    dma = pltpu.SemaphoreType.DMA
    shapes = [pltpu.VMEM((4,) + shape, F32)]
    shapes += [pltpu.VMEM((m,) + shape, F32) for m in (ng - 1, nz - 1, 1)]
    for m in (ng - 1, nz - 1, 1):
        shapes += [dma((m,)), dma((m,))]
    return shapes


PAIRS_A, PAIRS_B = (0, 1, 2, 3), (4, 5)


def act_pieces(n1, n2, width):
    out = []
    for j in range((n1 + n2) // width):
        cuts = [j * width] + ([n1] if j * width < n1 < (j + 1) * width else []) + [(j + 1) * width]
        out += [(j, start, stop) for start, stop in zip(cuts, cuts[1:])]
    return out


def plan(early, late):
    steps = [chunk.stages() for chunk in late[:2]]
    for first, second in zip(early, late[2:]):

        def join(first=first, second=second):
            first.collect()
            second.start_halves()

        steps.append([first.start_core, first.start_group, first.turn_group, join] + second.stages()[1:])
    return steps


def backward(ng, nz, length, *refs):
    at = Places(ng, nz)
    (gd_hbm, gu_hbm, go_hbm, td1_hbm, tu1_hbm, p_hbm, qkv_hbm, do_hbm, o_hbm, a1_hbm, wq_hbm, x_hbm, dh_hbm, h_hbm, act1_hbm, act2_hbm, d1_hbm, d2_hbm, vec_ref, sum_ref, gbu1_ref, gbu2_ref,
     ig_out, out_out, td1_out, tu1_out, td_out, tu_out, to_out, ta_out, tb_out, vec_out,
     qkv_s, do_s, o_s, a1_s, a1t, wq_s, x_s, dh_s, p_s, inner_s, ga_s, gb_s, w_s, stage, im_sem, big_sem, ig_sem, tz_d1, tz_u1, t_sem, h_sem, act_sem, down_sem, p_sem) = refs[:56]
    rest = refs[56:]
    early, late = [], []
    for src, load in ((gd_hbm, True), (gu_hbm, True), (go_hbm, True), (ga_s, False), (gb_s, False)):
        early.append(Early(at, src, load, rest))
        rest = early[-1].rest
    pieces = [tz_d1, tz_u1] + [e.tz for e in early]
    for tz, total in zip(pieces, (td1_out, tu1_out, td_out, tu_out, to_out, ta_out, tb_out)):
        kind = LateDirect if len(late) >= 5 else Late
        late.append(kind(at, tz, rest, total, *((1,) if len(late) < 2 else ())))
        rest = late[-1].rest
    v_s = rest[0]
    v_start, v_add = vector_sum(at, v_s, rest[1:4], rest[4:10])

    images = ig_sem.shape[0] // 2
    rows, width = do_s.shape
    full = rows // images
    scale = HEAD_DIM**-0.5

    def image_copies(i):
        return [
            pltpu.make_async_copy(src.at[rows_at(i * full, full), :], dst.at[rows_at(i * full, full), :], im_sem.at[j, i])
            for j, (src, dst) in enumerate(((qkv_hbm, qkv_s), (do_hbm, do_s), (o_hbm, o_s)))
        ]

    def big_copy(j):
        src, dst = ((a1_hbm, a1_s), (wq_hbm, wq_s), (x_hbm, x_s), (dh_hbm, dh_s))[j]
        return pltpu.make_async_copy(src, dst, big_sem.at[j])

    def probs_copy(i, pairs):
        count = 2 * len(pairs) * full
        src = p_hbm.at[rows_at((i * HEADS + 2 * pairs[0]) * full, count), :]
        slot = lax.rem(i, 2)
        return pltpu.make_async_copy(src, p_s.at[slot, 0:count, :], p_sem.at[slot])

    tz_copies = [pltpu.make_async_copy(td1_hbm, tz_d1, t_sem.at[0]), pltpu.make_async_copy(tu1_hbm, tz_u1, t_sem.at[1])]
    for copy in tz_copies:
        copy.start()
    for copy in image_copies(0) + image_copies(1):
        copy.start()
    probs_copy(0, PAIRS_A).start()
    at.greet(True, True)
    d1, u1, d2, u2, go, ga, gb = (iter(steps) for steps in plan(early, late))

    def advance(*chunks):
        for chunk in chunks:
            next(chunk)()

    advance(d2)
    for copy, chunk in zip(tz_copies, (d1, u1)):
        copy.wait()
        advance(chunk)
    advance(u2, go)

    low_half = lax.broadcasted_iota(jnp.int32, (full, 128), 1) < HEAD_DIM
    pick = lax.broadcasted_iota(jnp.int32, (width, 128), 0) // HEAD_DIM == lax.broadcasted_iota(jnp.int32, (width, 128), 1)
    pick = jnp.where(pick, 1.0, 0.0).astype(BF)

    def attend_back(i, pairs):
        @pl.when(i + 1 < images)
        def _():
            probs_copy(i + 1, pairs).start()

        im = rows_at(i * full, full)
        probs_copy(i, pairs).wait()
        slot = lax.rem(i, 2)
        for p in pairs:
            col = p * 128
            q = qkv_s[im, col : col + 128] * jnp.asarray(scale, BF)
            k = qkv_s[im, col + width : col + width + 128]
            v = qkv_s[im, col + 2 * width : col + 2 * width + 128]
            do = do_s[im, col : col + 128]
            zero = jnp.zeros_like(q)
            dom = jnp.concatenate([jnp.where(low_half, do, zero), jnp.where(low_half, zero, do)], 0)
            qm = jnp.concatenate([jnp.where(low_half, q, zero), jnp.where(low_half, zero, q)], 0)
            start = 2 * (p - pairs[0]) * full
            probs = p_s[slot, start : start + 2 * full, 0:full]
            inner = jnp.concatenate([inner_s[im, 2 * p : 2 * p + 1], inner_s[im, 2 * p + 1 : 2 * p + 2]], 0)
            ds = (probs.astype(F32) * (dot_t(dom, v) - inner)).astype(BF)
            dq = dot(ds, k)
            qkv_s[im, col : col + 128] = (jnp.where(low_half, dq[:full], dq[full:]) * scale).astype(BF)
            qkv_s[im, col + width : col + width + 128] = dot_tn(ds, qm).astype(BF)
            qkv_s[im, col + 2 * width : col + 2 * width + 128] = dot_tn(probs, dom).astype(BF)

    half_rows = rows // 2
    act_bufs = (do_s, o_s, a1_s, x_s)

    def act_copies(chunk):
        n1, n2 = d1_hbm.shape[0], d2_hbm.shape[0]
        out = []
        for n, (j, start, stop) in enumerate(act_pieces(n1, n2, width)):
            if j == chunk:
                src, first = (act1_hbm, start) if start < n1 else (act2_hbm, start - n1)
                col = start - j * width
                src, dst = src.at[:, first : first + stop - start], act_bufs[j].at[:, col : col + stop - start]
                out.append(pltpu.make_async_copy(src, dst, act_sem.at[n]))
        return out

    down_bufs = [w_s.at[0:width, :], w_s.at[width : 2 * width, :], a1t.at[0:width, 0:width], a1t.at[0:width, width : 2 * width]]

    def down_copies(chunk):
        n1, n2 = d1_hbm.shape[0], d2_hbm.shape[0]
        out = []
        for n, (j, start, stop) in enumerate(act_pieces(n1, n2, width)):
            if j == chunk:
                src, first = (d1_hbm, start) if start < n1 else (d2_hbm, start - n1)
                row = start - j * width
                src, dst = src.at[first : first + stop - start, :], down_bufs[j].at[row : row + stop - start, :]
                out.append(pltpu.make_async_copy(src, dst, down_sem.at[n]))
        return out

    def down_start(chunk):
        for copy in down_copies(chunk):
            copy.start()

    def act_start(bufs, first):
        for j in range(first, first + len(bufs)):
            for copy in act_copies(j):
                copy.start()

    def act_wait(chunk):
        for copy in act_copies(chunk) + down_copies(chunk):
            copy.wait()

    def when(i, index, *chunks):
        @pl.when(i == index)
        def _():
            advance(*chunks)

    def first_pass(i, _):
        for copy in image_copies(i):
            copy.wait()

        @pl.when(i + 2 < images)
        def _():
            for copy in image_copies(i + 2):
                copy.start()

        when(i, 2, d2)
        when(i, 3, u2, d1)
        when(i, 4, go, u1)
        when(i, 6, d2, d1)
        when(i, 7, u1)

        @pl.when(i == 3)
        def _():
            for j in range(4):
                big_copy(j).start()
            for j in range(2):
                down_start(j)

        im = rows_at(i * full, full)
        prod = do_s[im, :].astype(F32) * o_s[im, :].astype(F32)
        high = prod.astype(BF)
        inner_s[im, :] = dot(high, pick) + dot((prod - high.astype(F32)).astype(BF), pick)
        attend_back(i, PAIRS_A)
        return 0

    def weight_grad(pairs, g_ref, steps=()):
        start, stop = pairs[0] * 128, pairs[-1] * 128 + 128
        wide = stop - start
        for n in range(3):
            if n == 1:
                advance(*steps)
            dp = qkv_s[:, n * width + start : n * width + stop]
            both = dot(a1t[...], dp)
            g_ref[:, n * wide : (n + 1) * wide] = both[0:width].astype(BF)
            if n != 1:
                row = 0 if n == 0 else 1
                v_s[0, row : row + 1, start:stop] = both[width : width + 1]

    lax.fori_loop(0, images, first_pass, 0)
    probs_copy(0, PAIRS_B).start()
    big_copy(0).wait()
    a1t[0:width, :] = a1_s[...].T
    a1t[width:, :] = jnp.ones_like(a1t[width:, :])
    weight_grad(PAIRS_A, ga_s, (d2, u2))
    advance(ga, d2, go, d1, u1)

    def second_pass(i, _):
        when(i, 1, u2)
        when(i, 3, ga, go)
        when(i, 4, d2)
        when(i, 6, u2)
        when(i, 7, go)
        attend_back(i, PAIRS_B)
        return 0

    lax.fori_loop(0, images, second_pass, 0)
    weight_grad(PAIRS_B, gb_s)
    advance(gb, ga, d2, u2)

    for j in range(1, 4):
        big_copy(j).wait()
    act_start(act_bufs[:3], 0)
    for j in range(2, len(act_bufs)):
        down_start(j)
    v_s[0, 2:4, :] = sum_ref[0:2, :]
    v_s[0, 4:6, :] = jnp.zeros((2, width), F32)
    v_s[0, 6:8, :] = sum_ref[2:4, :]
    one, two = gbu1_ref.shape[1] // ng, gbu2_ref.shape[1] // ng
    for m in range(ng):
        row, col = divmod(m * (one + two), width)
        v_s[0, 8 + row : 9 + row, col : col + one] = gbu1_ref[0:1, m * one : (m + 1) * one]
        v_s[0, 8 + row : 9 + row, col + one : col + one + two] = gbu2_ref[0:1, m * two : (m + 1) * two]

    def input_copy(i):
        return pltpu.make_async_copy(stage.at[i], ig_out.at[i], ig_sem.at[i])

    def output_copy(i):
        return pltpu.make_async_copy(stage.at[i], out_out.at[i], ig_sem.at[images + i])

    h_copy = pltpu.make_async_copy(h_hbm, dh_s, h_sem.at[0])

    def input_pass(b, _):
        first = b * 2
        when(b, 0, go)
        when(b, 1, gb, d2)
        when(b, 2, ga, u2)
        when(b, 3, gb, go)
        im = rows_at(first * full, 2 * full)
        da = dot_t(qkv_s[im, :], wq_s[...])
        normed, rstd = normalize(x_s[im, :].astype(F32))
        grad = dh_s[im, :] + norm_back(da, normed, rstd, vec_ref[4:5, :])
        grad = grad.astype(BF).reshape(2, full, width)
        for i in range(2):
            stage[first + i] = grad[i, :length, :]
            input_copy(first + i).start()
        v_s[0, 4:5, :] += jnp.sum(da * normed, 0, keepdims=True)
        v_s[0, 5:6, :] += jnp.sum(da, 0, keepdims=True)
        return 0

    lax.fori_loop(0, images // 2, input_pass, 0)
    h_copy.start()
    act_start(act_bufs[3:], 3)
    for i in range(images):
        input_copy(i).wait()

    def output_pass(b, steps):
        im = rows_at(b * half_rows, half_rows)
        for j, buf in enumerate(act_bufs):
            dh_s[im, :] += dot(buf[im, :], down_bufs[j][...])
            if j == 1:
                advance(*steps)
        for i in range(images // 2):
            at_image = b * (images // 2) + i
            image = dh_s[rows_at(at_image * full, full), :] + vec_ref[3:4, :]
            stage[at_image] = image.astype(BF)[:length]
            output_copy(at_image).start()

    v_start(0)
    advance(gb)
    for j in range(len(act_bufs)):
        act_wait(j)
    h_copy.wait()
    output_pass(0, (ga, u2))
    v_add(0)
    v_start(1)
    advance(gb)
    output_pass(1, (go,))
    v_add(1)
    v_start(2)
    advance(ga)
    advance(gb)
    v_add(2)
    vec_out[...] = v_s[3]
    for chunk in (d1, u1, d2, u2, go, ga, gb):
        for step in chunk:
            step()
    for reducer in early:
        reducer.close()
    for reducer in late:
        reducer.finish()
    for i in range(images):
        output_copy(i).wait()


def run_backward(ng, nr, images, length, grads, firsts, probs, qkv, do, attended, a1, wq, tokens, dh, h, acts, downs, vecs, sums, g_bu):
    width = tokens.shape[1]
    full = dh.shape[0] // images
    nz = nr // 2
    any_spec = pl.BlockSpec(memory_space=pl.ANY)
    vmem = pl.BlockSpec(memory_space=pltpu.VMEM)
    dma = pltpu.SemaphoreType.DMA
    cols_a, cols_b = 3 * 128 * len(PAIRS_A), 3 * 128 * len(PAIRS_B)
    sizes = [(g.shape[0] // ng // 2, g.shape[1]) for g in grads]
    sizes += [(width // ng // 2, cols_a), (width // ng // 2, cols_b)]
    all_sizes = [(t.shape[0] * t.shape[1], t.shape[2]) for t in firsts] + sizes
    total_shapes = [(2, nz, h // nz, w) for h, w in all_sizes]
    vec_shape = vecs.shape
    scratch = [
        pltpu.VMEM(qkv.shape, BF),
        pltpu.VMEM(do.shape, BF),
        pltpu.VMEM(attended.shape, BF),
        pltpu.VMEM(a1.shape, BF),
        pltpu.VMEM((width + 16, images * full), BF),
        pltpu.VMEM(wq.shape, BF),
        pltpu.VMEM(tokens.shape, BF),
        pltpu.VMEM(dh.shape, F32),
        pltpu.VMEM((2, 2 * len(PAIRS_A) * full, 256), BF),
        pltpu.VMEM((images * full, 128), F32),
        pltpu.VMEM((width, cols_a), BF),
        pltpu.VMEM((width, cols_b), BF),
        pltpu.VMEM((2 * width, width), BF),
        pltpu.VMEM((images, length, width), BF),
        dma((3, images)),
        dma((6,)),
        dma((2 * images,)),
        pltpu.VMEM(firsts[0].shape, BF),
        pltpu.VMEM(firsts[1].shape, BF),
        dma((2,)),
        dma((1,)),
        dma((len(act_pieces(downs[0].shape[0], downs[1].shape[0], width)))),
        dma((len(act_pieces(downs[0].shape[0], downs[1].shape[0], width)))),
        dma((2,)),
    ]
    for i, (hh, w) in enumerate(sizes):
        scratch += early_scratch(ng, nz, hh, w, i < 3)
    for hh, w in all_sizes:
        scratch += late_scratch(nz, hh, w)
    scratch += vector_scratch(ng, nz, vec_shape)
    res = pl.pallas_call(
        functools.partial(backward, ng, nz, length),
        out_shape=(jax.ShapeDtypeStruct((images, length, width), BF),) * 2
        + tuple(jax.ShapeDtypeStruct(s, BF) for s in total_shapes)
        + (jax.ShapeDtypeStruct(vec_shape, F32),),
        in_specs=[any_spec] * 18 + [vmem] * 4,
        out_specs=(any_spec,) * 9 + (vmem,),
        scratch_shapes=scratch,
        compiler_params=params(62, collective_id=2, has_side_effects=True),
    )(*grads, *firsts, probs, qkv, do, attended, a1, wq, tokens, dh, h, *acts, *downs, vecs, sums, *g_bu)
    return res[0], res[1], res[2:9], res[9]


def whole_totals(ng, width, totals):
    down1, up1, down, up, out, qa, qb = [t.reshape(-1, t.shape[3]).astype(F32) for t in totals]
    down = jnp.concatenate([down1, down], 0)
    one, two = up1.shape[1] // ng, up.shape[1] // ng
    parts = []
    for m in range(ng):
        parts += [up1[:, m * one : (m + 1) * one], up[:, m * two : (m + 1) * two]]
    up = jnp.concatenate(parts, 1)
    wide_a, wide_b = qa.shape[1] // 3, qb.shape[1] // 3
    parts = []
    for n in range(3):
        parts += [qa[:, n * wide_a : (n + 1) * wide_a], qb[:, n * wide_b : (n + 1) * wide_b]]
    return [jnp.concatenate(parts, 1), out, up, down]


def rows_of(ref, cols):
    return ref[:, :, cols].reshape(ref.shape[0] * ref.shape[1], -1)


def adam_block(ng, *refs):
    vec = refs[7]
    states, results = refs[8:23], refs[23:]

    def update(index, place, gradient, rate, decay):
        w, m, v = (ref[place] for ref in states[3 * index : 3 * index + 3])
        first, second, new = adamw_update(w, m, v, gradient, rate, decay)
        for ref, value in zip(results[4 * index : 4 * index + 4], (gradient, first, second, new)):
            ref[place] = value

    qa, qb, out, up1, up2, down1, down2 = (ref.at[0] for ref in refs[:7])
    wide_a, wide_b = qa.shape[2] // 3, qb.shape[2] // 3
    for n in range(3):
        start = n * (wide_a + wide_b)
        update(0, (slice(None), slice(start, start + wide_a)), rows_of(qa, slice(n * wide_a, (n + 1) * wide_a)).astype(F32), 0.1, 0.05)
        start += wide_a
        update(0, (slice(None), slice(start, start + wide_b)), rows_of(qb, slice(n * wide_b, (n + 1) * wide_b)).astype(F32), 0.1, 0.05)
    update(1, ..., rows_of(out, slice(None)).astype(F32), 0.1, 0.05)
    strip = up1.shape[2] // ng
    for m in range(ng):
        for j, ref in enumerate((up1, up2)):
            start = (2 * m + j) * strip
            update(2, (slice(None), slice(start, start + strip)), rows_of(ref, slice(m * strip, (m + 1) * strip)).astype(F32), 0.1, 0.05)
    for j, ref in enumerate((down1, down2)):
        update(3, j, rows_of(ref, slice(None)).astype(F32), 0.1, 0.05)

    @pl.when(pl.program_id(0) == 0)
    def _():
        g = lax.axis_index("group")
        own = states[12].shape[1]
        total = jnp.zeros(states[12].shape, F32)
        for j in range(ng):
            total = total + jnp.where(g == j, vec[:, j * own : (j + 1) * own], 0.0)
        update(4, ..., total, 0.8, 0.0)


def run_adam(ng, totals, vec_total, states):
    down1, up1, down2, up2, out, qa, qb = totals
    nz, p = out.shape[1], out.shape[2]
    take = min(4, nz)

    def piece(t):
        return pl.BlockSpec((1, take) + t.shape[2:], lambda i: (i // (nz // take), i % (nz // take), 0, 0))

    def block(index, state):
        if index == 3:
            return pl.BlockSpec((2, take * down1.shape[2], state.shape[2]), lambda i: (0, i, 0))
        if index == 4:
            return pl.BlockSpec(state.shape, lambda i: (0, 0))
        return pl.BlockSpec((take * p, state.shape[1]), lambda i: (i, 0))

    pieces = [qa, qb, out, up1, up2, down1, down2]
    states = list(states)
    down_shape = states[9].shape
    states[9:12] = [s.reshape(2, down_shape[0] // 2, down_shape[1]) for s in states[9:12]]
    specs = [block(i // 3, s) for i, s in enumerate(states)]
    out_specs, out_shapes = [], []
    for index in range(5):
        out_specs += [specs[3 * index]] * 4
        out_shapes += [jax.ShapeDtypeStruct(states[3 * index].shape, F32)] * 4
    res = pl.pallas_call(
        functools.partial(adam_block, ng),
        grid=(2 * nz // take,),
        out_shape=tuple(out_shapes),
        in_specs=[piece(t) for t in pieces] + [pl.BlockSpec(vec_total.shape, lambda i: (0, 0))] + specs,
        out_specs=tuple(out_specs),
        compiler_params=params(),
    )(*pieces, vec_total, *states)
    res = list(res)
    res[12:16] = [r.reshape(down_shape) for r in res[12:16]]
    return res


def adamw_update(weight, first_moment, second, gradient, step_rate, decay_coef):
    first_new = beta_one * first_moment + (1.0 - beta_one) * gradient
    second_new = beta_two * second + (1.0 - beta_two) * gradient * gradient
    fix_one = 1.0 - beta_one**STEP
    fix_two = 1.0 - beta_two**STEP
    weight_new = weight - step_rate * (
        first_new * (1.0 / fix_one) / (jnp.sqrt(second_new * (1.0 / fix_two)) + adam_eps) + decay_coef * weight
    )
    return (first_new, second_new, weight_new)


def per_device(
    ng, nr, tokens, cotangent, w_qkv, m_qkv, v_qkv, w_out, m_out, v_out, w_up, m_up, v_up,
    w_down, m_down, v_down, vectors, m_vectors, v_vectors,
):
    images, length, width = tokens.shape
    full = -(-length // 16) * 16
    (wq, wo, u2, d2, vecs, a1, probs, qkv, attended, a2, dm, h, act1, d1, da, gd1, gu1, x, gbu1) = run_forward(
        ng, nr, full, tokens, cotangent, w_qkv, w_out, w_up, w_down, vectors
    )
    act2, dh, do, gd2, gu2, g_out, gbu2, sums, td1, tu1 = run_turn(
        ng, nr, a2, dm, h, da, attended, wo, u2, d2, gd1, gu1, vecs
    )
    input_grad, output, totals, vec_total = run_backward(
        ng, nr, images, length, (gd2, gu2, g_out), (td1, tu1), probs, qkv, do, attended, a1, wq, x, dh, h, (act1, act2), (d1, d2),
        vecs, sums, (gbu1, gbu2),
    )
    states = (
        w_qkv, m_qkv, v_qkv, w_out, m_out, v_out, w_up, m_up, v_up, w_down, m_down, v_down, vectors, m_vectors, v_vectors,
    )
    outcome = [output, input_grad]
    if td1.shape == totals[2].shape[1:] and totals[4].shape[2] % 8 == 0:
        return tuple(lax.optimization_barrier(outcome + run_adam(ng, totals, vec_total, states)))
    own = vectors.shape[1]
    gradients = whole_totals(ng, width, totals)
    gradients.append(lax.dynamic_slice_in_dim(vec_total, lax.axis_index("group") * own, own, 1))
    for index, gradient in enumerate(gradients):
        rate, decay = (0.8, 0.0) if index == 4 else (0.1, 0.05)
        outcome.append(gradient)
        outcome.extend(adamw_update(*states[3 * index : 3 * index + 3], gradient, rate, decay))
    return tuple(outcome)


def solution(mesh):
    ng, nr = mesh.shape["group"], mesh.shape["replica"]
    tokens_spec = P(("replica", "group"), None, None)
    rows_spec, cols_spec = P("group", None), P(None, "group")
    in_specs = (tokens_spec,) * 2 + (rows_spec,) * 12 + (cols_spec,) * 3
    out_specs = (tokens_spec,) * 2 + (rows_spec,) * 16 + (cols_spec,) * 4
    return jax.shard_map(
        functools.partial(per_device, ng, nr), mesh=mesh, in_specs=in_specs, out_specs=out_specs, check_vma=False
    )
```
